32 devices in a mesh: seq: 8 (over y, x, core), batch: 4 (over z).
Axes of the slice: x: 2, y: 2, z: 4, core: 2. Of those that a mesh axis runs over, the one named last changes fastest.
Arguments:
- inputs: bfloat16 [4, 2048, 2048], P('batch', 'seq'), may hold values from -106.50967 to 106.50967
- output_grad: bfloat16 [4, 2048, 2048], P('batch', 'seq'), may hold values from -6 to 6
- norm_gain: float32 [2048], replicated, may hold values from 0.1 to 1.9
- gate_bias: float32 [2048], P('seq'), as said below
- state_in: float32 [4, 2048], P('batch', 'seq'), may hold values from -6 to 6
- w_gate: bfloat16 [2048, 2048], P('seq'), may hold values from -0.44194174 to 0.44194174
- w_cand: bfloat16 [2048, 2048], P('seq'), may hold values from -0.125 to 0.125
- w_out: bfloat16 [2048, 2048], P('seq'), may hold values from -0.125 to 0.125
Outputs:
- layer_out: bfloat16 [4, 2048, 2048], P('batch', 'seq')
- input_grad: bfloat16 [4, 2048, 2048], P('batch', 'seq')
- state_grad: float32 [4, 2048], P('batch', 'seq')
- bias_grad: float32 [2048], P('seq')
The draws below stay inside these ranges and needn't reach their ends.
Inputs may be any that keep to these rules, and one draw needn't show every extreme that they name: `gate_bias`: every value is at least -ln(2048) - 1.5.
All inputs are finite; a program needn't handle non-finite values.
Results may differ from the reference program's by a relative error of at most 0.013.
Values may be sent and summed in bfloat16 or wider, within the bound.
No kernel may reach another device: no remote copies, remote signals or barrier semaphores. Data moves between devices by JAX's collectives and lax.ppermute only.
A program may use at most 128 MiB of HBM per device.

```python
import math
from functools import partial
import jax
import jax.numpy as jnp
from jax import lax

MODEL_WIDTH = 2048
H = 2048
BATCH_SEQUENCES = 4
WINDOW_TOKENS = 2048


def rate_plan(key):
    folded = jax.random.fold_in(key, 7)
    key_fast, key_slow, key_quick, key_aim = jax.random.split(folded, 4)
    fast_share = 0.5
    fast_flag = jax.random.uniform(key_fast, (H,)) < fast_share
    slow_bias = -math.log(WINDOW_TOKENS) - jax.random.uniform(key_slow, (H,), minval=0.2, maxval=1.5)
    quick_bias = jax.random.uniform(key_quick, (H,), minval=-4.3, maxval=-3.3)
    bias_values = jnp.where(fast_flag, quick_bias, slow_bias)
    lift_values = (-bias_values - 1.1) / math.sqrt(MODEL_WIDTH)
    target_vector = jax.random.normal(key_aim, (MODEL_WIDTH,))
    target_vector = target_vector / jnp.sqrt(jnp.sum(target_vector * target_vector))
    return (bias_values, lift_values, target_vector)


def draw_gate_bias(key, part):
    bias_values, lift_values, target_vector = rate_plan(key)
    return bias_values.astype(jnp.float32)


def draw_w_gate(key, part):
    bias_values, lift_values, target_vector = rate_plan(key)
    base_sample = jax.random.normal(jax.random.fold_in(key, 11), (MODEL_WIDTH, H))
    base_sample = jnp.clip(base_sample, -6.0, 6.0) / math.sqrt(MODEL_WIDTH)
    return (base_sample + target_vector[:, None] * lift_values[None, :]).astype(jnp.bfloat16)


def draw_inputs(key, part):
    bias_values, lift_values, target_vector = rate_plan(key)
    key_base = jax.random.fold_in(key, 13)
    key_positions = jax.random.fold_in(key, 17)
    base_sample = jnp.clip(jax.random.normal(key_base, (BATCH_SEQUENCES, WINDOW_TOKENS, MODEL_WIDTH)), -6.0, 6.0)
    spike_positions = jax.random.randint(key_positions, (BATCH_SEQUENCES, 3), 0, WINDOW_TOKENS)
    flagged_entries = jnp.any(jnp.arange(WINDOW_TOKENS)[None, :, None] == spike_positions[:, None, :], axis=-1)
    spike_rows = 0.1 * base_sample + 2.0 * math.sqrt(MODEL_WIDTH) * target_vector
    return jnp.where(flagged_entries[:, :, None], spike_rows, base_sample).astype(jnp.bfloat16)


def levels(rng, dims, cuts, low, top_value):
    loudness, own = 1.0, jax.random.fold_in(rng, 6)
    for position, blocks in cuts:
        draws = jnp.exp(jax.random.uniform(jax.random.fold_in(own, position), (blocks,), jnp.float32, low / len(cuts), top_value / len(cuts)))
        loudness = loudness * jnp.repeat(draws, dims[position] // blocks).reshape([-1 if axis == position else 1 for axis in range(len(dims))])
    return loudness


def gaussian(key, extent, scale, bound, shards=(), dtype=jnp.bfloat16):
    values = jax.random.normal(key, extent, jnp.float32) * scale
    if len(shards) > 0:
        values = levels(key, extent, shards, -0.22, 0.18) * values
    return jnp.clip(values, min=-bound, max=bound).astype(dtype)


def setup_inputs(seed: int = 0) -> dict:
    seeds = jax.random.split(jax.random.key(seed), 9)
    inputs = draw_inputs(jax.random.fold_in(seeds[8], 71), 0)
    output_grad = gaussian(seeds[1], (BATCH_SEQUENCES, WINDOW_TOKENS, MODEL_WIDTH), 1.0, 6.0, ((0, 4), (1, 8)))
    norm_gain = jnp.clip(1.0 + 0.18 * jax.random.normal(seeds[2], (MODEL_WIDTH,), jnp.float32), 0.1, 1.9)
    gate_bias = draw_gate_bias(jax.random.fold_in(seeds[8], 71), 0)
    state_in = gaussian(seeds[4], (BATCH_SEQUENCES, H), 1.0, 6.0, ((0, 4), (1, 8)), jnp.float32)
    w_gate = draw_w_gate(jax.random.fold_in(seeds[8], 71), 0)
    w_cand = gaussian(seeds[6], (MODEL_WIDTH, H), MODEL_WIDTH ** -0.5, 0.125, ((0, 8),))
    w_out = gaussian(seeds[7], (H, MODEL_WIDTH), H ** -0.5, 0.125, ((0, 8),))
    return {"inputs": inputs, "output_grad": output_grad, "norm_gain": norm_gain, "gate_bias": gate_bias, "state_in": state_in, "w_gate": w_gate, "w_cand": w_cand, "w_out": w_out}


EPSILON = 1e-06

def compose(earlier, later):
    return (earlier[0] * later[0], later[0] * earlier[1] + later[1])

def one_sequence(norm_gain, gate_bias, w_gate, w_cand, w_out, operands):
    seq_tokens, seq_grads, initial = operands
    residual = seq_tokens.astype(jnp.float32)
    mean_square = lax.optimization_barrier(jnp.mean(residual * residual, axis=-1, keepdims=True))
    inverse_rms = lax.rsqrt(mean_square + EPSILON)
    unit_rows = residual * inverse_rms
    normed = (unit_rows * norm_gain).astype(jnp.bfloat16)
    gate_pre = jnp.dot(normed, w_gate, preferred_element_type=jnp.float32).astype(jnp.bfloat16)
    cand_pre = jnp.dot(normed, w_cand, preferred_element_type=jnp.float32).astype(jnp.bfloat16)
    gate_input = gate_pre.astype(jnp.float32) + gate_bias
    update = jax.nn.sigmoid(gate_input)
    retain = jax.nn.sigmoid(-gate_input)
    candidate = cand_pre.astype(jnp.float32)
    drive_term = (update * candidate).at[0].add(retain[0] * initial)
    _, states = lax.associative_scan(compose, (retain, drive_term), axis=0)
    state_rows = states.astype(jnp.bfloat16)
    mixed_rows = (residual + jnp.dot(state_rows, w_out, preferred_element_type=jnp.float32)).astype(jnp.bfloat16)
    back_grads = jnp.dot(seq_grads, w_out.T, preferred_element_type=jnp.float32).astype(jnp.bfloat16)
    next_retain = jnp.concatenate([retain[1:], jnp.zeros((1, retain.shape[1]), jnp.float32)], axis=0)
    _, carried = lax.associative_scan(compose, (next_retain, back_grads.astype(jnp.float32)), axis=0, reverse=True)
    first_grad = retain[0] * carried[0]
    earlier_states = jnp.concatenate([initial[None, :], states[:-1]], axis=0)
    gate_grad = carried * (candidate - earlier_states) * update * retain
    cand_grad = carried * update
    bias_terms = lax.optimization_barrier(jnp.sum(gate_grad, axis=0))
    normed_grad = jnp.dot(gate_grad.astype(jnp.bfloat16), w_gate.T, preferred_element_type=jnp.float32)
    normed_grad = normed_grad + jnp.dot(cand_grad.astype(jnp.bfloat16), w_cand.T, preferred_element_type=jnp.float32)
    unit_grad = normed_grad * norm_gain
    input_rows = inverse_rms * (unit_grad - unit_rows * lax.optimization_barrier(jnp.mean(unit_grad * unit_rows, axis=-1, keepdims=True)))
    token_grad = (seq_grads.astype(jnp.float32) + input_rows).astype(jnp.bfloat16)
    return (mixed_rows, token_grad, first_grad, bias_terms)

def reference(inputs, output_grad, norm_gain, gate_bias, state_in, w_gate, w_cand, w_out):
    worker = partial(one_sequence, norm_gain, gate_bias, w_gate, w_cand, w_out)
    layer_out, input_grad, state_grad, bias_terms = lax.map(worker, (inputs, output_grad, state_in))
    return (layer_out, input_grad, state_grad, lax.optimization_barrier(jnp.sum(bias_terms, axis=0)))
```

```python
import functools

import jax
import jax.numpy as jnp
from jax import lax
from jax.experimental import pallas as pl
from jax.experimental.pallas import tpu as pltpu
from jax.sharding import PartitionSpec as P

EPSILON = 1e-06
SEGMENTS = 8
VMEM_LIMIT = 48 * 1024 * 1024
F32 = jnp.float32
BF16 = jnp.bfloat16


def params(semantics=None):
    return pltpu.CompilerParams(vmem_limit_bytes=VMEM_LIMIT, dimension_semantics=semantics)


def cost(flops, moved):
    return pl.CostEstimate(flops=int(flops), bytes_accessed=int(moved), transcendentals=0)


def hop(value, offset, count):
    return lax.ppermute(value, "seq", [(i, i ^ offset) for i in range(count)])


def swap_batch(value, offset, count):
    return lax.ppermute(value, "batch", [(i, i ^ offset) for i in range(count)])


def after(value, *earlier):
    return lax.optimization_barrier((value,) + earlier)[0]


def spread_over_cube(first, second, third, batches, ranks):
    half = first.shape[0] // 2
    cut = lambda w: [w[:half], w[half:]]
    f, s, t = {0: cut(first)}, {0: cut(second)}, {0: cut(third)}
    send = lambda value, offset: hop(value, offset, ranks)
    f2a, f4a = send(f[0][0], 2), send(f[0][0], 4)
    f2b, f4b = send(f[0][1], 2), send(f[0][1], 4)
    f6a = send(f2a, 4)
    f6b = send(f4b, 2)
    f[2], f[4], f[6] = [f2a, f2b], [f4a, f4b], [f6a, f6b]
    t2a, t4a = send(after(t[0][0], f2a), 2), send(after(t[0][0], f4a), 4)
    t2b, t4b = send(after(t[0][1], f2b), 2), send(after(t[0][1], f4b), 4)
    t6a = send(t2a, 4)
    t6b = send(t4b, 2)
    t[2], t[4], t[6] = [t2a, t2b], [t4a, t4b], [t6a, t6b]
    for offset in (2, 4, 6):
        s[offset] = [swap_batch(piece, 1, batches) for piece in f[offset]]
    for shards in (f, t, s):
        for offset in (0, 2, 4, 6):
            shards[offset + 1] = [send(piece, 1) for piece in shards[offset]]
    flat = lambda shards: [piece for offset in range(8) for piece in shards[offset]]
    return flat(f), flat(s), flat(t)


def from_every_rank(value, ranks):
    if ranks & (ranks - 1) == 0 and ranks <= 8:
        return [value] + [hop(value, offset, ranks) for offset in range(1, ranks)]
    return [lax.all_gather(value, "seq")]


def place(first_row_is_ordered, rows):
    steps = rows // SEGMENTS
    out = lax.broadcasted_iota(jnp.int32, (rows, rows), 0)
    inn = lax.broadcasted_iota(jnp.int32, (rows, rows), 1)
    if not first_row_is_ordered:
        out, inn = inn, out
    source = lax.rem(out, SEGMENTS) * steps + lax.div(out, SEGMENTS)
    return (source == inn).astype(F32).astype(BF16)


def dot(a, b):
    return lax.dot_general(a, b, (((1,), (0,)), ((), ())), preferred_element_type=F32)


def dot_t(a, b):
    return lax.dot_general(a, b, (((1,), (1,)), ((), ())), preferred_element_type=F32)


def joined(refs, cuts):
    blocks = []
    for start in range(0, len(refs), cuts):
        group = refs[start : start + cuts]
        blocks.append(group[0][...] if cuts == 1 else jnp.concatenate([r[...] for r in group], axis=0))
    return blocks


def norm_kernel(x_ref, g_ref, gain_ref, normed_ref, grads_ref, hold):
    rows, width = x_ref.shape
    step = min(32, rows)

    @pl.loop(0, rows // step)
    def _(index):
        span = pl.ds(pl.multiple_of(index * step, step), step)
        x = x_ref[span, :].astype(F32)
        scale = lax.rsqrt(jnp.mean(x * x, axis=-1, keepdims=True) + EPSILON)
        hold[span, :] = (x * scale * gain_ref[...]).astype(BF16)

    order = place(True, rows)
    tile = min(512, width)

    @pl.loop(0, width // tile)
    def _(index):
        span = pl.ds(pl.multiple_of(index * tile, tile), tile)
        normed_ref[:, span] = dot(order, hold[:, span]).astype(BF16)
        grads_ref[:, span] = dot(order, g_ref[:, span]).astype(BF16)


def norm_call(x, g, gain):
    return pl.pallas_call(
        norm_kernel,
        out_shape=[jax.ShapeDtypeStruct(x.shape, BF16)] * 2,
        in_specs=[pl.BlockSpec(memory_space=pltpu.VMEM)] * 3,
        out_specs=[pl.BlockSpec(memory_space=pltpu.VMEM)] * 2,
        scratch_shapes=[pltpu.VMEM(x.shape, BF16)],
        compiler_params=params(),
        cost_estimate=cost(4 * x.shape[0] * x.size, 8 * x.size),
        name="norm_rows",
    )(x, g, gain)


def column_product(where_ref, x_ref, refs, cuts):
    total = None
    for index, block in enumerate(joined(refs, cuts)):
        depth = block.shape[0]
        start = pl.multiple_of((where_ref[0] ^ index) * depth, depth)
        term = dot(x_ref[:, pl.ds(start, depth)], block)
        total = term if total is None else total + term
    return total


def weight_specs(pieces, tile):
    return [pl.BlockSpec((p.shape[0], tile), lambda j, *_: (0, j)) for p in pieces]


def project_call(where, x, pieces, cuts, tile):
    rows, width = x.shape[0], pieces[0].shape[1]

    def kernel(where_ref, x_ref, *refs):
        refs[-1][...] = column_product(where_ref, x_ref, refs[:-1], cuts).astype(BF16)

    return pl.pallas_call(
        kernel,
        grid_spec=pltpu.PrefetchScalarGridSpec(
            num_scalar_prefetch=1,
            grid=(width // tile,),
            in_specs=[pl.BlockSpec(x.shape, lambda j, *_: (0, 0))] + weight_specs(pieces, tile),
            out_specs=pl.BlockSpec((rows, tile), lambda j, *_: (0, j)),
        ),
        out_shape=jax.ShapeDtypeStruct((rows, width), BF16),
        compiler_params=params(("arbitrary",)),
        cost_estimate=cost(2 * x.size * width, 2 * x.shape[1] * width),
        name="project",
    )(where, x, *pieces)


def row_products(where_ref, total, pairs, cuts):
    first = pl.program_id(0) == 0
    blocks = [joined(refs, cuts) for _, refs in pairs]
    for index in range(len(blocks[0])):
        depth = blocks[0][index].shape[0]
        start = pl.multiple_of((where_ref[0] ^ index) * depth, depth)
        span = pl.ds(start, depth)
        term = None
        for (x, _), group in zip(pairs, blocks):
            part = dot_t(x, group[index])
            term = part if term is None else term + part

        @pl.when(first)
        def _():
            total[:, span] = term

        @pl.when(jnp.logical_not(first))
        def _():
            total[:, span] += term


def back_call(where, grads, pieces, cuts, tile):
    rows, width = grads.shape
    out_width = sum(p.shape[0] for p in pieces)

    def kernel(where_ref, g_ref, *refs):
        refs, out_ref, total = refs[:-2], refs[-2], refs[-1]
        row_products(where_ref, total, [(g_ref[...], refs)], cuts)

        @pl.when(pl.program_id(0) == pl.num_programs(0) - 1)
        def _():
            out_ref[...] = total[...].astype(BF16)

    return pl.pallas_call(
        kernel,
        grid_spec=pltpu.PrefetchScalarGridSpec(
            num_scalar_prefetch=1,
            grid=(width // tile,),
            in_specs=[pl.BlockSpec((rows, tile), lambda j, *_: (0, j))] + weight_specs(pieces, tile),
            out_specs=pl.BlockSpec((rows, out_width), lambda j, *_: (0, 0)),
            scratch_shapes=[pltpu.VMEM((rows, out_width), F32)],
        ),
        out_shape=jax.ShapeDtypeStruct((rows, out_width), BF16),
        compiler_params=params(("arbitrary",)),
        cost_estimate=cost(2 * grads.size * out_width, 2 * width * out_width),
        name="back_rows",
    )(where, grads, *pieces)


def gates(x):
    small = jnp.exp(-jnp.abs(x))
    large = 1.0 / (1.0 + small)
    small = small * large
    up = x >= 0
    return jnp.where(up, large, small), jnp.where(up, small, large)


def slab_pair(ref, pair):
    span = pl.ds(pl.multiple_of(pair * 2 * SEGMENTS, 2 * SEGMENTS), 2 * SEGMENTS)
    both = ref[span, :].astype(F32)
    return both[:SEGMENTS], both[SEGMENTS:]


def choose(where_ref, one, other):
    straight = where_ref[1] == 0
    return jnp.where(straight, one, other), jnp.where(straight, other, one)


def totals_call(where, x, pieces, cuts, first_pre, back, bias, tile):
    rows, width = first_pre.shape
    pairs = rows // (2 * SEGMENTS)

    def kernel(where_ref, x_ref, first_ref, back_ref, bias_ref, *refs):
        refs, (second_ref, parts_ref, whole_ref) = refs[:-3], refs[-3:]
        second_ref[...] = column_product(where_ref, x_ref, refs, cuts).astype(BF16)
        bias = bias_ref[...]

        def body(pair, carry):
            keep, state, leaving = carry
            for a, b, g in zip(slab_pair(first_ref, pair), slab_pair(second_ref, pair), slab_pair(back_ref, pair)):
                gate, cand = choose(where_ref, a, b)
                update, retain = gates(gate + bias)
                keep = keep * retain
                state = retain * state + update * cand
                leaving = leaving + keep * g
            return keep, state, leaving

        zero = jnp.zeros((SEGMENTS, tile), F32)
        keep, state, leaving = lax.fori_loop(0, pairs, body, (zero + 1.0, zero, zero))
        parts_ref[0], parts_ref[1], parts_ref[2] = keep, state, leaving
        whole_keep, whole_state = keep[0:1], state[0:1]
        for s in range(1, SEGMENTS):
            whole_state = keep[s : s + 1] * whole_state + state[s : s + 1]
            whole_keep = whole_keep * keep[s : s + 1]
        whole_leaving = leaving[SEGMENTS - 1 :]
        for s in range(SEGMENTS - 2, -1, -1):
            whole_leaving = keep[s : s + 1] * whole_leaving + leaving[s : s + 1]
        whole_ref[0:1], whole_ref[1:2], whole_ref[2:3] = whole_keep, whole_state, whole_leaving

    column = lambda j, *_: (0, j)
    return pl.pallas_call(
        kernel,
        grid_spec=pltpu.PrefetchScalarGridSpec(
            num_scalar_prefetch=1,
            grid=(width // tile,),
            in_specs=[
                pl.BlockSpec(x.shape, lambda j, *_: (0, 0)),
                pl.BlockSpec((rows, tile), column),
                pl.BlockSpec((rows, tile), column),
                pl.BlockSpec((1, tile), column),
            ]
            + weight_specs(pieces, tile),
            out_specs=[
                pl.BlockSpec((rows, tile), column),
                pl.BlockSpec((3, SEGMENTS, tile), lambda j, *_: (0, 0, j)),
                pl.BlockSpec((3, tile), column),
            ],
        ),
        out_shape=[
            jax.ShapeDtypeStruct((rows, width), BF16),
            jax.ShapeDtypeStruct((3, SEGMENTS, width), F32),
            jax.ShapeDtypeStruct((3, width), F32),
        ],
        compiler_params=params(("arbitrary",)),
        cost_estimate=cost(2 * x.size * width, 2 * x.shape[1] * width),
        name="project_totals",
    )(where, x, first_pre, back, bias, *pieces)


def scan_call(where, first_pre, second_pre, back, bias, initial, parts, wholes, ranks, tile):
    rows, width = first_pre.shape
    pairs = rows // (2 * SEGMENTS)
    stacked = len(wholes) == 1 and ranks > 1

    def kernel(where_ref, first_ref, second_ref, back_ref, bias_ref, initial_ref, parts_ref, *refs):
        whole_refs = refs[: len(wholes)]
        (state_ref, one_ref, other_ref, bias_grad_ref, state_grad_ref) = refs[len(wholes) : len(wholes) + 5]
        hold, kept, updates, slopes, one_hold, other_hold, state_hold = refs[len(wholes) + 5 :]
        me = where_ref[0]
        if stacked:

            @pl.loop(0, ranks)
            def _(rank):
                hold[rank, 0:3] = whole_refs[0][rank]
        else:
            for offset, ref in enumerate(whole_refs):
                hold[me ^ offset, 0:3] = ref[...]

        entering = initial_ref[...]
        for rank in range(ranks):
            block = hold[rank]
            entering = jnp.where(rank < me, block[0:1] * entering + block[1:2], entering)
        arriving = state_grad = hold[0, 2:3] * 0.0
        for rank in range(ranks - 1, -1, -1):
            block = hold[rank]
            arriving = jnp.where(rank == me, state_grad, arriving)
            state_grad = block[0:1] * state_grad + block[2:3]
        state_grad_ref[...] = state_grad

        keep, ends, leaves = parts_ref[0], parts_ref[1], parts_ref[2]
        starts = [entering]
        for s in range(SEGMENTS - 1):
            starts.append(keep[s : s + 1] * starts[-1] + ends[s : s + 1])
        tails = [arriving]
        for s in range(SEGMENTS - 1, 0, -1):
            tails.append(keep[s : s + 1] * tails[-1] + leaves[s : s + 1])
        start = jnp.concatenate(starts, axis=0)
        tail = jnp.concatenate(tails[::-1], axis=0)
        bias = bias_ref[...]

        def span_of(pair):
            return pl.ds(pl.multiple_of(pair * 2 * SEGMENTS, 2 * SEGMENTS), 2 * SEGMENTS)

        def forward(pair, state):
            states, retains, ups, slope = [], [], [], []
            for a, b in zip(slab_pair(first_ref, pair), slab_pair(second_ref, pair)):
                gate, cand = choose(where_ref, a, b)
                update, retain = gates(gate + bias)
                retains.append(retain)
                ups.append(update)
                slope.append((cand - state) * update * retain)
                state = retain * state + update * cand
                states.append(state)
            span = span_of(pair)
            state_hold[span, :] = jnp.concatenate(states, axis=0).astype(BF16)
            kept[span, :] = jnp.concatenate(retains, axis=0)
            updates[span, :] = jnp.concatenate(ups, axis=0)
            slopes[span, :] = jnp.concatenate(slope, axis=0)
            return state

        lax.fori_loop(0, pairs, forward, start)

        def backward(count, carry):
            leaving, total = carry
            pair = pairs - 1 - count
            span = span_of(pair)
            grads = slab_pair(back_ref, pair)
            retain, update, slope = kept[span, :], updates[span, :], slopes[span, :]
            late = grads[1] + leaving
            early = grads[0] + retain[SEGMENTS:] * late
            leaving = retain[:SEGMENTS] * early
            carried = jnp.concatenate([early, late], axis=0)
            gate_grad = carried * slope
            cand_grad = carried * update
            total = total + gate_grad[:SEGMENTS] + gate_grad[SEGMENTS:]
            one, other = choose(where_ref, gate_grad, cand_grad)
            one_hold[span, :] = one.astype(BF16)
            other_hold[span, :] = other.astype(BF16)
            return leaving, total

        _, total = lax.fori_loop(0, pairs, backward, (tail, jnp.zeros((SEGMENTS, tile), F32)))
        bias_grad_ref[...] = jnp.sum(total, axis=0, keepdims=True)
        order = place(False, rows)
        state_ref[...] = dot(order, state_hold[...]).astype(BF16)
        one_ref[...] = dot(order, one_hold[...]).astype(BF16)
        other_ref[...] = dot(order, other_hold[...]).astype(BF16)

    column = lambda j, *_: (0, j)
    deep = lambda j, *_: (0, 0, j)
    block = pl.BlockSpec((rows, tile), column)
    row = pl.BlockSpec((1, tile), column)
    whole_specs = [pl.BlockSpec((ranks, 3, tile), deep)] if stacked else [pl.BlockSpec((3, tile), column)] * len(wholes)
    wide = jax.ShapeDtypeStruct((rows, width), BF16)
    flat = jax.ShapeDtypeStruct((1, width), F32)
    return pl.pallas_call(
        kernel,
        grid_spec=pltpu.PrefetchScalarGridSpec(
            num_scalar_prefetch=1,
            grid=(width // tile,),
            in_specs=[block, block, block, row, row, pl.BlockSpec((3, SEGMENTS, tile), deep)] + whole_specs,
            out_specs=[block, block, block, row, row],
            scratch_shapes=[pltpu.VMEM((ranks, SEGMENTS, tile), F32)]
            + [pltpu.VMEM((rows, tile), F32)] * 3
            + [pltpu.VMEM((rows, tile), BF16)] * 3,
        ),
        out_shape=[wide, wide, wide, flat, flat],
        compiler_params=params(("arbitrary",)),
        cost_estimate=cost(6 * rows * rows * width, 12 * rows * width),
        name="scan_rows",
    )(where, first_pre, second_pre, back, bias, initial, parts, *wholes)


def layer_call(where, state_rows, residual, pieces, cuts, tile):
    rows, width = residual.shape

    def kernel(where_ref, x_ref, residual_ref, *refs):
        total = column_product(where_ref, x_ref, refs[:-1], cuts)
        refs[-1][...] = (residual_ref[...].astype(F32) + total).astype(BF16)

    column = lambda j, *_: (0, j)
    return pl.pallas_call(
        kernel,
        grid_spec=pltpu.PrefetchScalarGridSpec(
            num_scalar_prefetch=1,
            grid=(width // tile,),
            in_specs=[pl.BlockSpec(state_rows.shape, lambda j, *_: (0, 0)), pl.BlockSpec((rows, tile), column)]
            + weight_specs(pieces, tile),
            out_specs=pl.BlockSpec((rows, tile), column),
        ),
        out_shape=jax.ShapeDtypeStruct((rows, width), BF16),
        compiler_params=params(("arbitrary",)),
        cost_estimate=cost(2 * state_rows.size * width, 2 * state_rows.shape[1] * width),
        name="layer_rows",
    )(where, state_rows, residual, *pieces)


def input_grad_call(where, one, other, first, second, cuts, x, grads, gain, tile):
    rows, width = x.shape
    hidden = one.shape[1]

    def kernel(where_ref, one_ref, other_ref, x_ref, grads_ref, gain_ref, *refs):
        first_refs, second_refs = refs[: len(first)], refs[len(first) : len(first) + len(second)]
        out_ref, total = refs[-2], refs[-1]
        row_products(where_ref, total, [(one_ref[...], first_refs), (other_ref[...], second_refs)], cuts)

        @pl.when(pl.program_id(0) == pl.num_programs(0) - 1)
        def _():
            step = min(32, rows)

            @pl.loop(0, rows // step)
            def _(index):
                span = pl.ds(pl.multiple_of(index * step, step), step)
                x = x_ref[span, :].astype(F32)
                scale = lax.rsqrt(jnp.mean(x * x, axis=-1, keepdims=True) + EPSILON)
                unit = x * scale
                unit_grad = total[span, :] * gain_ref[...]
                along = jnp.mean(unit_grad * unit, axis=-1, keepdims=True)
                out = grads_ref[span, :].astype(F32) + scale * (unit_grad - unit * along)
                out_ref[span, :] = out.astype(BF16)

    column = lambda j, *_: (0, j)
    whole = pl.BlockSpec((rows, width), lambda j, *_: (0, 0))
    block = pl.BlockSpec((rows, tile), column)
    return pl.pallas_call(
        kernel,
        grid_spec=pltpu.PrefetchScalarGridSpec(
            num_scalar_prefetch=1,
            grid=(hidden // tile,),
            in_specs=[block, block, whole, whole, pl.BlockSpec((1, width), lambda j, *_: (0, 0))]
            + weight_specs(first, tile)
            + weight_specs(second, tile),
            out_specs=whole,
            scratch_shapes=[pltpu.VMEM((rows, width), F32)],
        ),
        out_shape=jax.ShapeDtypeStruct((rows, width), BF16),
        compiler_params=params(("arbitrary",)),
        cost_estimate=cost(4 * one.size * width, 4 * hidden * width),
        name="input_grad_rows",
    )(where, one, other, x, grads, gain, *first, *second)


def on_device(ranks, batches, inputs, output_grad, norm_gain, gate_bias, state_in, w_gate, w_cand, w_out):
    rows_in, grad_rows = inputs[0], output_grad[0]
    gain = norm_gain[None, :]
    hidden = w_gate.shape[1]
    tile = min(512, hidden)
    me = lax.axis_index("seq")
    cube = ranks == 8 and batches > 1 and batches & (batches - 1) == 0
    if cube:
        turned = lax.axis_index("batch") % 2
        first = jnp.where(turned == 0, w_gate, w_cand)
        second = jnp.where(turned == 0, w_cand, w_gate)
        first, second, third = spread_over_cube(first, second, w_out, batches, ranks)
        cuts = 2
        block_me = me
    else:
        turned = jnp.zeros((), jnp.int32)
        first, second, third = ([lax.all_gather(w, "seq", tiled=True)] for w in (w_gate, w_cand, w_out))
        cuts = 1
        block_me = jnp.zeros((), jnp.int32)
    where = jnp.stack([block_me, turned]).astype(jnp.int32)
    where_scan = jnp.stack([me, turned]).astype(jnp.int32)
    rows_both = lax.all_gather(jnp.stack([gate_bias, state_in[0]]), "seq", axis=1, tiled=True)
    bias, initial = rows_both[0:1], rows_both[1:2]

    normed, grads = norm_call(rows_in, grad_rows, gain)
    first_pre = project_call(where, normed, first, cuts, tile)
    back = back_call(where, grads, third, cuts, tile)
    second_pre, parts, whole = totals_call(where, normed, second, cuts, first_pre, back, bias, tile)
    wholes = from_every_rank(whole, ranks)
    state_rows, one, other, bias_part, state_grad = scan_call(
        where_scan, first_pre, second_pre, back, bias, initial, parts, wholes, ranks, tile
    )
    width = hidden // ranks
    if cube:
        over_seq = sum(hop(bias_part, offset, ranks) for offset in range(1, ranks)) + bias_part
        over_all = sum(swap_batch(over_seq, offset, batches) for offset in range(1, batches)) + over_seq
        bias_grad = lax.dynamic_slice_in_dim(over_all[0], me * width, width, 0)
    else:
        bias_grad = lax.psum(lax.psum_scatter(bias_part[0], "seq", scatter_dimension=0, tiled=True), "batch")
    layer_out = layer_call(where, state_rows, rows_in, third, cuts, tile)
    input_grad = input_grad_call(where, one, other, first, second, cuts, rows_in, grad_rows, gain, tile)
    state_out = lax.dynamic_slice_in_dim(state_grad, me * width, width, 1)
    return (layer_out[None], input_grad[None], state_out, bias_grad)


def solution(mesh):
    body = functools.partial(on_device, mesh.shape["seq"], mesh.shape["batch"])
    rows = P("batch", "seq", None)
    return jax.shard_map(
        body,
        mesh=mesh,
        in_specs=(rows, rows, P(), P("seq"), P("batch", "seq"), P("seq", None), P("seq", None), P("seq", None)),
        out_specs=(rows, rows, P("batch", "seq"), P("seq")),
        check_vma=False,
    )
```

```python
import functools

import jax
import jax.numpy as jnp
from jax import lax
from jax.experimental import pallas as pl
from jax.experimental.pallas import tpu as pltpu
from jax.sharding import PartitionSpec as P

EPSILON = 1e-06
SEGMENTS = 8
F32 = jnp.float32
BF16 = jnp.bfloat16


def params(mebibytes):
    return pltpu.CompilerParams(vmem_limit_bytes=mebibytes * 1024 * 1024)


def cost(flops, moved):
    return pl.CostEstimate(flops=int(flops), bytes_accessed=int(moved), transcendentals=0)


def hop(value, offset, count):
    return lax.ppermute(value, "seq", [(i, i ^ offset) for i in range(count)])


def swap_batch(value, offset, count):
    return lax.ppermute(value, "batch", [(i, i ^ offset) for i in range(count)])


def after(values, *earlier):
    return lax.optimization_barrier(tuple(values) + tuple(earlier))[: len(values)]


def place(rows):
    steps = rows // SEGMENTS
    out = lax.broadcasted_iota(jnp.int32, (rows, rows), 0)
    inn = lax.broadcasted_iota(jnp.int32, (rows, rows), 1)
    source = lax.rem(out, SEGMENTS) * steps + lax.div(out, SEGMENTS)
    return (source == inn).astype(F32).astype(BF16)


def place_back(rows):
    steps = rows // SEGMENTS
    out = lax.broadcasted_iota(jnp.int32, (rows, rows), 0)
    inn = lax.broadcasted_iota(jnp.int32, (rows, rows), 1)
    source = lax.rem(out, steps) * SEGMENTS + lax.div(out, steps)
    return (source == inn).astype(F32).astype(BF16)


def dot(a, b):
    return lax.dot_general(a, b, (((1,), (0,)), ((), ())), preferred_element_type=F32)


def tiles(count, tile, body):
    @pl.loop(0, count // tile)
    def _(index):
        body(pl.ds(pl.multiple_of(index * tile, tile), tile))


class Shards:
    def __init__(self, groups):
        self.groups = groups
        self.pieces = [piece for group in groups for piece in group]
        self.depth = sum(piece.shape[0] for piece in groups[0])
        self.width = groups[0][0].shape[1]

    def copies(self, refs, buffer, sems, slot_of):
        out, position = [], 0
        for index, group in enumerate(self.groups):
            start, made = slot_of(index) * self.depth, []
            for piece in group:
                rows = piece.shape[0]
                made.append(
                    pltpu.make_async_copy(refs[position], buffer.at[pl.ds(start, rows), :], sems.at[position])
                )
                start, position = start + rows, position + 1
            out.append(made)
        return out


VMEM_SPEC = pl.BlockSpec(memory_space=pltpu.VMEM)
SMEM_SPEC = pl.BlockSpec(memory_space=pltpu.SMEM)
ANY_SPEC = pl.BlockSpec(memory_space=pl.ANY)


def norm_call(where, x, g, gain, depth):
    rows, width = x.shape

    def kernel(where_ref, x_ref, g_ref, gain_ref, normed_ref, grads_ref, hold):
        def rows_body(span):
            x = x_ref[span, :].astype(F32)
            scale = lax.rsqrt(jnp.mean(x * x, axis=-1, keepdims=True) + EPSILON)
            hold[span, :] = (x * scale * gain_ref[...]).astype(BF16)

        tiles(rows, min(32, rows), rows_body)
        order = place(rows)
        for index in range(width // depth):
            source = pl.ds(pl.multiple_of((where_ref[0] ^ index) * depth, depth), depth)
            normed_ref[:, index * depth : (index + 1) * depth] = dot(order, hold[:, source]).astype(BF16)

        def grads_body(span):
            grads_ref[span, :] = dot(order, g_ref[:, span]).T.astype(BF16)

        tiles(width, min(512, width), grads_body)

    return pl.pallas_call(
        kernel,
        out_shape=[jax.ShapeDtypeStruct((rows, width), BF16), jax.ShapeDtypeStruct((width, rows), BF16)],
        in_specs=[SMEM_SPEC] + [VMEM_SPEC] * 3,
        out_specs=[VMEM_SPEC] * 2,
        scratch_shapes=[pltpu.VMEM(x.shape, BF16)],
        compiler_params=params(12),
        cost_estimate=cost(4 * rows * x.size, 8 * x.size),
        name="norm_rows",
    )(where, x, g, gain)


def project_call(x, shards, tile, dtype, skip=0):
    rows, width = x.shape[0], shards.width
    count, depth = len(shards.groups), shards.depth
    span_in = slice(skip, skip + count * depth)

    def kernel(x_ref, *refs):
        refs, (out_ref, held, sems) = refs[:-3], refs[-3:]
        copies = [c for made in shards.copies(refs, held, sems, lambda i: i) for c in made]
        for c in copies:
            c.start()
        for c in copies:
            c.wait()

        def body(span):
            out_ref[:, span] = dot(x_ref[:, span_in], held[:, span]).astype(dtype)

        tiles(width, tile, body)

    return pl.pallas_call(
        kernel,
        out_shape=jax.ShapeDtypeStruct((rows, width), dtype),
        in_specs=[VMEM_SPEC] + [ANY_SPEC] * len(shards.pieces),
        out_specs=VMEM_SPEC,
        scratch_shapes=[
            pltpu.VMEM((count * depth, width), BF16),
            pltpu.SemaphoreType.DMA((len(shards.pieces),)),
        ],
        compiler_params=params(16),
        cost_estimate=cost(2 * rows * count * depth * width, 2 * count * depth * width),
        name="project",
    )(x, *shards.pieces)


def back_call(where, grads, shards):
    width, rows = grads.shape
    count, depth = len(shards.groups), shards.depth

    def kernel(where_ref, g_ref, *refs):
        refs, (out_ref, held, sems) = refs[:-3], refs[-3:]
        copies = shards.copies(refs, held, sems, lambda i: i)
        for made in copies:
            for c in made:
                c.start()
        for index, made in enumerate(copies):
            for c in made:
                c.wait()
            target = pl.multiple_of((where_ref[0] ^ index) * depth, depth)
            for part in range(0, depth, min(depth, 256)):
                size = min(depth, 256)
                block = held[index * depth + part : index * depth + part + size, :]
                out_ref[:, pl.ds(pl.multiple_of(target + part, size), size)] = dot(block, g_ref[...]).T.astype(BF16)

    return pl.pallas_call(
        kernel,
        out_shape=jax.ShapeDtypeStruct((rows, count * depth), BF16),
        in_specs=[SMEM_SPEC, VMEM_SPEC] + [ANY_SPEC] * len(shards.pieces),
        out_specs=VMEM_SPEC,
        scratch_shapes=[
            pltpu.VMEM((count * depth, width), BF16),
            pltpu.SemaphoreType.DMA((len(shards.pieces),)),
        ],
        compiler_params=params(16),
        cost_estimate=cost(2 * rows * count * depth * width, 2 * count * depth * width),
        name="back_rows",
    )(where, grads, *shards.pieces)


def gates(x):
    small = jnp.exp(-jnp.abs(x))
    large = 1.0 / (1.0 + small)
    small = small * large
    up = x >= 0
    return jnp.where(up, large, small), jnp.where(up, small, large)


def slab_pair(ref, pair, span):
    both = ref[pair * 2 * SEGMENTS : (pair + 1) * 2 * SEGMENTS, span].astype(F32)
    return both[:SEGMENTS], both[SEGMENTS:]


def choose(where_ref, one, other):
    straight = where_ref[1] == 0
    return jnp.where(straight, one, other), jnp.where(straight, other, one)


def totals_call(where, x, partial, shards, skip, first_pre, back, bias, tile):
    rows, width = first_pre.shape
    pairs = rows // (2 * SEGMENTS)
    count, depth = len(shards.groups), shards.depth
    extra = [] if partial is None else [partial]

    def kernel(where_ref, x_ref, first_ref, back_ref, bias_ref, *refs):
        partial_refs, refs = refs[: len(extra)], refs[len(extra) :]
        refs, (second_ref, parts_ref, whole_ref, held, sems) = refs[:-5], refs[-5:]
        copies = [c for made in shards.copies(refs, held, sems, lambda i: i) for c in made]
        for c in copies:
            c.start()
        for c in copies:
            c.wait()

        def body(span):
            total = dot(x_ref[:, skip : skip + count * depth], held[:, span])
            for ref in partial_refs:
                total = total + ref[:, span]
            second_ref[:, span] = total.astype(BF16)
            bias = bias_ref[:, span]
            keep = jnp.ones((SEGMENTS, tile), F32)
            state = leaving = jnp.zeros((SEGMENTS, tile), F32)
            for pair in range(pairs):
                slabs = [slab_pair(ref, pair, span) for ref in (first_ref, second_ref, back_ref)]
                for a, b, g in zip(*slabs):
                    gate, cand = choose(where_ref, a, b)
                    update, retain = gates(gate + bias)
                    keep = keep * retain
                    state = retain * state + update * cand
                    leaving = leaving + keep * g
            parts_ref[0, :, span], parts_ref[1, :, span], parts_ref[2, :, span] = keep, state, leaving
            whole_keep, whole_state = keep[0:1], state[0:1]
            for s in range(1, SEGMENTS):
                whole_state = keep[s : s + 1] * whole_state + state[s : s + 1]
                whole_keep = whole_keep * keep[s : s + 1]
            whole_leaving = leaving[SEGMENTS - 1 :]
            for s in range(SEGMENTS - 2, -1, -1):
                whole_leaving = keep[s : s + 1] * whole_leaving + leaving[s : s + 1]
            whole_ref[0:1, span], whole_ref[1:2, span], whole_ref[2:3, span] = whole_keep, whole_state, whole_leaving

        tiles(width, tile, body)

    return pl.pallas_call(
        kernel,
        out_shape=[
            jax.ShapeDtypeStruct((rows, width), BF16),
            jax.ShapeDtypeStruct((3, SEGMENTS, width), F32),
            jax.ShapeDtypeStruct((3, width), F32),
        ],
        in_specs=[SMEM_SPEC] + [VMEM_SPEC] * (4 + len(extra)) + [ANY_SPEC] * len(shards.pieces),
        out_specs=[VMEM_SPEC] * 3,
        scratch_shapes=[
            pltpu.VMEM((count * depth, width), BF16),
            pltpu.SemaphoreType.DMA((len(shards.pieces),)),
        ],
        compiler_params=params(20),
        cost_estimate=cost(2 * rows * count * depth * width, 2 * count * depth * width),
        name="project_totals",
    )(where, x, first_pre, back, bias, *extra, *shards.pieces)


def scan_call(where, first_pre, second_pre, back, bias, initial, parts, wholes, ranks, tile):
    rows, width = first_pre.shape
    pairs = rows // (2 * SEGMENTS)

    def kernel(where_ref, first_ref, second_ref, back_ref, bias_ref, initial_ref, parts_ref, wholes_ref, *refs):
        (state_ref, one_ref, other_ref, bias_grad_ref, state_grad_ref) = refs[:5]
        kept, updates, slopes, one_hold, other_hold, state_hold = refs[5:]
        me = where_ref[2]
        order = place_back(rows)

        def body(span):
            entering = initial_ref[:, span]
            blocks = [wholes_ref[rank, :, span] for rank in range(ranks)]
            for rank in range(ranks):
                block = blocks[rank]
                entering = jnp.where(rank < me, block[0:1] * entering + block[1:2], entering)
            arriving = state_grad = blocks[0][2:3] * 0.0
            for rank in range(ranks - 1, -1, -1):
                block = blocks[rank]
                arriving = jnp.where(rank == me, state_grad, arriving)
                state_grad = block[0:1] * state_grad + block[2:3]
            state_grad_ref[:, span] = state_grad
            keep, ends, leaves = parts_ref[0, :, span], parts_ref[1, :, span], parts_ref[2, :, span]
            starts = [entering]
            for s in range(SEGMENTS - 1):
                starts.append(keep[s : s + 1] * starts[-1] + ends[s : s + 1])
            tails = [arriving]
            for s in range(SEGMENTS - 1, 0, -1):
                tails.append(keep[s : s + 1] * tails[-1] + leaves[s : s + 1])
            state = jnp.concatenate(starts, axis=0)
            leaving = jnp.concatenate(tails[::-1], axis=0)
            bias = bias_ref[:, span]

            for pair in range(pairs):
                states, retains, ups, slope = [], [], [], []
                for a, b in zip(slab_pair(first_ref, pair, span), slab_pair(second_ref, pair, span)):
                    gate, cand = choose(where_ref, a, b)
                    update, retain = gates(gate + bias)
                    retains.append(retain)
                    ups.append(update)
                    slope.append((cand - state) * update * retain)
                    state = retain * state + update * cand
                    states.append(state)
                here = slice(pair * 2 * SEGMENTS, (pair + 1) * 2 * SEGMENTS)
                state_hold[here, :] = jnp.concatenate(states, axis=0).astype(BF16)
                kept[here, :] = jnp.concatenate(retains, axis=0)
                updates[here, :] = jnp.concatenate(ups, axis=0)
                slopes[here, :] = jnp.concatenate(slope, axis=0)

            total = jnp.zeros((SEGMENTS, tile), F32)
            for pair in range(pairs - 1, -1, -1):
                here = slice(pair * 2 * SEGMENTS, (pair + 1) * 2 * SEGMENTS)
                grads = slab_pair(back_ref, pair, span)
                retain, update, slope = kept[here, :], updates[here, :], slopes[here, :]
                late = grads[1] + leaving
                early = grads[0] + retain[SEGMENTS:] * late
                leaving = retain[:SEGMENTS] * early
                carried = jnp.concatenate([early, late], axis=0)
                gate_grad = carried * slope
                cand_grad = carried * update
                total = total + gate_grad[:SEGMENTS] + gate_grad[SEGMENTS:]
                one, other = choose(where_ref, gate_grad, cand_grad)
                one_hold[here, :] = one.astype(BF16)
                other_hold[here, :] = other.astype(BF16)
            bias_grad_ref[:, span] = jnp.sum(total, axis=0, keepdims=True)
            state_ref[:, span] = dot(order, state_hold[...]).astype(BF16)
            one_ref[span, :] = dot(order, one_hold[...]).T.astype(BF16)
            other_ref[span, :] = dot(order, other_hold[...]).T.astype(BF16)

        tiles(width, tile, body)

    wide = jax.ShapeDtypeStruct((rows, width), BF16)
    tall = jax.ShapeDtypeStruct((width, rows), BF16)
    flat = jax.ShapeDtypeStruct((1, width), F32)
    return pl.pallas_call(
        kernel,
        out_shape=[wide, tall, tall, flat, flat],
        in_specs=[SMEM_SPEC] + [VMEM_SPEC] * 7,
        out_specs=[VMEM_SPEC] * 5,
        scratch_shapes=[pltpu.VMEM((rows, tile), F32)] * 3 + [pltpu.VMEM((rows, tile), BF16)] * 3,
        compiler_params=params(16),
        cost_estimate=cost(6 * rows * rows * width, 12 * rows * width),
        name="scan_rows",
    )(where, first_pre, second_pre, back, bias, initial, parts, wholes)


def layer_call(where, state_rows, residual, shards, tile):
    rows, width = residual.shape
    count, depth = len(shards.groups), shards.depth

    def kernel(where_ref, x_ref, residual_ref, *refs):
        refs, (out_ref, held, ordered, sems) = refs[:-4], refs[-4:]
        copies = [c for made in shards.copies(refs, held, sems, lambda i: i) for c in made]
        for c in copies:
            c.start()
        for index in range(count):
            source = pl.ds(pl.multiple_of((where_ref[0] ^ index) * depth, depth), depth)
            ordered[:, index * depth : (index + 1) * depth] = x_ref[:, source]
        for c in copies:
            c.wait()

        def body(span):
            out_ref[:, span] = (residual_ref[:, span].astype(F32) + dot(ordered[...], held[:, span])).astype(BF16)

        tiles(width, tile, body)

    return pl.pallas_call(
        kernel,
        out_shape=jax.ShapeDtypeStruct((rows, width), BF16),
        in_specs=[SMEM_SPEC] + [VMEM_SPEC] * 2 + [ANY_SPEC] * len(shards.pieces),
        out_specs=VMEM_SPEC,
        scratch_shapes=[
            pltpu.VMEM((count * depth, width), BF16),
            pltpu.VMEM((rows, count * depth), BF16),
            pltpu.SemaphoreType.DMA((len(shards.pieces),)),
        ],
        compiler_params=params(18),
        cost_estimate=cost(2 * rows * count * depth * width, 2 * count * depth * width),
        name="layer_rows",
    )(where, state_rows, residual, *shards.pieces)


def input_grad_call(where, one, other, first, second, x, grads, gain):
    rows, width = x.shape
    hidden = one.shape[0]
    count, depth = len(first.groups), first.depth
    slots = min(count, 4)

    def kernel(where_ref, one_ref, other_ref, x_ref, grads_ref, gain_ref, *refs):
        first_refs = refs[: len(first.pieces)]
        second_refs = refs[len(first.pieces) : len(first.pieces) + len(second.pieces)]
        out_ref, first_held, second_held, total, first_sems, second_sems = refs[-6:]
        copies = [
            a + b
            for a, b in zip(
                first.copies(first_refs, first_held, first_sems, lambda i: i % slots),
                second.copies(second_refs, second_held, second_sems, lambda i: i % slots),
            )
        ]
        for made in copies[:slots]:
            for c in made:
                c.start()
        size = min(depth, 256)
        for index, made in enumerate(copies):
            for c in made:
                c.wait()
            target = pl.multiple_of((where_ref[0] ^ index) * depth, depth)
            for part in range(0, depth, size):
                here = slice(index % slots * depth + part, index % slots * depth + part + size)
                term = dot(first_held[here, :], one_ref[...]) + dot(second_held[here, :], other_ref[...])
                total[:, pl.ds(pl.multiple_of(target + part, size), size)] = term.T
            if index + slots < count:
                for c in copies[index + slots]:
                    c.start()

        def body(span):
            x = x_ref[span, :].astype(F32)
            scale = lax.rsqrt(jnp.mean(x * x, axis=-1, keepdims=True) + EPSILON)
            unit = x * scale
            unit_grad = total[span, :] * gain_ref[...]
            along = jnp.mean(unit_grad * unit, axis=-1, keepdims=True)
            out = grads_ref[span, :].astype(F32) + scale * (unit_grad - unit * along)
            out_ref[span, :] = out.astype(BF16)

        tiles(rows, min(32, rows), body)

    return pl.pallas_call(
        kernel,
        out_shape=jax.ShapeDtypeStruct((rows, width), BF16),
        in_specs=[SMEM_SPEC] + [VMEM_SPEC] * 5 + [ANY_SPEC] * (len(first.pieces) + len(second.pieces)),
        out_specs=VMEM_SPEC,
        scratch_shapes=[
            pltpu.VMEM((slots * depth, hidden), BF16),
            pltpu.VMEM((slots * depth, hidden), BF16),
            pltpu.VMEM((rows, width), F32),
            pltpu.SemaphoreType.DMA((len(first.pieces),)),
            pltpu.SemaphoreType.DMA((len(second.pieces),)),
        ],
        compiler_params=params(24),
        cost_estimate=cost(4 * one.size * width, 4 * hidden * width),
        name="input_grad_rows",
    )(where, one, other, x, grads, gain, *first.pieces, *second.pieces)


def gathered_rows(gate_bias, state_in):
    both = lax.all_gather(jnp.stack([gate_bias, state_in[0]]), "seq", axis=1, tiled=True)
    return both[0:1], both[1:2]


def front_on_cube(ranks, batches, where, turned, tile, rows_in, grad_rows, gain, gate_bias, state_in, w_gate, w_cand, w_out):
    half = w_gate.shape[0] // 2
    depth = w_gate.shape[0]
    halves = lambda w: (w[:half], w[half:])
    straight = turned == 0
    own_f = [jnp.where(straight, a, b) for a, b in zip(halves(w_gate), halves(w_cand))]
    send = lambda value, offset: hop(value, offset, ranks)
    core = lambda value: hop(value, 1, ranks)
    over = lambda value: swap_batch(value, 1, batches)

    f2a, f4a = send(own_f[0], 2), send(own_f[0], 4)
    f2b, f4b = send(own_f[1], 2), send(own_f[1], 4)
    own_s = jnp.where(straight, w_cand, w_gate)
    own_t = halves(w_out)
    f1 = [core(v) for v in own_f]
    s1, t1 = core(own_s), core(w_out)
    bias, initial = gathered_rows(gate_bias, state_in)
    normed, grads = norm_call(where, rows_in, grad_rows, gain, depth)

    f2a, f4a, t2a_in, normed, grads, bias, initial = after((f2a, f4a, own_t[0], normed, grads, bias, initial))
    t2a, f6a, s2a = send(t2a_in, 2), send(f2a, 4), over(f2a)
    f3a, f5a = core(f2a), core(f4a)
    f2b, f4b, t4a_in, s4a_in = after((f2b, f4b, own_t[0], f4a))
    f6b, t4a, s4a = send(f4b, 2), send(t4a_in, 4), over(s4a_in)
    f3b, f5b = core(f2b), core(f4b)
    t2a, f6a, t2b_in, t4b_in, s2b_in = after((t2a, f6a, own_t[1], own_t[1], f2b), f6a)
    t2b, t4b, s2b = send(t2b_in, 2), send(t4b_in, 4), over(s2b_in)
    f7a, t3a = core(f6a), core(t2a)
    f6b, t4a, s2a, t2a_in, s4b_in = after((f6b, t4a, s2a, t2a, f4b))
    t6a, s4b = send(t2a_in, 4), over(s4b_in)
    f7b, t5a, s3a = core(f6b), core(t4a), core(s2a)
    first = Shards([own_f, f1, [f2a, f2b], [f3a, f3b], [f4a, f4b], [f5a, f5b], [f6a, f6b], [f7a, f7b]])
    first_pre = project_call(normed, first, tile, BF16)
    t2b, t4b, s4a, s6a_in, first_pre = after((t2b, t4b, s4a, f6a, first_pre))
    t6b, s6a = send(t4b, 2), over(s6a_in)
    t3b, t5b, s5a = core(t2b), core(t4b), core(s4a)
    t6a, t6b, s2b, s4b, s6b_in = after((t6a, t6b, s2b, s4b, f6b))
    s6b = over(s6b_in)
    t7a, t7b, s3b, s5b = core(t6a), core(t6b), core(s2b), core(s4b)
    third = Shards([[w_out], [t1], [t2a, t2b], [t3a, t3b], [t4a, t4b], [t5a, t5b], [t6a, t6b], [t7a, t7b]])
    (s6a,) = after((s6a,), t7b)
    s7a = core(s6a)
    most = [[own_s], [s1], [s2a, s2b], [s3a, s3b], [s4a, s4b], [s5a, s5b]]
    back = back_call(where, grads, third)
    partial = project_call(normed, Shards(most), tile, F32)
    s6b, back, partial = after((s6b, back, partial))
    s7b = core(s6b)
    last = [[s6a, s6b], [s7a, s7b]]
    second = Shards(most + last)
    second_pre, parts, whole = totals_call(
        where, normed, partial, Shards(last), len(most) * depth, first_pre, back, bias, tile
    )
    return first, second, third, first_pre, second_pre, back, bias, initial, parts, whole


def front(where, tile, rows_in, grad_rows, gain, gate_bias, state_in, w_gate, w_cand, w_out):
    first, second, third = (
        Shards([[lax.all_gather(w, "seq", tiled=True)]]) for w in (w_gate, w_cand, w_out)
    )
    bias, initial = gathered_rows(gate_bias, state_in)
    normed, grads = norm_call(where, rows_in, grad_rows, gain, first.depth)
    first_pre = project_call(normed, first, tile, BF16)
    back = back_call(where, grads, third)
    second_pre, parts, whole = totals_call(where, normed, None, second, 0, first_pre, back, bias, tile)
    return first, second, third, first_pre, second_pre, back, bias, initial, parts, whole


def on_device(ranks, batches, inputs, output_grad, norm_gain, gate_bias, state_in, w_gate, w_cand, w_out):
    rows_in, grad_rows = inputs[0], output_grad[0]
    gain = norm_gain[None, :]
    hidden = w_gate.shape[1]
    tile = min(512, hidden)
    me = lax.axis_index("seq")
    given = (rows_in, grad_rows, gain, gate_bias, state_in, w_gate, w_cand, w_out)
    if ranks == 8 and batches % 2 == 0:
        turned = lax.axis_index("batch") % 2
        where = jnp.stack([me, turned, me]).astype(jnp.int32)
        found = front_on_cube(ranks, batches, where, turned, tile, *given)
    else:
        nought = jnp.zeros_like(me)
        where = jnp.stack([nought, nought, me]).astype(jnp.int32)
        found = front(where, tile, *given)
    first, second, third, first_pre, second_pre, back, bias, initial, parts, whole = found
    wholes = lax.all_gather(whole, "seq")
    state_rows, one, other, bias_part, state_grad = scan_call(
        where, first_pre, second_pre, back, bias, initial, parts, wholes, ranks, tile
    )
    width = hidden // ranks
    everyone = lax.all_gather(bias_part[0], ("seq", "batch"))
    bias_grad = lax.dynamic_slice_in_dim(jnp.sum(everyone, axis=0), me * width, width, 0)
    layer_out = layer_call(where, state_rows, rows_in, third, tile)
    input_grad = input_grad_call(where, one, other, first, second, rows_in, grad_rows, gain)
    state_out = lax.dynamic_slice_in_dim(state_grad, me * width, width, 1)
    return (layer_out[None], input_grad[None], state_out, bias_grad)


def solution(mesh):
    body = functools.partial(on_device, mesh.shape["seq"], mesh.shape["batch"])
    rows = P("batch", "seq", None)
    return jax.shard_map(
        body,
        mesh=mesh,
        in_specs=(rows, rows, P(), P("seq"), P("batch", "seq"), P("seq", None), P("seq", None), P("seq", None)),
        out_specs=(rows, rows, P("batch", "seq"), P("seq")),
        check_vma=False,
    )
```

```python
import functools

import jax
import jax.numpy as jnp
from jax import lax
from jax.experimental import pallas as pl
from jax.experimental.pallas import tpu as pltpu
from jax.sharding import PartitionSpec as P

EPSILON = 1e-06
SEGMENTS = 8
F32 = jnp.float32
BF16 = jnp.bfloat16


def params(mebibytes):
    return pltpu.CompilerParams(vmem_limit_bytes=mebibytes * 1024 * 1024)


def cost(flops, moved):
    return pl.CostEstimate(flops=int(flops), bytes_accessed=int(moved), transcendentals=0)


def hop(value, offset, count):
    return lax.ppermute(value, "seq", [(i, i ^ offset) for i in range(count)])


def swap_batch(value, offset, count):
    return lax.ppermute(value, "batch", [(i, i ^ offset) for i in range(count)])


def after(values, *earlier):
    return lax.optimization_barrier(tuple(values) + tuple(earlier))[: len(values)]


def place(rows):
    steps = rows // SEGMENTS
    out = lax.broadcasted_iota(jnp.int32, (rows, rows), 0)
    inn = lax.broadcasted_iota(jnp.int32, (rows, rows), 1)
    source = lax.rem(out, SEGMENTS) * steps + lax.div(out, SEGMENTS)
    return (source == inn).astype(F32).astype(BF16)


def place_back(rows):
    steps = rows // SEGMENTS
    out = lax.broadcasted_iota(jnp.int32, (rows, rows), 0)
    inn = lax.broadcasted_iota(jnp.int32, (rows, rows), 1)
    source = lax.rem(out, steps) * SEGMENTS + lax.div(out, steps)
    return (source == inn).astype(F32).astype(BF16)


def dot(a, b):
    return lax.dot_general(a, b, (((1,), (0,)), ((), ())), preferred_element_type=F32)


def tiles(count, tile, body):
    @pl.loop(0, count // tile)
    def _(index):
        body(pl.ds(pl.multiple_of(index * tile, tile), tile))


class Shards:
    def __init__(self, groups):
        self.groups = groups
        self.pieces = [piece for group in groups for piece in group]
        self.depth = sum(piece.shape[0] for piece in groups[0])
        self.width = groups[0][0].shape[1]

    def operands(self):
        return [pltpu.with_memory_space_constraint(piece, pltpu.VMEM) for piece in self.pieces]

    def block(self, refs, index, part, size):
        position = sum(len(group) for group in self.groups[:index])
        found, start = [], 0
        for offset, piece in enumerate(self.groups[index]):
            rows = piece.shape[0]
            low, high = max(part, start), min(part + size, start + rows)
            if low < high:
                found.append(refs[position + offset][low - start : high - start, :])
            start += rows
        return found[0] if len(found) == 1 else jnp.concatenate(found, axis=0)

    def columns(self, refs, span):
        found = [ref[:, span] for ref in refs]
        return found[0] if len(found) == 1 else jnp.concatenate(found, axis=0)


VMEM_SPEC = pl.BlockSpec(memory_space=pltpu.VMEM)
SMEM_SPEC = pl.BlockSpec(memory_space=pltpu.SMEM)


def norm_call(where, x, g, gain, depth):
    rows, width = x.shape

    def kernel(where_ref, x_ref, g_ref, gain_ref, normed_ref, grads_ref, hold):
        def rows_body(span):
            x = x_ref[span, :].astype(F32)
            scale = lax.rsqrt(jnp.mean(x * x, axis=-1, keepdims=True) + EPSILON)
            hold[span, :] = (x * scale * gain_ref[...]).astype(BF16)

        tiles(rows, min(32, rows), rows_body)
        order = place(rows)
        for index in range(width // depth):
            source = pl.ds(pl.multiple_of((where_ref[0] ^ index) * depth, depth), depth)
            normed_ref[:, index * depth : (index + 1) * depth] = dot(order, hold[:, source]).astype(BF16)

        def grads_body(span):
            grads_ref[span, :] = dot(order, g_ref[:, span]).T.astype(BF16)

        tiles(width, min(512, width), grads_body)

    return pl.pallas_call(
        kernel,
        out_shape=[jax.ShapeDtypeStruct((rows, width), BF16), jax.ShapeDtypeStruct((width, rows), BF16)],
        in_specs=[SMEM_SPEC] + [VMEM_SPEC] * 3,
        out_specs=[VMEM_SPEC] * 2,
        scratch_shapes=[pltpu.VMEM(x.shape, BF16)],
        compiler_params=params(14),
        cost_estimate=cost(4 * rows * x.size, 8 * x.size),
        name="norm_rows",
    )(where, x, g, gain)


def project_call(x, shards, tile, dtype, skip=0):
    rows, width = x.shape[0], shards.width
    count, depth = len(shards.groups), shards.depth
    span_in = slice(skip, skip + count * depth)

    def kernel(x_ref, *refs):
        refs, out_ref = refs[:-1], refs[-1]

        def body(span):
            out_ref[:, span] = dot(x_ref[:, span_in], shards.columns(refs, span)).astype(dtype)

        tiles(width, tile, body)

    return pl.pallas_call(
        kernel,
        out_shape=jax.ShapeDtypeStruct((rows, width), dtype),
        in_specs=[VMEM_SPEC] + [VMEM_SPEC] * len(shards.pieces),
        out_specs=VMEM_SPEC,
        compiler_params=params(14),
        cost_estimate=cost(2 * rows * count * depth * width, 2 * count * depth * width),
        name="project",
    )(x, *shards.operands())


def back_call(where, grads, shards):
    width, rows = grads.shape
    count, depth = len(shards.groups), shards.depth

    def kernel(where_ref, g_ref, *refs):
        refs, out_ref = refs[:-1], refs[-1]
        size = min(depth, 256)
        for index in range(count):
            for part in range(0, depth, size):
                target = pl.multiple_of((where_ref[0] ^ index) * depth + part, size)
                term = dot(shards.block(refs, index, part, size), g_ref[...])
                out_ref[:, pl.ds(target, size)] = term.T.astype(BF16)

    return pl.pallas_call(
        kernel,
        out_shape=jax.ShapeDtypeStruct((rows, count * depth), BF16),
        in_specs=[SMEM_SPEC, VMEM_SPEC] + [VMEM_SPEC] * len(shards.pieces),
        out_specs=VMEM_SPEC,
        compiler_params=params(14),
        cost_estimate=cost(2 * rows * count * depth * width, 2 * count * depth * width),
        name="back_rows",
    )(where, grads, *shards.operands())


def gates(x):
    small = jnp.exp(-jnp.abs(x))
    large = 1.0 / (1.0 + small)
    small = small * large
    up = x >= 0
    return jnp.where(up, large, small), jnp.where(up, small, large)


def slab_pair(ref, pair, span):
    both = ref[pair * 2 * SEGMENTS : (pair + 1) * 2 * SEGMENTS, span].astype(F32)
    return both[:SEGMENTS], both[SEGMENTS:]


def choose(where_ref, one, other):
    straight = where_ref[1] == 0
    return jnp.where(straight, one, other), jnp.where(straight, other, one)


def totals_call(where, x, partial, shards, skip, first_pre, back, bias, tile):
    rows, width = first_pre.shape
    pairs = rows // (2 * SEGMENTS)
    count, depth = len(shards.groups), shards.depth
    extra = [] if partial is None else [partial]

    def kernel(where_ref, x_ref, first_ref, back_ref, bias_ref, *refs):
        partial_refs, refs = refs[: len(extra)], refs[len(extra) :]
        refs, (second_ref, parts_ref, whole_ref) = refs[:-3], refs[-3:]

        def body(span):
            total = dot(x_ref[:, skip : skip + count * depth], shards.columns(refs, span))
            for ref in partial_refs:
                total = total + ref[:, span]
            second_ref[:, span] = total.astype(BF16)
            bias = bias_ref[:, span]
            keep = jnp.ones((SEGMENTS, tile), F32)
            state = leaving = jnp.zeros((SEGMENTS, tile), F32)
            for pair in range(pairs):
                slabs = [slab_pair(ref, pair, span) for ref in (first_ref, second_ref, back_ref)]
                for a, b, g in zip(*slabs):
                    gate, cand = choose(where_ref, a, b)
                    update, retain = gates(gate + bias)
                    keep = keep * retain
                    state = retain * state + update * cand
                    leaving = leaving + keep * g
            parts_ref[0, :, span], parts_ref[1, :, span], parts_ref[2, :, span] = keep, state, leaving
            whole_keep, whole_state = keep[0:1], state[0:1]
            for s in range(1, SEGMENTS):
                whole_state = keep[s : s + 1] * whole_state + state[s : s + 1]
                whole_keep = whole_keep * keep[s : s + 1]
            whole_leaving = leaving[SEGMENTS - 1 :]
            for s in range(SEGMENTS - 2, -1, -1):
                whole_leaving = keep[s : s + 1] * whole_leaving + leaving[s : s + 1]
            whole_ref[0:1, span], whole_ref[1:2, span], whole_ref[2:3, span] = whole_keep, whole_state, whole_leaving

        tiles(width, tile, body)

    return pl.pallas_call(
        kernel,
        out_shape=[
            jax.ShapeDtypeStruct((rows, width), BF16),
            jax.ShapeDtypeStruct((3, SEGMENTS, width), F32),
            jax.ShapeDtypeStruct((3, width), F32),
        ],
        in_specs=[SMEM_SPEC] + [VMEM_SPEC] * (4 + len(extra)) + [VMEM_SPEC] * len(shards.pieces),
        out_specs=[VMEM_SPEC] * 3,
        compiler_params=params(14),
        cost_estimate=cost(2 * rows * count * depth * width, 2 * count * depth * width),
        name="project_totals",
    )(where, x, first_pre, back, bias, *extra, *shards.operands())


def scan_call(where, first_pre, second_pre, back, bias, initial, parts, wholes, ranks, tile):
    rows, width = first_pre.shape
    pairs = rows // (2 * SEGMENTS)

    def kernel(where_ref, first_ref, second_ref, back_ref, bias_ref, initial_ref, parts_ref, wholes_ref, *refs):
        (state_ref, one_ref, other_ref, bias_grad_ref, state_grad_ref) = refs[:5]
        kept, updates, slopes, one_hold, other_hold, state_hold = refs[5:]
        me = where_ref[2]
        order = place_back(rows)

        def body(span):
            entering = initial_ref[:, span]
            blocks = [wholes_ref[rank, :, span] for rank in range(ranks)]
            for rank in range(ranks):
                block = blocks[rank]
                entering = jnp.where(rank < me, block[0:1] * entering + block[1:2], entering)
            arriving = state_grad = blocks[0][2:3] * 0.0
            for rank in range(ranks - 1, -1, -1):
                block = blocks[rank]
                arriving = jnp.where(rank == me, state_grad, arriving)
                state_grad = block[0:1] * state_grad + block[2:3]
            state_grad_ref[:, span] = state_grad
            keep, ends, leaves = parts_ref[0, :, span], parts_ref[1, :, span], parts_ref[2, :, span]
            starts = [entering]
            for s in range(SEGMENTS - 1):
                starts.append(keep[s : s + 1] * starts[-1] + ends[s : s + 1])
            tails = [arriving]
            for s in range(SEGMENTS - 1, 0, -1):
                tails.append(keep[s : s + 1] * tails[-1] + leaves[s : s + 1])
            state = jnp.concatenate(starts, axis=0)
            leaving = jnp.concatenate(tails[::-1], axis=0)
            bias = bias_ref[:, span]

            for pair in range(pairs):
                states, retains, ups, slope = [], [], [], []
                for a, b in zip(slab_pair(first_ref, pair, span), slab_pair(second_ref, pair, span)):
                    gate, cand = choose(where_ref, a, b)
                    update, retain = gates(gate + bias)
                    retains.append(retain)
                    ups.append(update)
                    slope.append((cand - state) * update * retain)
                    state = retain * state + update * cand
                    states.append(state)
                here = slice(pair * 2 * SEGMENTS, (pair + 1) * 2 * SEGMENTS)
                state_hold[here, :] = jnp.concatenate(states, axis=0).astype(BF16)
                kept[here, :] = jnp.concatenate(retains, axis=0)
                updates[here, :] = jnp.concatenate(ups, axis=0)
                slopes[here, :] = jnp.concatenate(slope, axis=0)

            total = jnp.zeros((SEGMENTS, tile), F32)
            for pair in range(pairs - 1, -1, -1):
                here = slice(pair * 2 * SEGMENTS, (pair + 1) * 2 * SEGMENTS)
                grads = slab_pair(back_ref, pair, span)
                retain, update, slope = kept[here, :], updates[here, :], slopes[here, :]
                late = grads[1] + leaving
                early = grads[0] + retain[SEGMENTS:] * late
                leaving = retain[:SEGMENTS] * early
                carried = jnp.concatenate([early, late], axis=0)
                gate_grad = carried * slope
                cand_grad = carried * update
                total = total + gate_grad[:SEGMENTS] + gate_grad[SEGMENTS:]
                one, other = choose(where_ref, gate_grad, cand_grad)
                one_hold[here, :] = one.astype(BF16)
                other_hold[here, :] = other.astype(BF16)
            bias_grad_ref[:, span] = jnp.sum(total, axis=0, keepdims=True)
            state_ref[:, span] = dot(order, state_hold[...]).astype(BF16)
            one_ref[span, :] = dot(order, one_hold[...]).T.astype(BF16)
            other_ref[span, :] = dot(order, other_hold[...]).T.astype(BF16)

        tiles(width, tile, body)

    wide = jax.ShapeDtypeStruct((rows, width), BF16)
    tall = jax.ShapeDtypeStruct((width, rows), BF16)
    flat = jax.ShapeDtypeStruct((1, width), F32)
    return pl.pallas_call(
        kernel,
        out_shape=[wide, tall, tall, flat, flat],
        in_specs=[SMEM_SPEC] + [VMEM_SPEC] * 7,
        out_specs=[VMEM_SPEC] * 5,
        scratch_shapes=[pltpu.VMEM((rows, tile), F32)] * 3 + [pltpu.VMEM((rows, tile), BF16)] * 3,
        compiler_params=params(14),
        cost_estimate=cost(6 * rows * rows * width, 12 * rows * width),
        name="scan_rows",
    )(where, first_pre, second_pre, back, bias, initial, parts, wholes)


def layer_call(where, state_rows, residual, shards, tile):
    rows, width = residual.shape
    count, depth = len(shards.groups), shards.depth

    def kernel(where_ref, x_ref, residual_ref, *refs):
        refs, (out_ref, ordered) = refs[:-2], refs[-2:]
        for index in range(count):
            source = pl.ds(pl.multiple_of((where_ref[0] ^ index) * depth, depth), depth)
            ordered[:, index * depth : (index + 1) * depth] = x_ref[:, source]

        def body(span):
            total = dot(ordered[...], shards.columns(refs, span))
            out_ref[:, span] = (residual_ref[:, span].astype(F32) + total).astype(BF16)

        tiles(width, tile, body)

    return pl.pallas_call(
        kernel,
        out_shape=jax.ShapeDtypeStruct((rows, width), BF16),
        in_specs=[SMEM_SPEC] + [VMEM_SPEC] * 2 + [VMEM_SPEC] * len(shards.pieces),
        out_specs=VMEM_SPEC,
        scratch_shapes=[pltpu.VMEM((rows, count * depth), BF16)],
        compiler_params=params(14),
        cost_estimate=cost(2 * rows * count * depth * width, 2 * count * depth * width),
        name="layer_rows",
    )(where, state_rows, residual, *shards.operands())


def input_grad_call(where, one, other, first, second, x, grads, gain):
    rows, width = x.shape
    hidden = one.shape[0]
    count, depth = len(first.groups), first.depth

    def kernel(where_ref, one_ref, other_ref, x_ref, grads_ref, gain_ref, *refs):
        first_refs = refs[: len(first.pieces)]
        second_refs = refs[len(first.pieces) : len(first.pieces) + len(second.pieces)]
        out_ref, total = refs[-2:]
        size = min(depth, 256)
        for index in range(count):
            for part in range(0, depth, size):
                target = pl.multiple_of((where_ref[0] ^ index) * depth + part, size)
                term = dot(first.block(first_refs, index, part, size), one_ref[...])
                term = term + dot(second.block(second_refs, index, part, size), other_ref[...])
                total[:, pl.ds(target, size)] = term.T

        def body(span):
            x = x_ref[span, :].astype(F32)
            scale = lax.rsqrt(jnp.mean(x * x, axis=-1, keepdims=True) + EPSILON)
            unit = x * scale
            unit_grad = total[span, :] * gain_ref[...]
            along = jnp.mean(unit_grad * unit, axis=-1, keepdims=True)
            out = grads_ref[span, :].astype(F32) + scale * (unit_grad - unit * along)
            out_ref[span, :] = out.astype(BF16)

        tiles(rows, min(32, rows), body)

    return pl.pallas_call(
        kernel,
        out_shape=jax.ShapeDtypeStruct((rows, width), BF16),
        in_specs=[SMEM_SPEC] + [VMEM_SPEC] * 5 + [VMEM_SPEC] * (len(first.pieces) + len(second.pieces)),
        out_specs=VMEM_SPEC,
        scratch_shapes=[pltpu.VMEM((rows, width), F32)],
        compiler_params=params(14),
        cost_estimate=cost(4 * one.size * width, 4 * hidden * width),
        name="input_grad_rows",
    )(where, one, other, x, grads, gain, *first.operands(), *second.operands())


def gathered_rows(gate_bias, state_in):
    both = lax.all_gather(jnp.stack([gate_bias, state_in[0]]), "seq", axis=1, tiled=True)
    return both[0:1], both[1:2]


def front_on_cube(ranks, batches, where, turned, tile, rows_in, grad_rows, gain, gate_bias, state_in, w_gate, w_cand, w_out):
    half = w_gate.shape[0] // 2
    depth = w_gate.shape[0]
    halves = lambda w: (w[:half], w[half:])
    straight = turned == 0
    send = lambda value, offset: hop(value, offset, ranks)
    core = lambda value: hop(value, 1, ranks)
    over = lambda value: swap_batch(value, 1, batches)
    me = lax.axis_index("seq")

    def in_order(value, came, offset):
        low = (me // offset) % 2 == 0
        return jnp.where(low, jnp.concatenate([value, came], axis=1), jnp.concatenate([came, value], axis=1))

    own_f = [jnp.where(straight, a, b) for a, b in zip(halves(w_gate), halves(w_cand))]
    f2a, f4a = send(own_f[0], 2), send(own_f[0], 4)
    f1 = [core(v) for v in own_f]
    both = jnp.stack([gate_bias, state_in[0]])
    came = core(both)
    normed, grads = norm_call(where, rows_in, grad_rows, gain, depth)
    f2a, f4a, f1a, f1b, came, normed, grads, f_b, own_t, own_s0, own_s1 = after(
        (f2a, f4a, f1[0], f1[1], came, normed, grads, own_f[1], w_out, w_gate, w_cand)
    )
    f1 = [f1a, f1b]
    both = in_order(both, came, 1)
    t_a, t_b = halves(own_t)
    came = send(both, 2)
    f2b, f4b = send(f_b, 2), send(f_b, 4)
    s2a, s4a = over(f2a), over(f4a)
    t2a, t4a = send(t_a, 2), send(t_a, 4)
    f3a, f5a = core(f2a), core(f4a)
    own_s = jnp.where(straight, own_s1, own_s0)
    s1, t1 = core(own_s), core(own_t)
    came, f2b, f4b, s2a, s4a, t2a, t4a, f3a, f5a, s1, t1, own_s, t_b, f2a, both = after(
        (came, f2b, f4b, s2a, s4a, t2a, t4a, f3a, f5a, s1, t1, own_s, t_b, f2a, both)
    )
    both = in_order(both, came, 2)
    came = send(both, 4)
    f6a, f6b = send(f2a, 4), send(f4b, 2)
    s2b, s4b = over(f2b), over(f4b)
    t2b, t4b = send(t_b, 2), send(t_b, 4)
    f3b, f5b, s3a, s5a, t3a, t5a = core(f2b), core(f4b), core(s2a), core(s4a), core(t2a), core(t4a)
    came, f6a, f6b, s2b, s4b, t2b, t4b, f3b, f5b, s3a, s5a, t3a, t5a, both, t2a = after(
        (came, f6a, f6b, s2b, s4b, t2b, t4b, f3b, f5b, s3a, s5a, t3a, t5a, both, t2a)
    )
    both = in_order(both, came, 4)
    bias, initial = both[0:1], both[1:2]
    s6a, s6b = over(f6a), over(f6b)
    t6a, t6b = send(t2a, 4), send(t4b, 2)
    f7a, f7b, s3b, s5b, t3b, t5b = core(f6a), core(f6b), core(s2b), core(s4b), core(t2b), core(t4b)
    first = Shards([own_f, f1, [f2a, f2b], [f3a, f3b], [f4a, f4b], [f5a, f5b], [f6a, f6b], [f7a, f7b]])
    most = [[own_s], [s1], [s2a, s2b], [s3a, s3b], [s4a, s4b], [s5a, s5b]]
    first_pre = project_call(normed, first, tile, BF16)
    t6a, t6b, s6a, first_pre, normed, grads = after((t6a, t6b, s6a, first_pre, normed, grads))
    t7a, t7b, s7a = core(t6a), core(t6b), core(s6a)
    third = Shards([[own_t], [t1], [t2a, t2b], [t3a, t3b], [t4a, t4b], [t5a, t5b], [t6a, t6b], [t7a, t7b]])
    partial = project_call(normed, Shards(most), tile, F32)
    back = back_call(where, grads, third)
    s6b, s7a, back, partial = after((s6b, s7a, back, partial))
    s7b = core(s6b)
    last = [[s6a, s6b], [s7a, s7b]]
    second = Shards(most + last)
    second_pre, parts, whole = totals_call(
        where, normed, partial, Shards(last), len(most) * depth, first_pre, back, bias, tile
    )
    return first, second, third, first_pre, second_pre, back, bias, initial, parts, whole


def front(where, tile, rows_in, grad_rows, gain, gate_bias, state_in, w_gate, w_cand, w_out):
    first, second, third = (
        Shards([[lax.all_gather(w, "seq", tiled=True)]]) for w in (w_gate, w_cand, w_out)
    )
    bias, initial = gathered_rows(gate_bias, state_in)
    normed, grads = norm_call(where, rows_in, grad_rows, gain, first.depth)
    first_pre = project_call(normed, first, tile, BF16)
    back = back_call(where, grads, third)
    second_pre, parts, whole = totals_call(where, normed, None, second, 0, first_pre, back, bias, tile)
    return first, second, third, first_pre, second_pre, back, bias, initial, parts, whole


def on_device(ranks, batches, inputs, output_grad, norm_gain, gate_bias, state_in, w_gate, w_cand, w_out):
    rows_in, grad_rows = inputs[0], output_grad[0]
    gain = norm_gain[None, :]
    hidden = w_gate.shape[1]
    tile = min(512, hidden)
    me = lax.axis_index("seq")
    given = (rows_in, grad_rows, gain, gate_bias, state_in, w_gate, w_cand, w_out)
    cube = ranks == 8 and batches in (2, 4, 8)
    if cube:
        turned = lax.axis_index("batch") % 2
        where = jnp.stack([me, turned, me]).astype(jnp.int32)
        found = front_on_cube(ranks, batches, where, turned, tile, *given)
    else:
        nought = jnp.zeros_like(me)
        where = jnp.stack([nought, nought, me]).astype(jnp.int32)
        found = front(where, tile, *given)
    first, second, third, first_pre, second_pre, back, bias, initial, parts, whole = found
    wholes = lax.all_gather(whole, "seq")
    state_rows, one, other, bias_part, state_grad = scan_call(
        where, first_pre, second_pre, back, bias, initial, parts, wholes, ranks, tile
    )
    width = hidden // ranks
    own_width = lambda row: lax.dynamic_slice_in_dim(row, me * width, width, 0)
    if cube:
        pair = bias_part + hop(bias_part, 1, ranks)
        near = [hop(pair, offset, ranks) for offset in (2, 4, 6)]
        layer_out = layer_call(where, state_rows, rows_in, third, tile)
        layer_out, *near = after((layer_out,) + tuple(near))
        plane = own_width((pair + near[0] + near[1] + near[2])[0])
        far = [swap_batch(plane, offset, batches) for offset in range(1, batches)]
        bias_grad = plane + sum(far[1:], far[0])
        one, other, plane = after((one, other, plane), layer_out)
    else:
        over_seq = lax.psum_scatter(bias_part[0], "seq", scatter_dimension=0, tiled=True)
        bias_grad = lax.psum(over_seq, "batch")
        layer_out = layer_call(where, state_rows, rows_in, third, tile)
    input_grad = input_grad_call(where, one, other, first, second, rows_in, grad_rows, gain)
    state_out = lax.dynamic_slice_in_dim(state_grad, me * width, width, 1)
    return (layer_out[None], input_grad[None], state_out, bias_grad)


def solution(mesh):
    body = functools.partial(on_device, mesh.shape["seq"], mesh.shape["batch"])
    rows = P("batch", "seq", None)
    return jax.shard_map(
        body,
        mesh=mesh,
        in_specs=(rows, rows, P(), P("seq"), P("batch", "seq"), P("seq", None), P("seq", None), P("seq", None)),
        out_specs=(rows, rows, P("batch", "seq"), P("seq")),
        check_vma=False,
    )
```

```python
import functools

import jax
import jax.numpy as jnp
from jax import lax
from jax.experimental import pallas as pl
from jax.experimental.pallas import tpu as pltpu
from jax.sharding import PartitionSpec as P

EPSILON = 1e-06
SEGMENTS = 8
F32 = jnp.float32
BF16 = jnp.bfloat16


def params(mebibytes):
    return pltpu.CompilerParams(vmem_limit_bytes=mebibytes * 1024 * 1024)


def cost(flops, moved):
    return pl.CostEstimate(flops=int(flops), bytes_accessed=int(moved), transcendentals=0)


def hop(value, offset, count):
    return lax.ppermute(value, "seq", [(i, i ^ offset) for i in range(count)])


def swap_batch(value, offset, count):
    return lax.ppermute(value, "batch", [(i, i ^ offset) for i in range(count)])


def after(values, *earlier):
    return lax.optimization_barrier(tuple(values) + tuple(earlier))[: len(values)]


def place(rows):
    steps = rows // SEGMENTS
    out = lax.broadcasted_iota(jnp.int32, (rows, rows), 0)
    inn = lax.broadcasted_iota(jnp.int32, (rows, rows), 1)
    source = lax.rem(out, SEGMENTS) * steps + lax.div(out, SEGMENTS)
    return (source == inn).astype(F32).astype(BF16)


def place_back(rows):
    steps = rows // SEGMENTS
    out = lax.broadcasted_iota(jnp.int32, (rows, rows), 0)
    inn = lax.broadcasted_iota(jnp.int32, (rows, rows), 1)
    source = lax.rem(out, steps) * SEGMENTS + lax.div(out, steps)
    return (source == inn).astype(F32).astype(BF16)


def dot(a, b):
    return lax.dot_general(a, b, (((1,), (0,)), ((), ())), preferred_element_type=F32)


def tiles(count, tile, body):
    @pl.loop(0, count // tile)
    def _(index):
        body(pl.ds(pl.multiple_of(index * tile, tile), tile))


class Shards:
    def __init__(self, groups):
        self.pieces, self.groups = [], []
        for group in groups:
            made = []
            for piece in group:
                array, start, rows = piece if isinstance(piece, tuple) else (piece, 0, piece.shape[0])
                known = [index for index, other in enumerate(self.pieces) if other is array]
                if not known:
                    known = [len(self.pieces)]
                    self.pieces.append(array)
                made.append((known[0], start, rows))
            self.groups.append(made)
        self.depth = sum(rows for _, _, rows in self.groups[0])
        self.width = self.pieces[0].shape[1]

    def operands(self):
        return [pltpu.with_memory_space_constraint(piece, pltpu.VMEM) for piece in self.pieces]

    def block(self, refs, index, part, size):
        found, begin = [], 0
        for which, start, rows in self.groups[index]:
            low, high = max(part, begin), min(part + size, begin + rows)
            if low < high:
                found.append(refs[which][start + low - begin : start + high - begin, :])
            begin += rows
        return found[0] if len(found) == 1 else jnp.concatenate(found, axis=0)

    def product(self, x_ref, skip, refs, span):
        total = None
        joint = max(1, min(len(self.groups), 4))
        for index in range(0, len(self.groups), joint):
            groups = self.groups[index : index + joint]
            found = [refs[which][start : start + rows, span] for group in groups for which, start, rows in group]
            block = found[0] if len(found) == 1 else jnp.concatenate(found, axis=0)
            start = skip + index * self.depth
            term = dot(x_ref[:, start : start + len(groups) * self.depth], block)
            total = term if total is None else total + term
        return total


VMEM_SPEC = pl.BlockSpec(memory_space=pltpu.VMEM)
SMEM_SPEC = pl.BlockSpec(memory_space=pltpu.SMEM)


def norm_call(where, x, g, gain, depth):
    rows, width = x.shape

    def kernel(where_ref, x_ref, g_ref, gain_ref, normed_ref, grads_ref, hold):
        def rows_body(span):
            x = x_ref[span, :].astype(F32)
            scale = lax.rsqrt(jnp.mean(x * x, axis=-1, keepdims=True) + EPSILON)
            hold[span, :] = (x * scale * gain_ref[...]).astype(BF16)

        tiles(rows, min(32, rows), rows_body)
        order = place(rows)
        for index in range(width // depth):
            source = pl.ds(pl.multiple_of((where_ref[0] ^ index) * depth, depth), depth)
            normed_ref[:, index * depth : (index + 1) * depth] = dot(order, hold[:, source]).astype(BF16)

        def grads_body(span):
            grads_ref[span, :] = dot(order, g_ref[:, span]).T.astype(BF16)

        tiles(width, min(512, width), grads_body)

    return pl.pallas_call(
        kernel,
        out_shape=[jax.ShapeDtypeStruct((rows, width), BF16), jax.ShapeDtypeStruct((width, rows), BF16)],
        in_specs=[SMEM_SPEC] + [VMEM_SPEC] * 3,
        out_specs=[VMEM_SPEC] * 2,
        scratch_shapes=[pltpu.VMEM(x.shape, BF16)],
        compiler_params=params(14),
        cost_estimate=cost(4 * rows * x.size, 8 * x.size),
        name="norm_rows",
    )(where, x, g, gain)


def project_call(x, shards, tile, dtype, skip=0):
    rows, width = x.shape[0], shards.width
    count, depth = len(shards.groups), shards.depth

    def kernel(x_ref, *refs):
        refs, out_ref = refs[:-1], refs[-1]

        def body(span):
            out_ref[:, span] = shards.product(x_ref, skip, refs, span).astype(dtype)

        tiles(width, tile, body)

    return pl.pallas_call(
        kernel,
        out_shape=jax.ShapeDtypeStruct((rows, width), dtype),
        in_specs=[VMEM_SPEC] + [VMEM_SPEC] * len(shards.pieces),
        out_specs=VMEM_SPEC,
        compiler_params=params(14),
        cost_estimate=cost(2 * rows * count * depth * width, 2 * count * depth * width),
        name="project",
    )(x, *shards.operands())


def back_call(where, grads, shards):
    width, rows = grads.shape
    count, depth = len(shards.groups), shards.depth

    def kernel(where_ref, g_ref, *refs):
        refs, out_ref = refs[:-1], refs[-1]
        size = min(depth, 256)
        for index in range(count):
            for part in range(0, depth, size):
                target = pl.multiple_of((where_ref[0] ^ index) * depth + part, size)
                term = dot(shards.block(refs, index, part, size), g_ref[...])
                out_ref[:, pl.ds(target, size)] = term.T.astype(BF16)

    return pl.pallas_call(
        kernel,
        out_shape=jax.ShapeDtypeStruct((rows, count * depth), BF16),
        in_specs=[SMEM_SPEC, VMEM_SPEC] + [VMEM_SPEC] * len(shards.pieces),
        out_specs=VMEM_SPEC,
        compiler_params=params(14),
        cost_estimate=cost(2 * rows * count * depth * width, 2 * count * depth * width),
        name="back_rows",
    )(where, grads, *shards.operands())


def gates(x):
    small = jnp.exp(-jnp.abs(x))
    large = 1.0 / (1.0 + small)
    small = small * large
    up = x >= 0
    return jnp.where(up, large, small), jnp.where(up, small, large)


def slab_pair(ref, pair, span):
    both = ref[pair * 2 * SEGMENTS : (pair + 1) * 2 * SEGMENTS, span].astype(F32)
    return both[:SEGMENTS], both[SEGMENTS:]


def choose(where_ref, one, other):
    straight = where_ref[1] == 0
    return jnp.where(straight, one, other), jnp.where(straight, other, one)


def totals_call(where, x, partial, shards, skip, first_pre, back, both, block, tile):
    rows, width = first_pre.shape
    pairs = rows // (2 * SEGMENTS)
    count, depth = len(shards.groups), shards.depth
    extra = [] if partial is None else [partial]

    def kernel(where_ref, x_ref, first_ref, back_ref, both_ref, *refs):
        partial_refs, refs = refs[: len(extra)], refs[len(extra) :]
        refs, (second_ref, parts_ref, whole_ref, rows_ref) = refs[:-4], refs[-4:]
        for index in range(width // block):
            target = pl.multiple_of((where_ref[0] ^ index) * block, block)
            rows_ref[:, pl.ds(target, block)] = both_ref[:, index * block : (index + 1) * block]

        def body(span):
            total = shards.product(x_ref, skip, refs, span)
            for ref in partial_refs:
                total = total + ref[:, span]
            second_ref[:, span] = total.astype(BF16)
            bias = rows_ref[0:1, span]
            keep = jnp.ones((SEGMENTS, tile), F32)
            state = leaving = jnp.zeros((SEGMENTS, tile), F32)
            for pair in range(pairs):
                slabs = [slab_pair(ref, pair, span) for ref in (first_ref, second_ref, back_ref)]
                for a, b, g in zip(*slabs):
                    gate, cand = choose(where_ref, a, b)
                    update, retain = gates(gate + bias)
                    keep = keep * retain
                    state = retain * state + update * cand
                    leaving = leaving + keep * g
            parts_ref[0, :, span], parts_ref[1, :, span], parts_ref[2, :, span] = keep, state, leaving
            whole_keep, whole_state = keep[0:1], state[0:1]
            for s in range(1, SEGMENTS):
                whole_state = keep[s : s + 1] * whole_state + state[s : s + 1]
                whole_keep = whole_keep * keep[s : s + 1]
            whole_leaving = leaving[SEGMENTS - 1 :]
            for s in range(SEGMENTS - 2, -1, -1):
                whole_leaving = keep[s : s + 1] * whole_leaving + leaving[s : s + 1]
            whole_ref[0:1, span], whole_ref[1:2, span], whole_ref[2:3, span] = whole_keep, whole_state, whole_leaving

        tiles(width, tile, body)

    return pl.pallas_call(
        kernel,
        out_shape=[
            jax.ShapeDtypeStruct((rows, width), BF16),
            jax.ShapeDtypeStruct((3, SEGMENTS, width), F32),
            jax.ShapeDtypeStruct((3, width), F32),
            jax.ShapeDtypeStruct((2, width), F32),
        ],
        in_specs=[SMEM_SPEC] + [VMEM_SPEC] * (4 + len(extra)) + [VMEM_SPEC] * len(shards.pieces),
        out_specs=[VMEM_SPEC] * 4,
        compiler_params=params(14),
        cost_estimate=cost(2 * rows * count * depth * width, 2 * count * depth * width),
        name="project_totals",
    )(where, x, first_pre, back, both, *extra, *shards.operands())


def scan_call(where, first_pre, second_pre, back, both, parts, wholes, ranks, tile):
    rows, width = first_pre.shape
    pairs = rows // (2 * SEGMENTS)

    def kernel(where_ref, first_ref, second_ref, back_ref, both_ref, parts_ref, wholes_ref, *refs):
        (state_ref, one_ref, other_ref, bias_grad_ref, state_grad_ref) = refs[:5]
        kept, updates, slopes, one_hold, other_hold, state_hold = refs[5:]
        me = where_ref[2]
        order = place_back(rows)

        def body(span):
            entering = both_ref[1:2, span]
            blocks = [wholes_ref[rank, :, span] for rank in range(ranks)]
            for rank in range(ranks):
                block = blocks[rank]
                entering = jnp.where(rank < me, block[0:1] * entering + block[1:2], entering)
            arriving = state_grad = blocks[0][2:3] * 0.0
            for rank in range(ranks - 1, -1, -1):
                block = blocks[rank]
                arriving = jnp.where(rank == me, state_grad, arriving)
                state_grad = block[0:1] * state_grad + block[2:3]
            state_grad_ref[:, span] = state_grad
            keep, ends, leaves = parts_ref[0, :, span], parts_ref[1, :, span], parts_ref[2, :, span]
            starts = [entering]
            for s in range(SEGMENTS - 1):
                starts.append(keep[s : s + 1] * starts[-1] + ends[s : s + 1])
            tails = [arriving]
            for s in range(SEGMENTS - 1, 0, -1):
                tails.append(keep[s : s + 1] * tails[-1] + leaves[s : s + 1])
            state = jnp.concatenate(starts, axis=0)
            leaving = jnp.concatenate(tails[::-1], axis=0)
            bias = both_ref[0:1, span]

            for pair in range(pairs):
                states, retains, ups, slope = [], [], [], []
                for a, b in zip(slab_pair(first_ref, pair, span), slab_pair(second_ref, pair, span)):
                    gate, cand = choose(where_ref, a, b)
                    update, retain = gates(gate + bias)
                    retains.append(retain)
                    ups.append(update)
                    slope.append((cand - state) * update * retain)
                    state = retain * state + update * cand
                    states.append(state)
                here = slice(pair * 2 * SEGMENTS, (pair + 1) * 2 * SEGMENTS)
                state_hold[here, :] = jnp.concatenate(states, axis=0).astype(BF16)
                kept[here, :] = jnp.concatenate(retains, axis=0)
                updates[here, :] = jnp.concatenate(ups, axis=0)
                slopes[here, :] = jnp.concatenate(slope, axis=0)

            total = jnp.zeros((SEGMENTS, tile), F32)
            for pair in range(pairs - 1, -1, -1):
                here = slice(pair * 2 * SEGMENTS, (pair + 1) * 2 * SEGMENTS)
                grads = slab_pair(back_ref, pair, span)
                retain, update, slope = kept[here, :], updates[here, :], slopes[here, :]
                late = grads[1] + leaving
                early = grads[0] + retain[SEGMENTS:] * late
                leaving = retain[:SEGMENTS] * early
                carried = jnp.concatenate([early, late], axis=0)
                gate_grad = carried * slope
                cand_grad = carried * update
                total = total + gate_grad[:SEGMENTS] + gate_grad[SEGMENTS:]
                one, other = choose(where_ref, gate_grad, cand_grad)
                one_hold[here, :] = one.astype(BF16)
                other_hold[here, :] = other.astype(BF16)
            bias_grad_ref[:, span] = jnp.sum(total, axis=0, keepdims=True)
            state_ref[:, span] = dot(order, state_hold[...]).astype(BF16)
            one_ref[span, :] = dot(order, one_hold[...]).T.astype(BF16)
            other_ref[span, :] = dot(order, other_hold[...]).T.astype(BF16)

        tiles(width, tile, body)

    wide = jax.ShapeDtypeStruct((rows, width), BF16)
    tall = jax.ShapeDtypeStruct((width, rows), BF16)
    flat = jax.ShapeDtypeStruct((1, width), F32)
    return pl.pallas_call(
        kernel,
        out_shape=[wide, tall, tall, flat, flat],
        in_specs=[SMEM_SPEC] + [VMEM_SPEC] * 6,
        out_specs=[VMEM_SPEC] * 5,
        scratch_shapes=[pltpu.VMEM((rows, tile), F32)] * 3 + [pltpu.VMEM((rows, tile), BF16)] * 3,
        compiler_params=params(14),
        cost_estimate=cost(6 * rows * rows * width, 12 * rows * width),
        name="scan_rows",
    )(where, first_pre, second_pre, back, both, parts, wholes)


def layer_call(where, state_rows, residual, shards, tile):
    rows, width = residual.shape
    count, depth = len(shards.groups), shards.depth

    def kernel(where_ref, x_ref, residual_ref, *refs):
        refs, (out_ref, ordered) = refs[:-2], refs[-2:]
        for index in range(count):
            source = pl.ds(pl.multiple_of((where_ref[0] ^ index) * depth, depth), depth)
            ordered[:, index * depth : (index + 1) * depth] = x_ref[:, source]

        def body(span):
            total = shards.product(ordered, 0, refs, span)
            out_ref[:, span] = (residual_ref[:, span].astype(F32) + total).astype(BF16)

        tiles(width, tile, body)

    return pl.pallas_call(
        kernel,
        out_shape=jax.ShapeDtypeStruct((rows, width), BF16),
        in_specs=[SMEM_SPEC] + [VMEM_SPEC] * 2 + [VMEM_SPEC] * len(shards.pieces),
        out_specs=VMEM_SPEC,
        scratch_shapes=[pltpu.VMEM((rows, count * depth), BF16)],
        compiler_params=params(14),
        cost_estimate=cost(2 * rows * count * depth * width, 2 * count * depth * width),
        name="layer_rows",
    )(where, state_rows, residual, *shards.operands())


def input_grad_call(where, one, other, first, second, x, grads, gain):
    rows, width = x.shape
    hidden = one.shape[0]
    count, depth = len(first.groups), first.depth

    def kernel(where_ref, one_ref, other_ref, x_ref, grads_ref, gain_ref, *refs):
        first_refs = refs[: len(first.pieces)]
        second_refs = refs[len(first.pieces) : len(first.pieces) + len(second.pieces)]
        out_ref, total = refs[-2:]
        size = min(depth, 256)
        for index in range(count):
            for part in range(0, depth, size):
                target = pl.multiple_of((where_ref[0] ^ index) * depth + part, size)
                term = dot(first.block(first_refs, index, part, size), one_ref[...])
                term = term + dot(second.block(second_refs, index, part, size), other_ref[...])
                total[:, pl.ds(target, size)] = term.T

        def body(span):
            x = x_ref[span, :].astype(F32)
            scale = lax.rsqrt(jnp.mean(x * x, axis=-1, keepdims=True) + EPSILON)
            unit = x * scale
            unit_grad = total[span, :] * gain_ref[...]
            along = jnp.mean(unit_grad * unit, axis=-1, keepdims=True)
            out = grads_ref[span, :].astype(F32) + scale * (unit_grad - unit * along)
            out_ref[span, :] = out.astype(BF16)

        tiles(rows, min(32, rows), body)

    return pl.pallas_call(
        kernel,
        out_shape=jax.ShapeDtypeStruct((rows, width), BF16),
        in_specs=[SMEM_SPEC] + [VMEM_SPEC] * 5 + [VMEM_SPEC] * (len(first.pieces) + len(second.pieces)),
        out_specs=VMEM_SPEC,
        scratch_shapes=[pltpu.VMEM((rows, width), F32)],
        compiler_params=params(14),
        cost_estimate=cost(4 * one.size * width, 4 * hidden * width),
        name="input_grad_rows",
    )(where, one, other, x, grads, gain, *first.operands(), *second.operands())


def close_call(where, state_grad, rows, block):
    def kernel(where_ref, state_ref, *refs):
        refs, (state_out_ref, bias_out_ref) = refs[:-2], refs[-2:]
        here = pl.ds(pl.multiple_of(where_ref[2] * block, block), block)
        state_out_ref[...] = state_ref[:, here]
        bias_out_ref[...] = sum((ref[:, here] for ref in refs[1:]), refs[0][:, here])

    return pl.pallas_call(
        kernel,
        out_shape=[jax.ShapeDtypeStruct((1, block), F32)] * 2,
        in_specs=[SMEM_SPEC] + [VMEM_SPEC] * (1 + len(rows)),
        out_specs=[VMEM_SPEC] * 2,
        compiler_params=params(2),
        cost_estimate=cost(1, 4 * state_grad.size),
        name="close_rows",
    )(where, state_grad, *rows)


def front_on_cube(ranks, batches, where, turned, tile, rows_in, grad_rows, gain, gate_bias, state_in, w_gate, w_cand, w_out):
    half = w_gate.shape[0] // 2
    depth = w_gate.shape[0]
    halves = lambda w: (w[:half], w[half:])
    straight = turned == 0
    send = lambda value, offset: hop(value, offset, ranks)
    core = lambda value: hop(value, 1, ranks)
    over = lambda value: swap_batch(value, 1, batches)
    f_a = jnp.where(straight, w_gate[:half], w_cand[:half])
    f_a, where, w_gate, w_cand, own_t = after((f_a, where, w_gate, w_cand, w_out))
    own_f = [f_a, jnp.where(straight, w_gate[half:], w_cand[half:])]
    f2a, f4a = send(own_f[0], 2), send(own_f[0], 4)
    f1 = [core(v) for v in own_f]
    both = jnp.stack([gate_bias, state_in[0]])
    both = jnp.concatenate([both, core(both)], axis=1)
    normed, grads = norm_call(where, rows_in, grad_rows, gain, depth)
    own_s = jnp.where(straight, w_cand, w_gate)
    t_a, t_b = halves(own_t)
    f2a, f4a, f1a, f1b, both, normed, grads, f_b, own_s, own_t, t_a, t_b = after(
        (f2a, f4a, f1[0], f1[1], both, normed, grads, own_f[1], own_s, own_t, t_a, t_b)
    )
    f1 = [f1a, f1b]
    f2b, f4b = send(f_b, 2), send(f_b, 4)
    t2a, t4a = send(t_a, 2), send(t_a, 4)
    sa = over(jnp.concatenate([f2a, f4a], axis=0))
    f2b, f4b, both, f3a, f5a, s1, t1 = after((f2b, f4b, both, f2a, f4a, own_s, own_t))
    came, f3a, f5a, s1, t1 = send(both, 2), core(f3a), core(f5a), core(s1), core(t1)
    both = jnp.concatenate([both, came], axis=1)
    both, f2b, f4b, sa, t2a, t4a, f3a, f5a, s1, t1, t_b, f2a = after(
        (both, f2b, f4b, sa, t2a, t4a, f3a, f5a, s1, t1, t_b, f2a)
    )
    f6a, f6b = send(f2a, 4), send(f4b, 2)
    t2b, t4b = send(t_b, 2), send(t_b, 4)
    sb = over(jnp.concatenate([f2b, f4b], axis=0))
    f6a, f6b, both, f3b, f5b, t3a, t5a, ca = after((f6a, f6b, both, f2b, f4b, t2a, t4a, sa))
    came, f3b, f5b, t3a, t5a, ca = send(both, 4), core(f3b), core(f5b), core(t3a), core(t5a), core(ca)
    f7a, f7b = core(f6a), core(f6b)
    both = jnp.concatenate([both, came], axis=1)
    both, f6a, f6b, f7a, f7b, sb, t2b, t4b, f3b, f5b, t3a, t5a, ca, t2a = after(
        (both, f6a, f6b, f7a, f7b, sb, t2b, t4b, f3b, f5b, t3a, t5a, ca, t2a)
    )
    t6a, t6b = send(t2a, 4), send(t4b, 2)
    s6 = over(jnp.concatenate([f6a, f6b], axis=0))
    first = Shards([own_f, f1, [f2a, f2b], [f3a, f3b], [f4a, f4b], [f5a, f5b], [f6a, f6b], [f7a, f7b]])
    first_pre = project_call(normed, first, tile, BF16)
    first_pre, t3b, t5b, cb = after((first_pre, t2b, t4b, sb))
    t3b, t5b, cb = core(t3b), core(t5b), core(cb)
    pairs = lambda one, two, row: [(one, row, half), (two, row, half)]
    most = [
        [own_s],
        [s1],
        pairs(sa, sb, 0),
        pairs(ca, cb, 0),
        pairs(sa, sb, half),
        pairs(ca, cb, half),
    ]
    partial = project_call(normed, Shards(most), tile, F32)
    t6a, t6b, t3b, t5b, partial = after((t6a, t6b, t3b, t5b, partial))
    t7a, t7b = core(t6a), core(t6b)
    third = Shards([[own_t], [t1], [t2a, t2b], [t3a, t3b], [t4a, t4b], [t5a, t5b], [t6a, t6b], [t7a, t7b]])
    back = back_call(where, grads, third)
    s6, back = after((s6, back))
    last = [[s6], [core(s6)]]
    second = Shards(most + last)
    second_pre, parts, whole, both = totals_call(
        where, normed, partial, Shards(last), len(most) * depth, first_pre, back, both, depth, tile
    )
    return where, first, second, third, first_pre, second_pre, back, both, parts, whole


def front(where, tile, rows_in, grad_rows, gain, gate_bias, state_in, w_gate, w_cand, w_out):
    first, second, third = (
        Shards([[lax.all_gather(w, "seq", tiled=True)]]) for w in (w_gate, w_cand, w_out)
    )
    both = lax.all_gather(jnp.stack([gate_bias, state_in[0]]), "seq", axis=1, tiled=True)
    normed, grads = norm_call(where, rows_in, grad_rows, gain, first.depth)
    first_pre = project_call(normed, first, tile, BF16)
    back = back_call(where, grads, third)
    second_pre, parts, whole, both = totals_call(
        where, normed, None, second, 0, first_pre, back, both, first.depth, tile
    )
    return where, first, second, third, first_pre, second_pre, back, both, parts, whole


def on_device(ranks, batches, inputs, output_grad, norm_gain, gate_bias, state_in, w_gate, w_cand, w_out):
    rows_in, grad_rows = inputs[0], output_grad[0]
    gain = norm_gain[None, :]
    hidden = w_gate.shape[1]
    tile = min(512, hidden)
    me = lax.axis_index("seq")
    given = (rows_in, grad_rows, gain, gate_bias, state_in, w_gate, w_cand, w_out)
    cube = ranks == 8 and batches in (2, 4, 8)
    if cube:
        turned = lax.axis_index("batch") % 2
        where = jnp.stack([me, turned, me]).astype(jnp.int32)
        found = front_on_cube(ranks, batches, where, turned, tile, *given)
    else:
        nought = jnp.zeros_like(me)
        where = jnp.stack([nought, nought, me]).astype(jnp.int32)
        found = front(where, tile, *given)
    where, first, second, third, first_pre, second_pre, back, both, parts, whole = found
    wholes = lax.all_gather(whole, "seq")
    state_rows, one, other, bias_part, state_grad = scan_call(
        where, first_pre, second_pre, back, both, parts, wholes, ranks, tile
    )
    width = hidden // ranks
    if cube:
        pair = bias_part + hop(bias_part, 1, ranks)
        layer_out = layer_call(where, state_rows, rows_in, third, tile)
        near = [hop(pair, offset, ranks) for offset in (2, 4, 6)]
        layer_out, pair, *near = after((layer_out, pair) + tuple(near))
        plane = pair + near[0] + near[1] + near[2]
        far = [swap_batch(plane, offset, batches) for offset in range(1, batches)]
        one, other, plane = after((one, other, plane), layer_out)
        input_grad = input_grad_call(where, one, other, first, second, rows_in, grad_rows, gain)
        state_out, bias_grad = close_call(where, state_grad, [plane] + far, width)
        bias_grad = bias_grad[0]
    else:
        over_seq = lax.psum_scatter(bias_part[0], "seq", scatter_dimension=0, tiled=True)
        bias_grad = lax.psum(over_seq, "batch")
        layer_out = layer_call(where, state_rows, rows_in, third, tile)
        input_grad = input_grad_call(where, one, other, first, second, rows_in, grad_rows, gain)
        state_out = lax.dynamic_slice_in_dim(state_grad, me * width, width, 1)
    return (layer_out[None], input_grad[None], state_out, bias_grad)


def solution(mesh):
    body = functools.partial(on_device, mesh.shape["seq"], mesh.shape["batch"])
    rows = P("batch", "seq", None)
    return jax.shard_map(
        body,
        mesh=mesh,
        in_specs=(rows, rows, P(), P("seq"), P("batch", "seq"), P("seq", None), P("seq", None), P("seq", None)),
        out_specs=(rows, rows, P("batch", "seq"), P("seq")),
        check_vma=False,
    )
```

```python
import functools

import jax
import jax.numpy as jnp
from jax import lax
from jax.experimental import pallas as pl
from jax.experimental.pallas import tpu as pltpu
from jax.sharding import PartitionSpec as P

EPSILON = 1e-06
SEGMENTS = 8
F32 = jnp.float32
BF16 = jnp.bfloat16


def params(mebibytes):
    return pltpu.CompilerParams(vmem_limit_bytes=mebibytes * 1024 * 1024)


def cost(flops, moved):
    return pl.CostEstimate(flops=int(flops), bytes_accessed=int(moved), transcendentals=0)


def hop(value, offset, count):
    return lax.ppermute(value, "seq", [(i, i ^ offset) for i in range(count)])


def swap_batch(value, offset, count):
    return lax.ppermute(value, "batch", [(i, i ^ offset) for i in range(count)])


def after(values, *earlier):
    return lax.optimization_barrier(tuple(values) + tuple(earlier))[: len(values)]


def place(rows):
    steps = rows // SEGMENTS
    out = lax.broadcasted_iota(jnp.int32, (rows, rows), 0)
    inn = lax.broadcasted_iota(jnp.int32, (rows, rows), 1)
    source = lax.rem(out, SEGMENTS) * steps + lax.div(out, SEGMENTS)
    return (source == inn).astype(F32).astype(BF16)


def place_back(rows):
    steps = rows // SEGMENTS
    out = lax.broadcasted_iota(jnp.int32, (rows, rows), 0)
    inn = lax.broadcasted_iota(jnp.int32, (rows, rows), 1)
    source = lax.rem(out, steps) * SEGMENTS + lax.div(out, steps)
    return (source == inn).astype(F32).astype(BF16)


def dot(a, b):
    return lax.dot_general(a, b, (((1,), (0,)), ((), ())), preferred_element_type=F32)


def tiles(count, tile, body):
    @pl.loop(0, count // tile)
    def _(index):
        body(pl.ds(pl.multiple_of(index * tile, tile), tile))


class Shards:
    def __init__(self, groups):
        self.pieces, self.groups = [], []
        for group in groups:
            made = []
            for piece in group:
                array, start, rows = piece if isinstance(piece, tuple) else (piece, 0, piece.shape[0])
                known = [index for index, other in enumerate(self.pieces) if other is array]
                if not known:
                    known = [len(self.pieces)]
                    self.pieces.append(array)
                made.append((known[0], start, rows))
            self.groups.append(made)
        self.depth = sum(rows for _, _, rows in self.groups[0])
        self.width = self.pieces[0].shape[1]

    def operands(self):
        return [pltpu.with_memory_space_constraint(piece, pltpu.VMEM) for piece in self.pieces]

    def block(self, refs, index, part, size):
        found, begin = [], 0
        for which, start, rows in self.groups[index]:
            low, high = max(part, begin), min(part + size, begin + rows)
            if low < high:
                found.append(refs[which][start + low - begin : start + high - begin, :])
            begin += rows
        return found[0] if len(found) == 1 else jnp.concatenate(found, axis=0)

    def product(self, x_ref, skip, refs, span):
        total = None
        joint = max(1, min(len(self.groups), 4))
        for index in range(0, len(self.groups), joint):
            groups = self.groups[index : index + joint]
            found = [refs[which][start : start + rows, span] for group in groups for which, start, rows in group]
            block = found[0] if len(found) == 1 else jnp.concatenate(found, axis=0)
            start = skip + index * self.depth
            term = dot(x_ref[:, start : start + len(groups) * self.depth], block)
            total = term if total is None else total + term
        return total


def near(value):
    return pltpu.with_memory_space_constraint(value, pltpu.VMEM)


VMEM_SPEC = pl.BlockSpec(memory_space=pltpu.VMEM)
SMEM_SPEC = pl.BlockSpec(memory_space=pltpu.SMEM)


def norm_call(where, x, g, gain, depth):
    rows, width = x.shape

    def kernel(where_ref, x_ref, g_ref, gain_ref, normed_ref, grads_ref, hold):
        def rows_body(span):
            x = x_ref[span, :].astype(F32)
            scale = lax.rsqrt(jnp.mean(x * x, axis=-1, keepdims=True) + EPSILON)
            hold[span, :] = (x * scale * gain_ref[...]).astype(BF16)

        tiles(rows, min(32, rows), rows_body)
        order = place(rows)
        for index in range(width // depth):
            source = pl.ds(pl.multiple_of((where_ref[0] ^ index) * depth, depth), depth)
            normed_ref[:, index * depth : (index + 1) * depth] = dot(order, hold[:, source]).astype(BF16)

        def grads_body(span):
            grads_ref[span, :] = dot(order, g_ref[:, span]).T.astype(BF16)

        tiles(width, min(512, width), grads_body)

    return pl.pallas_call(
        kernel,
        out_shape=[jax.ShapeDtypeStruct((rows, width), BF16), jax.ShapeDtypeStruct((width, rows), BF16)],
        in_specs=[SMEM_SPEC] + [VMEM_SPEC] * 3,
        out_specs=[VMEM_SPEC] * 2,
        scratch_shapes=[pltpu.VMEM(x.shape, BF16)],
        compiler_params=params(14),
        cost_estimate=cost(4 * rows * x.size, 8 * x.size),
        name="norm_rows",
    )(where, near(x), near(g), near(gain))


def project_call(x, shards, tile, dtype, skip=0):
    rows, width = x.shape[0], shards.width
    count, depth = len(shards.groups), shards.depth

    def kernel(x_ref, *refs):
        refs, out_ref = refs[:-1], refs[-1]

        def body(span):
            out_ref[:, span] = shards.product(x_ref, skip, refs, span).astype(dtype)

        tiles(width, tile, body)

    return pl.pallas_call(
        kernel,
        out_shape=jax.ShapeDtypeStruct((rows, width), dtype),
        in_specs=[VMEM_SPEC] + [VMEM_SPEC] * len(shards.pieces),
        out_specs=VMEM_SPEC,
        compiler_params=params(14),
        cost_estimate=cost(2 * rows * count * depth * width, 2 * count * depth * width),
        name="project",
    )(near(x), *shards.operands())


def back_call(where, grads, shards):
    width, rows = grads.shape
    count, depth = len(shards.groups), shards.depth

    def kernel(where_ref, g_ref, *refs):
        refs, out_ref = refs[:-1], refs[-1]
        size = min(depth, 256)
        for index in range(count):
            for part in range(0, depth, size):
                target = pl.multiple_of((where_ref[0] ^ index) * depth + part, size)
                term = dot(shards.block(refs, index, part, size), g_ref[...])
                out_ref[:, pl.ds(target, size)] = term.T.astype(BF16)

    return pl.pallas_call(
        kernel,
        out_shape=jax.ShapeDtypeStruct((rows, count * depth), BF16),
        in_specs=[SMEM_SPEC, VMEM_SPEC] + [VMEM_SPEC] * len(shards.pieces),
        out_specs=VMEM_SPEC,
        compiler_params=params(14),
        cost_estimate=cost(2 * rows * count * depth * width, 2 * count * depth * width),
        name="back_rows",
    )(where, near(grads), *shards.operands())


def gates(x):
    small = jnp.exp(-jnp.abs(x))
    large = 1.0 / (1.0 + small)
    small = small * large
    up = x >= 0
    return jnp.where(up, large, small), jnp.where(up, small, large)


def slab_pair(ref, pair, span):
    both = ref[pair * 2 * SEGMENTS : (pair + 1) * 2 * SEGMENTS, span].astype(F32)
    return both[:SEGMENTS], both[SEGMENTS:]


def choose(where_ref, one, other):
    straight = where_ref[1] == 0
    return jnp.where(straight, one, other), jnp.where(straight, other, one)


def totals_call(where, x, partial, shards, skip, first_pre, back, both, block, tile):
    rows, width = first_pre.shape
    pairs = rows // (2 * SEGMENTS)
    count, depth = len(shards.groups), shards.depth
    extra = [] if partial is None else [partial]

    def kernel(where_ref, x_ref, first_ref, back_ref, both_ref, *refs):
        partial_refs, refs = refs[: len(extra)], refs[len(extra) :]
        refs, (second_ref, parts_ref, whole_ref, rows_ref) = refs[:-4], refs[-4:]
        for index in range(width // block):
            target = pl.multiple_of((where_ref[0] ^ index) * block, block)
            rows_ref[:, pl.ds(target, block)] = both_ref[:, index * block : (index + 1) * block]

        def body(span):
            total = shards.product(x_ref, skip, refs, span)
            for ref in partial_refs:
                total = total + ref[:, span]
            second_ref[:, span] = total.astype(BF16)
            bias = rows_ref[0:1, span]
            keep = jnp.ones((SEGMENTS, tile), F32)
            state = leaving = jnp.zeros((SEGMENTS, tile), F32)
            for pair in range(pairs):
                slabs = [slab_pair(ref, pair, span) for ref in (first_ref, second_ref, back_ref)]
                for a, b, g in zip(*slabs):
                    gate, cand = choose(where_ref, a, b)
                    update, retain = gates(gate + bias)
                    keep = keep * retain
                    state = retain * state + update * cand
                    leaving = leaving + keep * g
            parts_ref[0, :, span], parts_ref[1, :, span], parts_ref[2, :, span] = keep, state, leaving
            whole_keep, whole_state = keep[0:1], state[0:1]
            for s in range(1, SEGMENTS):
                whole_state = keep[s : s + 1] * whole_state + state[s : s + 1]
                whole_keep = whole_keep * keep[s : s + 1]
            whole_leaving = leaving[SEGMENTS - 1 :]
            for s in range(SEGMENTS - 2, -1, -1):
                whole_leaving = keep[s : s + 1] * whole_leaving + leaving[s : s + 1]
            whole_ref[0:1, span], whole_ref[1:2, span], whole_ref[2:3, span] = whole_keep, whole_state, whole_leaving

        tiles(width, tile, body)

    return pl.pallas_call(
        kernel,
        out_shape=[
            jax.ShapeDtypeStruct((rows, width), BF16),
            jax.ShapeDtypeStruct((3, SEGMENTS, width), F32),
            jax.ShapeDtypeStruct((3, width), F32),
            jax.ShapeDtypeStruct((2, width), F32),
        ],
        in_specs=[SMEM_SPEC] + [VMEM_SPEC] * (4 + len(extra)) + [VMEM_SPEC] * len(shards.pieces),
        out_specs=[VMEM_SPEC] * 4,
        compiler_params=params(14),
        cost_estimate=cost(2 * rows * count * depth * width, 2 * count * depth * width),
        name="project_totals",
    )(where, *map(near, (x, first_pre, back, both, *extra)), *shards.operands())


def scan_call(where, first_pre, second_pre, back, both, parts, wholes, ranks, tile):
    rows, width = first_pre.shape
    pairs = rows // (2 * SEGMENTS)

    def kernel(where_ref, first_ref, second_ref, back_ref, both_ref, parts_ref, wholes_ref, *refs):
        (state_ref, one_ref, other_ref, bias_grad_ref, state_grad_ref) = refs[:5]
        kept, updates, slopes, one_hold, other_hold, state_hold = refs[5:]
        me = where_ref[2]
        order = place_back(rows)

        def body(span):
            entering = both_ref[1:2, span]
            blocks = [wholes_ref[rank, :, span] for rank in range(ranks)]
            for rank in range(ranks):
                block = blocks[rank]
                entering = jnp.where(rank < me, block[0:1] * entering + block[1:2], entering)
            arriving = state_grad = blocks[0][2:3] * 0.0
            for rank in range(ranks - 1, -1, -1):
                block = blocks[rank]
                arriving = jnp.where(rank == me, state_grad, arriving)
                state_grad = block[0:1] * state_grad + block[2:3]
            state_grad_ref[:, span] = state_grad
            keep, ends, leaves = parts_ref[0, :, span], parts_ref[1, :, span], parts_ref[2, :, span]
            starts = [entering]
            for s in range(SEGMENTS - 1):
                starts.append(keep[s : s + 1] * starts[-1] + ends[s : s + 1])
            tails = [arriving]
            for s in range(SEGMENTS - 1, 0, -1):
                tails.append(keep[s : s + 1] * tails[-1] + leaves[s : s + 1])
            state = jnp.concatenate(starts, axis=0)
            leaving = jnp.concatenate(tails[::-1], axis=0)
            bias = both_ref[0:1, span]

            for pair in range(pairs):
                states, retains, ups, slope = [], [], [], []
                for a, b in zip(slab_pair(first_ref, pair, span), slab_pair(second_ref, pair, span)):
                    gate, cand = choose(where_ref, a, b)
                    update, retain = gates(gate + bias)
                    retains.append(retain)
                    ups.append(update)
                    slope.append((cand - state) * update * retain)
                    state = retain * state + update * cand
                    states.append(state)
                here = slice(pair * 2 * SEGMENTS, (pair + 1) * 2 * SEGMENTS)
                state_hold[here, :] = jnp.concatenate(states, axis=0).astype(BF16)
                kept[here, :] = jnp.concatenate(retains, axis=0)
                updates[here, :] = jnp.concatenate(ups, axis=0)
                slopes[here, :] = jnp.concatenate(slope, axis=0)

            total = jnp.zeros((SEGMENTS, tile), F32)
            for pair in range(pairs - 1, -1, -1):
                here = slice(pair * 2 * SEGMENTS, (pair + 1) * 2 * SEGMENTS)
                grads = slab_pair(back_ref, pair, span)
                retain, update, slope = kept[here, :], updates[here, :], slopes[here, :]
                late = grads[1] + leaving
                early = grads[0] + retain[SEGMENTS:] * late
                leaving = retain[:SEGMENTS] * early
                carried = jnp.concatenate([early, late], axis=0)
                gate_grad = carried * slope
                cand_grad = carried * update
                total = total + gate_grad[:SEGMENTS] + gate_grad[SEGMENTS:]
                one, other = choose(where_ref, gate_grad, cand_grad)
                one_hold[here, :] = one.astype(BF16)
                other_hold[here, :] = other.astype(BF16)
            bias_grad_ref[:, span] = jnp.sum(total, axis=0, keepdims=True)
            state_ref[:, span] = dot(order, state_hold[...]).astype(BF16)
            one_ref[span, :] = dot(order, one_hold[...]).T.astype(BF16)
            other_ref[span, :] = dot(order, other_hold[...]).T.astype(BF16)

        tiles(width, tile, body)

    wide = jax.ShapeDtypeStruct((rows, width), BF16)
    tall = jax.ShapeDtypeStruct((width, rows), BF16)
    flat = jax.ShapeDtypeStruct((1, width), F32)
    return pl.pallas_call(
        kernel,
        out_shape=[wide, tall, tall, flat, flat],
        in_specs=[SMEM_SPEC] + [VMEM_SPEC] * 6,
        out_specs=[VMEM_SPEC] * 5,
        scratch_shapes=[pltpu.VMEM((rows, tile), F32)] * 3 + [pltpu.VMEM((rows, tile), BF16)] * 3,
        compiler_params=params(14),
        cost_estimate=cost(6 * rows * rows * width, 12 * rows * width),
        name="scan_rows",
    )(where, *map(near, (first_pre, second_pre, back, both, parts, wholes)))


def layer_call(where, state_rows, residual, shards, tile):
    rows, width = residual.shape
    count, depth = len(shards.groups), shards.depth

    def kernel(where_ref, x_ref, residual_ref, *refs):
        refs, (out_ref, ordered) = refs[:-2], refs[-2:]
        for index in range(count):
            source = pl.ds(pl.multiple_of((where_ref[0] ^ index) * depth, depth), depth)
            ordered[:, index * depth : (index + 1) * depth] = x_ref[:, source]

        def body(span):
            total = shards.product(ordered, 0, refs, span)
            out_ref[:, span] = (residual_ref[:, span].astype(F32) + total).astype(BF16)

        tiles(width, tile, body)

    return pl.pallas_call(
        kernel,
        out_shape=jax.ShapeDtypeStruct((rows, width), BF16),
        in_specs=[SMEM_SPEC] + [VMEM_SPEC] * 2 + [VMEM_SPEC] * len(shards.pieces),
        out_specs=VMEM_SPEC,
        scratch_shapes=[pltpu.VMEM((rows, count * depth), BF16)],
        compiler_params=params(14),
        cost_estimate=cost(2 * rows * count * depth * width, 2 * count * depth * width),
        name="layer_rows",
    )(where, near(state_rows), near(residual), *shards.operands())


def input_grad_call(where, one, other, first, second, x, grads, gain):
    rows, width = x.shape
    hidden = one.shape[0]
    count, depth = len(first.groups), first.depth

    def kernel(where_ref, one_ref, other_ref, x_ref, grads_ref, gain_ref, *refs):
        first_refs = refs[: len(first.pieces)]
        second_refs = refs[len(first.pieces) : len(first.pieces) + len(second.pieces)]
        out_ref, total = refs[-2:]
        size = min(depth, 256)
        for index in range(count):
            for part in range(0, depth, size):
                target = pl.multiple_of((where_ref[0] ^ index) * depth + part, size)
                term = dot(first.block(first_refs, index, part, size), one_ref[...])
                term = term + dot(second.block(second_refs, index, part, size), other_ref[...])
                total[:, pl.ds(target, size)] = term.T

        def body(span):
            x = x_ref[span, :].astype(F32)
            scale = lax.rsqrt(jnp.mean(x * x, axis=-1, keepdims=True) + EPSILON)
            unit = x * scale
            unit_grad = total[span, :] * gain_ref[...]
            along = jnp.mean(unit_grad * unit, axis=-1, keepdims=True)
            out = grads_ref[span, :].astype(F32) + scale * (unit_grad - unit * along)
            out_ref[span, :] = out.astype(BF16)

        tiles(rows, min(32, rows), body)

    return pl.pallas_call(
        kernel,
        out_shape=jax.ShapeDtypeStruct((rows, width), BF16),
        in_specs=[SMEM_SPEC] + [VMEM_SPEC] * 5 + [VMEM_SPEC] * (len(first.pieces) + len(second.pieces)),
        out_specs=VMEM_SPEC,
        scratch_shapes=[pltpu.VMEM((rows, width), F32)],
        compiler_params=params(14),
        cost_estimate=cost(4 * one.size * width, 4 * hidden * width),
        name="input_grad_rows",
    )(where, *map(near, (one, other, x, grads, gain)), *first.operands(), *second.operands())


def close_call(where, state_grad, rows, block):
    def kernel(where_ref, state_ref, *refs):
        refs, (state_out_ref, bias_out_ref) = refs[:-2], refs[-2:]
        here = pl.ds(pl.multiple_of(where_ref[2] * block, block), block)
        state_out_ref[...] = state_ref[:, here]
        bias_out_ref[...] = sum((ref[:, here] for ref in refs[1:]), refs[0][:, here])

    return pl.pallas_call(
        kernel,
        out_shape=[jax.ShapeDtypeStruct((1, block), F32)] * 2,
        in_specs=[SMEM_SPEC] + [VMEM_SPEC] * (1 + len(rows)),
        out_specs=[VMEM_SPEC] * 2,
        compiler_params=params(2),
        cost_estimate=cost(1, 4 * state_grad.size),
        name="close_rows",
    )(where, state_grad, *rows)


def front_on_cube(ranks, batches, where, turned, tile, rows_in, grad_rows, gain, gate_bias, state_in, w_gate, w_cand, w_out):
    half = w_gate.shape[0] // 2
    depth = w_gate.shape[0]
    halves = lambda w: (w[:half], w[half:])
    straight = turned == 0
    send = lambda value, offset: hop(value, offset, ranks)
    core = lambda value: hop(value, 1, ranks)
    over = lambda value: swap_batch(value, 1, batches)
    f_a = jnp.where(straight, w_gate[:half], w_cand[:half])
    f_a, where, w_gate, w_cand, own_t = after((f_a, where, w_gate, w_cand, w_out))
    own_f = [f_a, jnp.where(straight, w_gate[half:], w_cand[half:])]
    stack = lambda *parts: jnp.concatenate(parts, axis=0)
    cut = lambda held, *starts: [(held, start * half, half) for start in starts]
    f2a, f4a = send(own_f[0], 2), send(own_f[0], 4)
    f1 = [core(v) for v in own_f]
    both = jnp.stack([gate_bias, state_in[0]])
    both = jnp.concatenate([both, core(both)], axis=1)
    both = jnp.concatenate([both, send(both, 2)], axis=1)
    normed, grads = norm_call(where, rows_in, grad_rows, gain, depth)
    own_s = jnp.where(straight, w_cand, w_gate)
    t_a, t_b = halves(own_t)
    f2a, f4a, f1a, f1b, both, normed, grads, f_b, own_s, own_t, t_a, t_b = after(
        (f2a, f4a, f1[0], f1[1], both, normed, grads, own_f[1], own_s, own_t, t_a, t_b)
    )
    f2b, f4b = send(f_b, 2), send(f_b, 4)
    t2a, t4a = send(t_a, 2), send(t_a, 4)
    sa = over(stack(f2a, f4a))
    f2b, f4b, f3a, f5a, s1 = after((f2b, f4b, f2a, f4a, own_s))
    f3a, f5a, s1 = core(f3a), core(f5a), core(s1)
    f2b, f4b, sa, t2a, t4a, f3a, f5a, s1, t_b, f2a = after((f2b, f4b, sa, t2a, t4a, f3a, f5a, s1, t_b, f2a))
    f6a, f6b = send(f2a, 4), send(f4b, 2)
    t2b, t4b = send(t_b, 2), send(t_b, 4)
    sb = over(stack(f2b, f4b))
    f6a, f6b, f3b, f5b, t3a, t5a, ca = after((f6a, f6b, f2b, f4b, t2a, t4a, sa))
    f3b, f5b, t3a, t5a, ca = core(f3b), core(f5b), core(t3a), core(t5a), core(ca)
    both, f6a, f6b, sb, t2b, t4b, f3b, f5b, t3a, t5a, ca, t2a = after(
        (both, f6a, f6b, sb, t2b, t4b, f3b, f5b, t3a, t5a, ca, t2a)
    )
    t6a, t6b = send(t2a, 4), send(t4b, 2)
    s6a = over(f6a)
    f7, cb = core(stack(f6a, f6b)), core(sb)
    first = Shards([own_f, [f1a, f1b], [f2a, f2b], [f3a, f3b], [f4a, f4b], [f5a, f5b], [f6a, f6b], [f7]])
    pairs = lambda one, two, row: cut(one, row) + cut(two, row)
    most = [[own_s], [s1], pairs(sa, sb, 0), pairs(ca, cb, 0), pairs(sa, sb, 1), pairs(ca, cb, 1)]
    first_pre = project_call(normed, first, tile, BF16)
    partial = project_call(normed, Shards(most), tile, F32)
    t6a, t6b, s6a, f6b, first_pre, partial, own_t, both = after(
        (t6a, t6b, s6a, f6b, first_pre, partial, own_t, both)
    )
    s6b, s7a = over(f6b), core(s6a)
    c4 = core(stack(t6a, t6b, t2b, t4b, own_t))
    third = Shards(
        [[own_t], cut(c4, 4, 5), [t2a, t2b], [t3a, (c4, 2 * half, half)], [t4a, t4b], [t5a, (c4, 3 * half, half)]]
        + [[t6a, t6b], cut(c4, 0, 1)]
    )
    both = jnp.concatenate([both, send(both, 4)], axis=1)
    back = back_call(where, grads, third)
    s6b, s7a, back, both = after((s6b, s7a, back, both))
    last = [[s6a, s6b], [s7a, core(s6b)]]
    second = Shards(most + last)
    second_pre, parts, whole, both = totals_call(
        where, normed, partial, Shards(last), len(most) * depth, first_pre, back, both, depth, tile
    )
    return where, first, second, third, first_pre, second_pre, back, both, parts, whole


def front(where, tile, rows_in, grad_rows, gain, gate_bias, state_in, w_gate, w_cand, w_out):
    first, second, third = (
        Shards([[lax.all_gather(w, "seq", tiled=True)]]) for w in (w_gate, w_cand, w_out)
    )
    both = lax.all_gather(jnp.stack([gate_bias, state_in[0]]), "seq", axis=1, tiled=True)
    normed, grads = norm_call(where, rows_in, grad_rows, gain, first.depth)
    first_pre = project_call(normed, first, tile, BF16)
    back = back_call(where, grads, third)
    second_pre, parts, whole, both = totals_call(
        where, normed, None, second, 0, first_pre, back, both, first.depth, tile
    )
    return where, first, second, third, first_pre, second_pre, back, both, parts, whole


def on_device(ranks, batches, inputs, output_grad, norm_gain, gate_bias, state_in, w_gate, w_cand, w_out):
    rows_in, grad_rows = inputs[0], output_grad[0]
    gain = norm_gain[None, :]
    hidden = w_gate.shape[1]
    tile = min(512, hidden)
    me = lax.axis_index("seq")
    given = (rows_in, grad_rows, gain, gate_bias, state_in, w_gate, w_cand, w_out)
    cube = ranks == 8 and batches in (2, 4, 8)
    if cube:
        turned = lax.axis_index("batch") % 2
        where = jnp.stack([me, turned, me]).astype(jnp.int32)
        found = front_on_cube(ranks, batches, where, turned, tile, *given)
    else:
        nought = jnp.zeros_like(me)
        where = jnp.stack([nought, nought, me]).astype(jnp.int32)
        found = front(where, tile, *given)
    where, first, second, third, first_pre, second_pre, back, both, parts, whole = found
    wholes = lax.all_gather(whole, "seq")
    state_rows, one, other, bias_part, state_grad = scan_call(
        where, first_pre, second_pre, back, both, parts, wholes, ranks, tile
    )
    width = hidden // ranks
    if cube:
        pair = bias_part + hop(bias_part, 1, ranks)
        layer_out = layer_call(where, state_rows, rows_in, third, tile)
        plane = [hop(pair, offset, ranks) for offset in (2, 4, 6)]
        layer_out, pair, *plane = after((layer_out, pair) + tuple(plane))
        plane = pair + plane[0] + plane[1] + plane[2]
        far = [swap_batch(plane, offset, batches) for offset in range(1, batches)]
        one, other, plane = after((one, other, plane), layer_out)
        input_grad = input_grad_call(where, one, other, first, second, rows_in, grad_rows, gain)
        state_out, bias_grad = close_call(where, state_grad, [plane] + far, width)
        bias_grad = bias_grad[0]
    else:
        over_seq = lax.psum_scatter(bias_part[0], "seq", scatter_dimension=0, tiled=True)
        bias_grad = lax.psum(over_seq, "batch")
        layer_out = layer_call(where, state_rows, rows_in, third, tile)
        input_grad = input_grad_call(where, one, other, first, second, rows_in, grad_rows, gain)
        state_out = lax.dynamic_slice_in_dim(state_grad, me * width, width, 1)
    return (layer_out[None], input_grad[None], state_out, bias_grad)


def solution(mesh):
    body = functools.partial(on_device, mesh.shape["seq"], mesh.shape["batch"])
    rows = P("batch", "seq", None)
    return jax.shard_map(
        body,
        mesh=mesh,
        in_specs=(rows, rows, P(), P("seq"), P("batch", "seq"), P("seq", None), P("seq", None), P("seq", None)),
        out_specs=(rows, rows, P("batch", "seq"), P("seq")),
        check_vma=False,
    )
```

```python
import functools

import jax
import jax.numpy as jnp
from jax import lax
from jax.experimental import pallas as pl
from jax.experimental.pallas import tpu as pltpu
from jax.sharding import PartitionSpec as P

EPSILON = 1e-06
SEGMENTS = 8
F32 = jnp.float32
BF16 = jnp.bfloat16


def params(mebibytes):
    return pltpu.CompilerParams(vmem_limit_bytes=mebibytes * 1024 * 1024)


def cost(flops, moved):
    return pl.CostEstimate(flops=int(flops), bytes_accessed=int(moved), transcendentals=0)


def hop(value, offset, count):
    return lax.ppermute(value, "seq", [(i, i ^ offset) for i in range(count)])


def swap_batch(value, offset, count):
    return lax.ppermute(value, "batch", [(i, i ^ offset) for i in range(count)])


def after(values, *earlier):
    return lax.optimization_barrier(tuple(values) + tuple(earlier))[: len(values)]


def place(rows):
    steps = rows // SEGMENTS
    out = lax.broadcasted_iota(jnp.int32, (rows, rows), 0)
    inn = lax.broadcasted_iota(jnp.int32, (rows, rows), 1)
    source = lax.rem(out, SEGMENTS) * steps + lax.div(out, SEGMENTS)
    return (source == inn).astype(F32).astype(BF16)


def place_back(rows):
    steps = rows // SEGMENTS
    out = lax.broadcasted_iota(jnp.int32, (rows, rows), 0)
    inn = lax.broadcasted_iota(jnp.int32, (rows, rows), 1)
    source = lax.rem(out, steps) * SEGMENTS + lax.div(out, steps)
    return (source == inn).astype(F32).astype(BF16)


def dot(a, b):
    return lax.dot_general(a, b, (((1,), (0,)), ((), ())), preferred_element_type=F32)


def tiles(count, tile, body):
    @pl.loop(0, count // tile)
    def _(index):
        body(pl.ds(pl.multiple_of(index * tile, tile), tile))


class Shards:
    def __init__(self, groups):
        self.pieces, self.groups = [], []
        for group in groups:
            made = []
            for piece in group:
                array, start, rows = piece if isinstance(piece, tuple) else (piece, 0, piece.shape[0])
                known = [index for index, other in enumerate(self.pieces) if other is array]
                if not known:
                    known = [len(self.pieces)]
                    self.pieces.append(array)
                made.append((known[0], start, rows))
            self.groups.append(made)
        self.depth = sum(rows for _, _, rows in self.groups[0])
        self.width = self.pieces[0].shape[1]

    def operands(self):
        return [pltpu.with_memory_space_constraint(piece, pltpu.VMEM) for piece in self.pieces]

    def block(self, refs, index, part, size):
        found, begin = [], 0
        for which, start, rows in self.groups[index]:
            low, high = max(part, begin), min(part + size, begin + rows)
            if low < high:
                found.append(refs[which][start + low - begin : start + high - begin, :])
            begin += rows
        return found[0] if len(found) == 1 else jnp.concatenate(found, axis=0)

    def product(self, x_ref, skip, refs, span):
        total = None
        joint = max(1, min(len(self.groups), 4))
        for index in range(0, len(self.groups), joint):
            groups = self.groups[index : index + joint]
            found = [refs[which][start : start + rows, span] for group in groups for which, start, rows in group]
            block = found[0] if len(found) == 1 else jnp.concatenate(found, axis=0)
            start = skip + index * self.depth
            term = dot(x_ref[:, start : start + len(groups) * self.depth], block)
            total = term if total is None else total + term
        return total


def near(value):
    return pltpu.with_memory_space_constraint(value, pltpu.VMEM)


VMEM_SPEC = pl.BlockSpec(memory_space=pltpu.VMEM)
SMEM_SPEC = pl.BlockSpec(memory_space=pltpu.SMEM)


def norm_call(where, x, g, gain, depth):
    rows, width = x.shape

    def kernel(where_ref, x_ref, g_ref, gain_ref, normed_ref, grads_ref, hold):
        def rows_body(span):
            x = x_ref[span, :].astype(F32)
            scale = lax.rsqrt(jnp.mean(x * x, axis=-1, keepdims=True) + EPSILON)
            hold[span, :] = (x * scale * gain_ref[...]).astype(BF16)

        tiles(rows, min(32, rows), rows_body)
        order = place(rows)
        for index in range(width // depth):
            source = pl.ds(pl.multiple_of((where_ref[0] ^ index) * depth, depth), depth)
            normed_ref[:, index * depth : (index + 1) * depth] = dot(order, hold[:, source]).astype(BF16)

        def grads_body(span):
            grads_ref[span, :] = dot(order, g_ref[:, span]).T.astype(BF16)

        tiles(width, min(512, width), grads_body)

    return pl.pallas_call(
        kernel,
        out_shape=[jax.ShapeDtypeStruct((rows, width), BF16), jax.ShapeDtypeStruct((width, rows), BF16)],
        in_specs=[SMEM_SPEC] + [VMEM_SPEC] * 3,
        out_specs=[VMEM_SPEC] * 2,
        scratch_shapes=[pltpu.VMEM(x.shape, BF16)],
        compiler_params=params(14),
        cost_estimate=cost(4 * rows * x.size, 8 * x.size),
        name="norm_rows",
    )(where, near(x), near(g), near(gain))


def project_call(x, shards, tile, dtype, skip=0):
    rows, width = x.shape[0], shards.width
    count, depth = len(shards.groups), shards.depth

    def kernel(x_ref, *refs):
        refs, out_ref = refs[:-1], refs[-1]

        def body(span):
            out_ref[:, span] = shards.product(x_ref, skip, refs, span).astype(dtype)

        tiles(width, tile, body)

    return pl.pallas_call(
        kernel,
        out_shape=jax.ShapeDtypeStruct((rows, width), dtype),
        in_specs=[VMEM_SPEC] + [VMEM_SPEC] * len(shards.pieces),
        out_specs=VMEM_SPEC,
        compiler_params=params(14),
        cost_estimate=cost(2 * rows * count * depth * width, 2 * count * depth * width),
        name="project",
    )(near(x), *shards.operands())


def back_call(where, grads, shards):
    width, rows = grads.shape
    count, depth = len(shards.groups), shards.depth

    def kernel(where_ref, g_ref, *refs):
        refs, out_ref = refs[:-1], refs[-1]
        size = min(depth, 256)
        for index in range(count):
            for part in range(0, depth, size):
                target = pl.multiple_of((where_ref[0] ^ index) * depth + part, size)
                term = dot(shards.block(refs, index, part, size), g_ref[...])
                out_ref[:, pl.ds(target, size)] = term.T.astype(BF16)

    return pl.pallas_call(
        kernel,
        out_shape=jax.ShapeDtypeStruct((rows, count * depth), BF16),
        in_specs=[SMEM_SPEC, VMEM_SPEC] + [VMEM_SPEC] * len(shards.pieces),
        out_specs=VMEM_SPEC,
        compiler_params=params(14),
        cost_estimate=cost(2 * rows * count * depth * width, 2 * count * depth * width),
        name="back_rows",
    )(where, near(grads), *shards.operands())


def gates(x):
    small = jnp.exp(-jnp.abs(x))
    large = 1.0 / (1.0 + small)
    small = small * large
    up = x >= 0
    return jnp.where(up, large, small), jnp.where(up, small, large)


def slab_pair(ref, pair, span):
    both = ref[pair * 2 * SEGMENTS : (pair + 1) * 2 * SEGMENTS, span].astype(F32)
    return both[:SEGMENTS], both[SEGMENTS:]


def choose(where_ref, one, other):
    straight = where_ref[1] == 0
    return jnp.where(straight, one, other), jnp.where(straight, other, one)


def totals_call(where, x, partial, shards, skip, first_pre, back, both, block, tile):
    rows, width = first_pre.shape
    pairs = rows // (2 * SEGMENTS)
    count, depth = len(shards.groups), shards.depth
    extra = [] if partial is None else [partial]

    def kernel(where_ref, x_ref, first_ref, back_ref, both_ref, *refs):
        partial_refs, refs = refs[: len(extra)], refs[len(extra) :]
        refs, (second_ref, parts_ref, whole_ref, rows_ref) = refs[:-4], refs[-4:]
        for index in range(width // block):
            target = pl.multiple_of((where_ref[0] ^ index) * block, block)
            rows_ref[:, pl.ds(target, block)] = both_ref[:, index * block : (index + 1) * block]

        def body(span):
            total = shards.product(x_ref, skip, refs, span)
            for ref in partial_refs:
                total = total + ref[:, span]
            second_ref[:, span] = total.astype(BF16)
            bias = rows_ref[0:1, span]
            keep = jnp.ones((SEGMENTS, tile), F32)
            state = leaving = jnp.zeros((SEGMENTS, tile), F32)
            for pair in range(pairs):
                slabs = [slab_pair(ref, pair, span) for ref in (first_ref, second_ref, back_ref)]
                for a, b, g in zip(*slabs):
                    gate, cand = choose(where_ref, a, b)
                    update, retain = gates(gate + bias)
                    keep = keep * retain
                    state = retain * state + update * cand
                    leaving = leaving + keep * g
            parts_ref[0, :, span], parts_ref[1, :, span], parts_ref[2, :, span] = keep, state, leaving
            whole_keep, whole_state = keep[0:1], state[0:1]
            for s in range(1, SEGMENTS):
                whole_state = keep[s : s + 1] * whole_state + state[s : s + 1]
                whole_keep = whole_keep * keep[s : s + 1]
            whole_leaving = leaving[SEGMENTS - 1 :]
            for s in range(SEGMENTS - 2, -1, -1):
                whole_leaving = keep[s : s + 1] * whole_leaving + leaving[s : s + 1]
            whole_ref[0:1, span], whole_ref[1:2, span], whole_ref[2:3, span] = whole_keep, whole_state, whole_leaving

        tiles(width, tile, body)

    return pl.pallas_call(
        kernel,
        out_shape=[
            jax.ShapeDtypeStruct((rows, width), BF16),
            jax.ShapeDtypeStruct((3, SEGMENTS, width), F32),
            jax.ShapeDtypeStruct((3, width), F32),
            jax.ShapeDtypeStruct((2, width), F32),
        ],
        in_specs=[SMEM_SPEC] + [VMEM_SPEC] * (4 + len(extra)) + [VMEM_SPEC] * len(shards.pieces),
        out_specs=[VMEM_SPEC] * 4,
        compiler_params=params(14),
        cost_estimate=cost(2 * rows * count * depth * width, 2 * count * depth * width),
        name="project_totals",
    )(where, *map(near, (x, first_pre, back, both, *extra)), *shards.operands())


def scan_call(where, first_pre, second_pre, back, both, parts, wholes, ranks, tile):
    rows, width = first_pre.shape
    pairs = rows // (2 * SEGMENTS)

    def kernel(where_ref, first_ref, second_ref, back_ref, both_ref, parts_ref, *refs):
        whole_refs, refs = refs[: len(wholes)], refs[len(wholes) :]
        (state_ref, one_ref, other_ref, bias_grad_ref, state_grad_ref) = refs[:5]
        hold, kept, updates, slopes, one_hold, other_hold, state_hold = refs[5:]
        me = where_ref[2]
        order = place_back(rows)

        def body(span):
            entering = both_ref[1:2, span]
            per = ranks // len(wholes)
            for index, ref in enumerate(whole_refs):
                for member in range(per):
                    offset = index * per + member
                    hold[me ^ offset if len(wholes) > 1 else offset, 0:3, :] = ref[member, :, span]
            blocks = [hold[rank] for rank in range(ranks)]
            for rank in range(ranks):
                block = blocks[rank]
                entering = jnp.where(rank < me, block[0:1] * entering + block[1:2], entering)
            arriving = state_grad = blocks[0][2:3] * 0.0
            for rank in range(ranks - 1, -1, -1):
                block = blocks[rank]
                arriving = jnp.where(rank == me, state_grad, arriving)
                state_grad = block[0:1] * state_grad + block[2:3]
            state_grad_ref[:, span] = state_grad
            keep, ends, leaves = parts_ref[0, :, span], parts_ref[1, :, span], parts_ref[2, :, span]
            starts = [entering]
            for s in range(SEGMENTS - 1):
                starts.append(keep[s : s + 1] * starts[-1] + ends[s : s + 1])
            tails = [arriving]
            for s in range(SEGMENTS - 1, 0, -1):
                tails.append(keep[s : s + 1] * tails[-1] + leaves[s : s + 1])
            state = jnp.concatenate(starts, axis=0)
            leaving = jnp.concatenate(tails[::-1], axis=0)
            bias = both_ref[0:1, span]

            for pair in range(pairs):
                states, retains, ups, slope = [], [], [], []
                for a, b in zip(slab_pair(first_ref, pair, span), slab_pair(second_ref, pair, span)):
                    gate, cand = choose(where_ref, a, b)
                    update, retain = gates(gate + bias)
                    retains.append(retain)
                    ups.append(update)
                    slope.append((cand - state) * update * retain)
                    state = retain * state + update * cand
                    states.append(state)
                here = slice(pair * 2 * SEGMENTS, (pair + 1) * 2 * SEGMENTS)
                state_hold[here, :] = jnp.concatenate(states, axis=0).astype(BF16)
                kept[here, :] = jnp.concatenate(retains, axis=0)
                updates[here, :] = jnp.concatenate(ups, axis=0)
                slopes[here, :] = jnp.concatenate(slope, axis=0)

            total = jnp.zeros((SEGMENTS, tile), F32)
            for pair in range(pairs - 1, -1, -1):
                here = slice(pair * 2 * SEGMENTS, (pair + 1) * 2 * SEGMENTS)
                grads = slab_pair(back_ref, pair, span)
                retain, update, slope = kept[here, :], updates[here, :], slopes[here, :]
                late = grads[1] + leaving
                early = grads[0] + retain[SEGMENTS:] * late
                leaving = retain[:SEGMENTS] * early
                carried = jnp.concatenate([early, late], axis=0)
                gate_grad = carried * slope
                cand_grad = carried * update
                total = total + gate_grad[:SEGMENTS] + gate_grad[SEGMENTS:]
                one, other = choose(where_ref, gate_grad, cand_grad)
                one_hold[here, :] = one.astype(BF16)
                other_hold[here, :] = other.astype(BF16)
            bias_grad_ref[:, span] = jnp.sum(total, axis=0, keepdims=True)
            state_ref[:, span] = dot(order, state_hold[...]).astype(BF16)
            one_ref[span, :] = dot(order, one_hold[...]).T.astype(BF16)
            other_ref[span, :] = dot(order, other_hold[...]).T.astype(BF16)

        tiles(width, tile, body)

    wide = jax.ShapeDtypeStruct((rows, width), BF16)
    tall = jax.ShapeDtypeStruct((width, rows), BF16)
    flat = jax.ShapeDtypeStruct((1, width), F32)
    return pl.pallas_call(
        kernel,
        out_shape=[wide, tall, tall, flat, flat],
        in_specs=[SMEM_SPEC] + [VMEM_SPEC] * (5 + len(wholes)),
        out_specs=[VMEM_SPEC] * 5,
        scratch_shapes=[pltpu.VMEM((ranks, SEGMENTS, tile), F32)]
        + [pltpu.VMEM((rows, tile), F32)] * 3
        + [pltpu.VMEM((rows, tile), BF16)] * 3,
        compiler_params=params(14),
        cost_estimate=cost(6 * rows * rows * width, 12 * rows * width),
        name="scan_rows",
    )(where, *map(near, (first_pre, second_pre, back, both, parts, *wholes)))


def layer_call(where, state_rows, residual, shards, tile):
    rows, width = residual.shape
    count, depth = len(shards.groups), shards.depth

    def kernel(where_ref, x_ref, residual_ref, *refs):
        refs, (out_ref, ordered) = refs[:-2], refs[-2:]
        for index in range(count):
            source = pl.ds(pl.multiple_of((where_ref[0] ^ index) * depth, depth), depth)
            ordered[:, index * depth : (index + 1) * depth] = x_ref[:, source]

        def body(span):
            total = shards.product(ordered, 0, refs, span)
            out_ref[:, span] = (residual_ref[:, span].astype(F32) + total).astype(BF16)

        tiles(width, tile, body)

    return pl.pallas_call(
        kernel,
        out_shape=jax.ShapeDtypeStruct((rows, width), BF16),
        in_specs=[SMEM_SPEC] + [VMEM_SPEC] * 2 + [VMEM_SPEC] * len(shards.pieces),
        out_specs=VMEM_SPEC,
        scratch_shapes=[pltpu.VMEM((rows, count * depth), BF16)],
        compiler_params=params(14),
        cost_estimate=cost(2 * rows * count * depth * width, 2 * count * depth * width),
        name="layer_rows",
    )(where, near(state_rows), near(residual), *shards.operands())


def input_grad_call(where, one, other, first, second, x, grads, gain):
    rows, width = x.shape
    hidden = one.shape[0]
    count, depth = len(first.groups), first.depth

    def kernel(where_ref, one_ref, other_ref, x_ref, grads_ref, gain_ref, *refs):
        first_refs = refs[: len(first.pieces)]
        second_refs = refs[len(first.pieces) : len(first.pieces) + len(second.pieces)]
        out_ref, total = refs[-2:]
        size = min(depth, 256)
        for index in range(count):
            for part in range(0, depth, size):
                target = pl.multiple_of((where_ref[0] ^ index) * depth + part, size)
                term = dot(first.block(first_refs, index, part, size), one_ref[...])
                term = term + dot(second.block(second_refs, index, part, size), other_ref[...])
                total[:, pl.ds(target, size)] = term.T

        def body(span):
            x = x_ref[span, :].astype(F32)
            scale = lax.rsqrt(jnp.mean(x * x, axis=-1, keepdims=True) + EPSILON)
            unit = x * scale
            unit_grad = total[span, :] * gain_ref[...]
            along = jnp.mean(unit_grad * unit, axis=-1, keepdims=True)
            out = grads_ref[span, :].astype(F32) + scale * (unit_grad - unit * along)
            out_ref[span, :] = out.astype(BF16)

        tiles(rows, min(32, rows), body)

    return pl.pallas_call(
        kernel,
        out_shape=jax.ShapeDtypeStruct((rows, width), BF16),
        in_specs=[SMEM_SPEC] + [VMEM_SPEC] * 5 + [VMEM_SPEC] * (len(first.pieces) + len(second.pieces)),
        out_specs=VMEM_SPEC,
        scratch_shapes=[pltpu.VMEM((rows, width), F32)],
        compiler_params=params(14),
        cost_estimate=cost(4 * one.size * width, 4 * hidden * width),
        name="input_grad_rows",
    )(where, *map(near, (one, other, x, grads, gain)), *first.operands(), *second.operands())


def close_call(where, state_grad, rows, block):
    def kernel(where_ref, state_ref, *refs):
        refs, (state_out_ref, bias_out_ref) = refs[:-2], refs[-2:]
        here = pl.ds(pl.multiple_of(where_ref[2] * block, block), block)
        state_out_ref[...] = state_ref[:, here]
        bias_out_ref[...] = sum((ref[:, here] for ref in refs[1:]), refs[0][:, here])

    return pl.pallas_call(
        kernel,
        out_shape=[jax.ShapeDtypeStruct((1, block), F32)] * 2,
        in_specs=[SMEM_SPEC] + [VMEM_SPEC] * (1 + len(rows)),
        out_specs=[VMEM_SPEC] * 2,
        compiler_params=params(2),
        cost_estimate=cost(1, 4 * state_grad.size),
        name="close_rows",
    )(where, state_grad, *rows)


def front_on_cube(ranks, batches, where, turned, tile, rows_in, grad_rows, gain, gate_bias, state_in, w_gate, w_cand, w_out):
    half = w_gate.shape[0] // 2
    depth = w_gate.shape[0]
    halves = lambda w: (w[:half], w[half:])
    straight = turned == 0
    send = lambda value, offset: hop(value, offset, ranks)
    core = lambda value: hop(value, 1, ranks)
    over = lambda value: swap_batch(value, 1, batches)
    f_a = jnp.where(straight, w_gate[:half], w_cand[:half])
    f_a, where, w_gate, w_cand, own_t = after((f_a, where, w_gate, w_cand, w_out))
    own_f = [f_a, jnp.where(straight, w_gate[half:], w_cand[half:])]
    stack = lambda *parts: jnp.concatenate(parts, axis=0)
    cut = lambda held, *starts: [(held, start * half, half) for start in starts]
    f2a, f4a = send(own_f[0], 2), send(own_f[0], 4)
    f1 = [core(v) for v in own_f]
    both = jnp.stack([gate_bias, state_in[0]])
    both = jnp.concatenate([both, core(both)], axis=1)
    both = jnp.concatenate([both, send(both, 2)], axis=1)
    normed, grads = norm_call(where, rows_in, grad_rows, gain, depth)
    own_s = jnp.where(straight, w_cand, w_gate)
    t_a, t_b = halves(own_t)
    f2a, f4a, f1a, f1b, both, normed, grads, f_b, own_s, own_t, t_a, t_b = after(
        (f2a, f4a, f1[0], f1[1], both, normed, grads, own_f[1], own_s, own_t, t_a, t_b)
    )
    f2b, f4b = send(f_b, 2), send(f_b, 4)
    t2a, t4a = send(t_a, 2), send(t_a, 4)
    sa = over(stack(f2a, f4a))
    f2b, f4b, f3a, f5a, s1 = after((f2b, f4b, f2a, f4a, own_s))
    f3a, f5a, s1 = core(f3a), core(f5a), core(s1)
    f2b, f4b, sa, t2a, t4a, f3a, f5a, s1, t_b, f2a = after((f2b, f4b, sa, t2a, t4a, f3a, f5a, s1, t_b, f2a))
    f6a, f6b = send(f2a, 4), send(f4b, 2)
    t2b, t4b = send(t_b, 2), send(t_b, 4)
    sb = over(stack(f2b, f4b))
    f6a, f6b, f3b, f5b, t3a, t5a = after((f6a, f6b, f2b, f4b, t2a, t4a))
    f3b, f5b, t3a, t5a = core(f3b), core(f5b), core(t3a), core(t5a)
    both, f6a, f6b, sb, t2b, t4b, f3b, f5b, t3a, t5a, sa, t2a = after(
        (both, f6a, f6b, sb, t2b, t4b, f3b, f5b, t3a, t5a, sa, t2a)
    )
    t6a, t6b = send(t2a, 4), send(t4b, 2)
    s6a = over(f6a)
    f7, cs = core(stack(f6a, f6b)), core(stack(sa, sb))
    first = Shards([own_f, [f1a, f1b], [f2a, f2b], [f3a, f3b], [f4a, f4b], [f5a, f5b], [f6a, f6b], [f7]])
    pairs = lambda one, two, row: cut(one, row) + cut(two, row)
    most = [[own_s], [s1], pairs(sa, sb, 0), cut(cs, 0, 2), pairs(sa, sb, 1), cut(cs, 1, 3)]
    first_pre = project_call(normed, first, tile, BF16)
    partial = project_call(normed, Shards(most), tile, F32)
    t6a, t6b, s6a, sb_out, first_pre, partial, own_t, both = after(
        (t6a, t6b, s6a, sb, first_pre, partial, own_t, both)
    )
    quarter = half // 2
    s6b = [send(sb_out[half : half + quarter], 2), send(sb_out[quarter:half], 4)]
    s7a = core(s6a)
    c4 = core(stack(t6a, t6b, t2b, t4b, own_t))
    third = Shards(
        [[own_t], cut(c4, 4, 5), [t2a, t2b], [t3a, (c4, 2 * half, half)], [t4a, t4b], [t5a, (c4, 3 * half, half)]]
        + [[t6a, t6b], cut(c4, 0, 1)]
    )
    both = jnp.concatenate([both, send(both, 4)], axis=1)
    back = back_call(where, grads, third)
    s6b_low, s6b_high, s7a, back, both = after((*s6b, s7a, back, both))
    last = [[s6a, s6b_low, s6b_high], [s7a, core(stack(s6b_low, s6b_high))]]
    second = Shards(most + last)
    second_pre, parts, whole, both = totals_call(
        where, normed, partial, Shards(last), len(most) * depth, first_pre, back, both, depth, tile
    )
    return where, first, second, third, first_pre, second_pre, back, both, parts, whole


def front(where, tile, rows_in, grad_rows, gain, gate_bias, state_in, w_gate, w_cand, w_out):
    first, second, third = (
        Shards([[lax.all_gather(w, "seq", tiled=True)]]) for w in (w_gate, w_cand, w_out)
    )
    both = lax.all_gather(jnp.stack([gate_bias, state_in[0]]), "seq", axis=1, tiled=True)
    normed, grads = norm_call(where, rows_in, grad_rows, gain, first.depth)
    first_pre = project_call(normed, first, tile, BF16)
    back = back_call(where, grads, third)
    second_pre, parts, whole, both = totals_call(
        where, normed, None, second, 0, first_pre, back, both, first.depth, tile
    )
    return where, first, second, third, first_pre, second_pre, back, both, parts, whole


def on_device(ranks, batches, inputs, output_grad, norm_gain, gate_bias, state_in, w_gate, w_cand, w_out):
    rows_in, grad_rows = inputs[0], output_grad[0]
    gain = norm_gain[None, :]
    hidden = w_gate.shape[1]
    tile = min(512, hidden)
    me = lax.axis_index("seq")
    given = (rows_in, grad_rows, gain, gate_bias, state_in, w_gate, w_cand, w_out)
    cube = ranks == 8 and batches in (2, 4, 8)
    if cube:
        turned = lax.axis_index("batch") % 2
        where = jnp.stack([me, turned, me]).astype(jnp.int32)
        found = front_on_cube(ranks, batches, where, turned, tile, *given)
    else:
        nought = jnp.zeros_like(me)
        where = jnp.stack([nought, nought, me]).astype(jnp.int32)
        found = front(where, tile, *given)
    where, first, second, third, first_pre, second_pre, back, both, parts, whole = found
    if cube:
        chip = jnp.stack([whole, hop(whole, 1, ranks)])
        wholes = [chip] + [hop(chip, offset, ranks) for offset in (2, 4, 6)]
    else:
        wholes = [lax.all_gather(whole, "seq")]
    state_rows, one, other, bias_part, state_grad = scan_call(
        where, first_pre, second_pre, back, both, parts, wholes, ranks, tile
    )
    width = hidden // ranks
    if cube:
        pair = bias_part + hop(bias_part, 1, ranks)
        layer_out = layer_call(where, state_rows, rows_in, third, tile)
        plane = [hop(pair, offset, ranks) for offset in (2, 4, 6)]
        layer_out, pair, *plane = after((layer_out, pair) + tuple(plane))
        plane = pair + plane[0] + plane[1] + plane[2]
        far = [swap_batch(plane, offset, batches) for offset in range(1, batches)]
        one, other, plane = after((one, other, plane), layer_out)
        input_grad = input_grad_call(where, one, other, first, second, rows_in, grad_rows, gain)
        state_out, bias_grad = close_call(where, state_grad, [plane] + far, width)
        bias_grad = bias_grad[0]
    else:
        over_seq = lax.psum_scatter(bias_part[0], "seq", scatter_dimension=0, tiled=True)
        bias_grad = lax.psum(over_seq, "batch")
        layer_out = layer_call(where, state_rows, rows_in, third, tile)
        input_grad = input_grad_call(where, one, other, first, second, rows_in, grad_rows, gain)
        state_out = lax.dynamic_slice_in_dim(state_grad, me * width, width, 1)
    return (layer_out[None], input_grad[None], state_out, bias_grad)


def solution(mesh):
    body = functools.partial(on_device, mesh.shape["seq"], mesh.shape["batch"])
    rows = P("batch", "seq", None)
    return jax.shard_map(
        body,
        mesh=mesh,
        in_specs=(rows, rows, P(), P("seq"), P("batch", "seq"), P("seq", None), P("seq", None), P("seq", None)),
        out_specs=(rows, rows, P("batch", "seq"), P("seq")),
        check_vma=False,
    )
```

```python
import functools

import jax
import jax.numpy as jnp
from jax import lax
from jax.experimental import pallas as pl
from jax.experimental.pallas import tpu as pltpu
from jax.sharding import PartitionSpec as P

EPSILON = 1e-06
SEGMENTS = 8
LARGE = 1e37
F32 = jnp.float32
BF16 = jnp.bfloat16


def params(mebibytes):
    return pltpu.CompilerParams(vmem_limit_bytes=mebibytes * 1024 * 1024)


def cost(flops, moved):
    return pl.CostEstimate(flops=int(flops), bytes_accessed=int(moved), transcendentals=0)


def hop(value, offset, count):
    return lax.ppermute(value, "seq", [(i, i ^ offset) for i in range(count)])


def swap_batch(value, offset, count):
    return lax.ppermute(value, "batch", [(i, i ^ offset) for i in range(count)])


def after(values, *earlier):
    return lax.optimization_barrier(tuple(values) + tuple(earlier))[: len(values)]


def place(rows):
    steps = rows // SEGMENTS
    out = lax.broadcasted_iota(jnp.int32, (rows, rows), 0)
    inn = lax.broadcasted_iota(jnp.int32, (rows, rows), 1)
    source = lax.rem(out, SEGMENTS) * steps + lax.div(out, SEGMENTS)
    return (source == inn).astype(F32).astype(BF16)


def place_back(rows):
    steps = rows // SEGMENTS
    out = lax.broadcasted_iota(jnp.int32, (rows, rows), 0)
    inn = lax.broadcasted_iota(jnp.int32, (rows, rows), 1)
    source = lax.rem(out, steps) * SEGMENTS + lax.div(out, steps)
    return (source == inn).astype(F32).astype(BF16)


def dot(a, b):
    return lax.dot_general(a, b, (((1,), (0,)), ((), ())), preferred_element_type=F32)


def tiles(count, tile, body):
    @pl.loop(0, count // tile)
    def _(index):
        body(pl.ds(pl.multiple_of(index * tile, tile), tile))


class Shards:
    def __init__(self, groups):
        self.pieces, self.groups = [], []
        for group in groups:
            made = []
            for piece in group:
                array, start, rows = piece if isinstance(piece, tuple) else (piece, 0, piece.shape[0])
                known = [index for index, other in enumerate(self.pieces) if other is array]
                if not known:
                    known = [len(self.pieces)]
                    self.pieces.append(array)
                made.append((known[0], start, rows))
            self.groups.append(made)
        self.depth = sum(rows for _, _, rows in self.groups[0])
        self.width = self.pieces[0].shape[1]

    def operands(self):
        return [pltpu.with_memory_space_constraint(piece, pltpu.VMEM) for piece in self.pieces]

    def block(self, refs, index, part, size):
        found, begin = [], 0
        for which, start, rows in self.groups[index]:
            low, high = max(part, begin), min(part + size, begin + rows)
            if low < high:
                found.append(refs[which][start + low - begin : start + high - begin, :])
            begin += rows
        return found[0] if len(found) == 1 else jnp.concatenate(found, axis=0)

    def product(self, x_ref, skip, refs, span):
        total = None
        joint = max(1, min(len(self.groups), 4))
        for index in range(0, len(self.groups), joint):
            groups = self.groups[index : index + joint]
            found = [refs[which][start : start + rows, span] for group in groups for which, start, rows in group]
            block = found[0] if len(found) == 1 else jnp.concatenate(found, axis=0)
            start = skip + index * self.depth
            term = dot(x_ref[:, start : start + len(groups) * self.depth], block)
            total = term if total is None else total + term
        return total


def near(value):
    return pltpu.with_memory_space_constraint(value, pltpu.VMEM)


VMEM_SPEC = pl.BlockSpec(memory_space=pltpu.VMEM)
SMEM_SPEC = pl.BlockSpec(memory_space=pltpu.SMEM)


def norm_call(where, x, g, gain, depth):
    rows, width = x.shape

    def kernel(where_ref, x_ref, g_ref, gain_ref, normed_ref, grads_ref, hold):
        def rows_body(span):
            x = x_ref[span, :].astype(F32)
            scale = lax.rsqrt(jnp.mean(x * x, axis=-1, keepdims=True) + EPSILON)
            hold[span, :] = (x * scale * gain_ref[...]).astype(BF16)

        tiles(rows, min(32, rows), rows_body)
        order = place(rows)
        for index in range(width // depth):
            source = pl.ds(pl.multiple_of((where_ref[0] ^ index) * depth, depth), depth)
            normed_ref[:, index * depth : (index + 1) * depth] = dot(order, hold[:, source]).astype(BF16)

        def grads_body(span):
            grads_ref[span, :] = dot(order, g_ref[:, span]).T.astype(BF16)

        tiles(width, min(512, width), grads_body)

    return pl.pallas_call(
        kernel,
        out_shape=[jax.ShapeDtypeStruct((rows, width), BF16), jax.ShapeDtypeStruct((width, rows), BF16)],
        in_specs=[SMEM_SPEC] + [VMEM_SPEC] * 3,
        out_specs=[VMEM_SPEC] * 2,
        scratch_shapes=[pltpu.VMEM(x.shape, BF16)],
        compiler_params=params(14),
        cost_estimate=cost(4 * rows * x.size, 8 * x.size),
        name="norm_rows",
    )(where, near(x), near(g), near(gain))


def project_call(x, shards, tile, dtype, skip=0):
    rows, width = x.shape[0], shards.width
    count, depth = len(shards.groups), shards.depth

    def kernel(x_ref, *refs):
        refs, out_ref = refs[:-1], refs[-1]

        def body(span):
            out_ref[:, span] = shards.product(x_ref, skip, refs, span).astype(dtype)

        tiles(width, tile, body)

    return pl.pallas_call(
        kernel,
        out_shape=jax.ShapeDtypeStruct((rows, width), dtype),
        in_specs=[VMEM_SPEC] + [VMEM_SPEC] * len(shards.pieces),
        out_specs=VMEM_SPEC,
        compiler_params=params(14),
        cost_estimate=cost(2 * rows * count * depth * width, 2 * count * depth * width),
        name="project",
    )(near(x), *shards.operands())


def back_call(where, grads, shards):
    width, rows = grads.shape
    count, depth = len(shards.groups), shards.depth

    def kernel(where_ref, g_ref, *refs):
        refs, out_ref = refs[:-1], refs[-1]
        size = min(depth, 256)
        for index in range(count):
            for part in range(0, depth, size):
                target = pl.multiple_of((where_ref[0] ^ index) * depth + part, size)
                term = dot(shards.block(refs, index, part, size), g_ref[...])
                out_ref[:, pl.ds(target, size)] = term.T.astype(BF16)

    return pl.pallas_call(
        kernel,
        out_shape=jax.ShapeDtypeStruct((rows, count * depth), BF16),
        in_specs=[SMEM_SPEC, VMEM_SPEC] + [VMEM_SPEC] * len(shards.pieces),
        out_specs=VMEM_SPEC,
        compiler_params=params(14),
        cost_estimate=cost(2 * rows * count * depth * width, 2 * count * depth * width),
        name="back_rows",
    )(where, near(grads), *shards.operands())


def gates(x):
    under = 1.0 + jnp.minimum(jnp.exp(-x), LARGE)
    rough = pl.reciprocal(under, approx=True)
    update = rough * (2.0 - under * rough)
    return update, 1.0 - update


def slab_pair(ref, pair, span):
    return split(ref[pair * 2 * SEGMENTS : (pair + 1) * 2 * SEGMENTS, span])


def split(both):
    both = both.astype(F32)
    return both[:SEGMENTS], both[SEGMENTS:]


def chosen_pair(where_ref, first_ref, second_ref, pair, span):
    here = slice(pair * 2 * SEGMENTS, (pair + 1) * 2 * SEGMENTS)
    gate, cand = choose(where_ref, first_ref[here, span], second_ref[here, span])
    return split(gate), split(cand)


def choose(where_ref, one, other):
    straight = where_ref[1] == 0
    return jnp.where(straight, one, other), jnp.where(straight, other, one)


def totals_call(where, x, partial, shards, skip, first_pre, back, both, block, tile):
    rows, width = first_pre.shape
    pairs = rows // (2 * SEGMENTS)
    count, depth = len(shards.groups), shards.depth
    extra = [] if partial is None else [partial]

    def kernel(where_ref, x_ref, first_ref, back_ref, both_ref, *refs):
        partial_refs, refs = refs[: len(extra)], refs[len(extra) :]
        refs, (second_ref, parts_ref, whole_ref, rows_ref) = refs[:-4], refs[-4:]
        for index in range(width // block):
            target = pl.multiple_of((where_ref[0] ^ index) * block, block)
            rows_ref[:, pl.ds(target, block)] = both_ref[:, index * block : (index + 1) * block]

        def body(span):
            total = shards.product(x_ref, skip, refs, span)
            for ref in partial_refs:
                total = total + ref[:, span]
            second_ref[:, span] = total.astype(BF16)
            bias = rows_ref[0:1, span]
            keep = jnp.ones((SEGMENTS, tile), F32)
            state = leaving = jnp.zeros((SEGMENTS, tile), F32)
            for pair in range(pairs):
                slabs = chosen_pair(where_ref, first_ref, second_ref, pair, span)
                for gate, cand, g in zip(*slabs, slab_pair(back_ref, pair, span)):
                    update, retain = gates(gate + bias)
                    keep = keep * retain
                    state = retain * state + update * cand
                    leaving = leaving + keep * g
            parts_ref[0, :, span], parts_ref[1, :, span], parts_ref[2, :, span] = keep, state, leaving
            whole_keep, whole_state = keep[0:1], state[0:1]
            for s in range(1, SEGMENTS):
                whole_state = keep[s : s + 1] * whole_state + state[s : s + 1]
                whole_keep = whole_keep * keep[s : s + 1]
            whole_leaving = leaving[SEGMENTS - 1 :]
            for s in range(SEGMENTS - 2, -1, -1):
                whole_leaving = keep[s : s + 1] * whole_leaving + leaving[s : s + 1]
            whole_ref[0:1, span], whole_ref[1:2, span], whole_ref[2:3, span] = whole_keep, whole_state, whole_leaving

        tiles(width, tile, body)

    return pl.pallas_call(
        kernel,
        out_shape=[
            jax.ShapeDtypeStruct((rows, width), BF16),
            jax.ShapeDtypeStruct((3, SEGMENTS, width), F32),
            jax.ShapeDtypeStruct((3, width), F32),
            jax.ShapeDtypeStruct((2, width), F32),
        ],
        in_specs=[SMEM_SPEC] + [VMEM_SPEC] * (4 + len(extra)) + [VMEM_SPEC] * len(shards.pieces),
        out_specs=[VMEM_SPEC] * 4,
        compiler_params=params(14),
        cost_estimate=cost(2 * rows * count * depth * width, 2 * count * depth * width),
        name="project_totals",
    )(where, *map(near, (x, first_pre, back, both, *extra)), *shards.operands())


def scan_call(where, first_pre, second_pre, back, both, parts, wholes, ranks, tile):
    rows, width = first_pre.shape
    pairs = rows // (2 * SEGMENTS)

    def kernel(where_ref, first_ref, second_ref, back_ref, both_ref, parts_ref, *refs):
        whole_refs, refs = refs[: len(wholes)], refs[len(wholes) :]
        (state_ref, one_ref, other_ref, bias_grad_ref, state_grad_ref) = refs[:5]
        hold, kept, updates, slopes, one_hold, other_hold, state_hold = refs[5:]
        me = where_ref[2]
        order = place_back(rows)

        def body(span):
            entering = both_ref[1:2, span]
            per = ranks // len(wholes)
            for index, ref in enumerate(whole_refs):
                for member in range(per):
                    offset = index * per + member
                    hold[me ^ offset if len(wholes) > 1 else offset, 0:3, :] = ref[member, :, span]
            blocks = [hold[rank] for rank in range(ranks)]
            for rank in range(ranks):
                block = blocks[rank]
                entering = jnp.where(rank < me, block[0:1] * entering + block[1:2], entering)
            arriving = state_grad = blocks[0][2:3] * 0.0
            for rank in range(ranks - 1, -1, -1):
                block = blocks[rank]
                arriving = jnp.where(rank == me, state_grad, arriving)
                state_grad = block[0:1] * state_grad + block[2:3]
            state_grad_ref[:, span] = state_grad
            keep, ends, leaves = parts_ref[0, :, span], parts_ref[1, :, span], parts_ref[2, :, span]
            starts = [entering]
            for s in range(SEGMENTS - 1):
                starts.append(keep[s : s + 1] * starts[-1] + ends[s : s + 1])
            tails = [arriving]
            for s in range(SEGMENTS - 1, 0, -1):
                tails.append(keep[s : s + 1] * tails[-1] + leaves[s : s + 1])
            state = jnp.concatenate(starts, axis=0)
            leaving = jnp.concatenate(tails[::-1], axis=0)
            bias = both_ref[0:1, span]

            for pair in range(pairs):
                states, retains, ups, slope = [], [], [], []
                for gate, cand in zip(*chosen_pair(where_ref, first_ref, second_ref, pair, span)):
                    update, retain = gates(gate + bias)
                    retains.append(retain)
                    ups.append(update)
                    slope.append((cand - state) * update * retain)
                    state = retain * state + update * cand
                    states.append(state)
                here = slice(pair * 2 * SEGMENTS, (pair + 1) * 2 * SEGMENTS)
                state_hold[here, :] = jnp.concatenate(states, axis=0).astype(BF16)
                kept[here, :] = jnp.concatenate(retains, axis=0)
                updates[here, :] = jnp.concatenate(ups, axis=0)
                slopes[here, :] = jnp.concatenate(slope, axis=0)

            total = jnp.zeros((SEGMENTS, tile), F32)
            for pair in range(pairs - 1, -1, -1):
                here = slice(pair * 2 * SEGMENTS, (pair + 1) * 2 * SEGMENTS)
                grads = slab_pair(back_ref, pair, span)
                retain, update, slope = kept[here, :], updates[here, :], slopes[here, :]
                late = grads[1] + leaving
                early = grads[0] + retain[SEGMENTS:] * late
                leaving = retain[:SEGMENTS] * early
                carried = jnp.concatenate([early, late], axis=0)
                gate_grad = carried * slope
                cand_grad = carried * update
                total = total + gate_grad[:SEGMENTS] + gate_grad[SEGMENTS:]
                one, other = choose(where_ref, gate_grad.astype(BF16), cand_grad.astype(BF16))
                one_hold[here, :] = one
                other_hold[here, :] = other
            bias_grad_ref[:, span] = jnp.sum(total, axis=0, keepdims=True)
            state_ref[:, span] = dot(order, state_hold[...]).astype(BF16)
            one_ref[span, :] = dot(order, one_hold[...]).T.astype(BF16)
            other_ref[span, :] = dot(order, other_hold[...]).T.astype(BF16)

        tiles(width, tile, body)

    wide = jax.ShapeDtypeStruct((rows, width), BF16)
    tall = jax.ShapeDtypeStruct((width, rows), BF16)
    flat = jax.ShapeDtypeStruct((1, width), F32)
    return pl.pallas_call(
        kernel,
        out_shape=[wide, tall, tall, flat, flat],
        in_specs=[SMEM_SPEC] + [VMEM_SPEC] * (5 + len(wholes)),
        out_specs=[VMEM_SPEC] * 5,
        scratch_shapes=[pltpu.VMEM((ranks, SEGMENTS, tile), F32)]
        + [pltpu.VMEM((rows, tile), F32)] * 3
        + [pltpu.VMEM((rows, tile), BF16)] * 3,
        compiler_params=params(14),
        cost_estimate=cost(6 * rows * rows * width, 12 * rows * width),
        name="scan_rows",
    )(where, *map(near, (first_pre, second_pre, back, both, parts, *wholes)))


def layer_call(where, state_rows, residual, shards, tile):
    rows, width = residual.shape
    count, depth = len(shards.groups), shards.depth

    def kernel(where_ref, x_ref, residual_ref, *refs):
        refs, (out_ref, ordered) = refs[:-2], refs[-2:]
        for index in range(count):
            source = pl.ds(pl.multiple_of((where_ref[0] ^ index) * depth, depth), depth)
            ordered[:, index * depth : (index + 1) * depth] = x_ref[:, source]

        def body(span):
            total = shards.product(ordered, 0, refs, span)
            out_ref[:, span] = (residual_ref[:, span].astype(F32) + total).astype(BF16)

        tiles(width, tile, body)

    return pl.pallas_call(
        kernel,
        out_shape=jax.ShapeDtypeStruct((rows, width), BF16),
        in_specs=[SMEM_SPEC] + [VMEM_SPEC] * 2 + [VMEM_SPEC] * len(shards.pieces),
        out_specs=VMEM_SPEC,
        scratch_shapes=[pltpu.VMEM((rows, count * depth), BF16)],
        compiler_params=params(14),
        cost_estimate=cost(2 * rows * count * depth * width, 2 * count * depth * width),
        name="layer_rows",
    )(where, near(state_rows), near(residual), *shards.operands())


def input_grad_call(where, one, other, first, second, x, grads, gain):
    rows, width = x.shape
    hidden = one.shape[0]
    count, depth = len(first.groups), first.depth

    def kernel(where_ref, one_ref, other_ref, x_ref, grads_ref, gain_ref, *refs):
        first_refs = refs[: len(first.pieces)]
        second_refs = refs[len(first.pieces) : len(first.pieces) + len(second.pieces)]
        out_ref, total = refs[-2:]
        size = min(depth, 256)
        for index in range(count):
            for part in range(0, depth, size):
                target = pl.multiple_of((where_ref[0] ^ index) * depth + part, size)
                term = dot(first.block(first_refs, index, part, size), one_ref[...])
                term = term + dot(second.block(second_refs, index, part, size), other_ref[...])
                total[:, pl.ds(target, size)] = term.T

        def body(span):
            x = x_ref[span, :].astype(F32)
            scale = lax.rsqrt(jnp.mean(x * x, axis=-1, keepdims=True) + EPSILON)
            unit = x * scale
            unit_grad = total[span, :] * gain_ref[...]
            along = jnp.mean(unit_grad * unit, axis=-1, keepdims=True)
            out = grads_ref[span, :].astype(F32) + scale * (unit_grad - unit * along)
            out_ref[span, :] = out.astype(BF16)

        tiles(rows, min(32, rows), body)

    return pl.pallas_call(
        kernel,
        out_shape=jax.ShapeDtypeStruct((rows, width), BF16),
        in_specs=[SMEM_SPEC] + [VMEM_SPEC] * 5 + [VMEM_SPEC] * (len(first.pieces) + len(second.pieces)),
        out_specs=VMEM_SPEC,
        scratch_shapes=[pltpu.VMEM((rows, width), F32)],
        compiler_params=params(14),
        cost_estimate=cost(4 * one.size * width, 4 * hidden * width),
        name="input_grad_rows",
    )(where, *map(near, (one, other, x, grads, gain)), *first.operands(), *second.operands())


def close_call(where, state_grad, rows, block):
    def kernel(where_ref, state_ref, *refs):
        refs, (state_out_ref, bias_out_ref) = refs[:-2], refs[-2:]
        here = pl.ds(pl.multiple_of(where_ref[2] * block, block), block)
        state_out_ref[...] = state_ref[:, here]
        bias_out_ref[...] = sum((ref[:, here] for ref in refs[1:]), refs[0][:, here])

    return pl.pallas_call(
        kernel,
        out_shape=[jax.ShapeDtypeStruct((1, block), F32)] * 2,
        in_specs=[SMEM_SPEC] + [VMEM_SPEC] * (1 + len(rows)),
        out_specs=[VMEM_SPEC] * 2,
        compiler_params=params(2),
        cost_estimate=cost(1, 4 * state_grad.size),
        name="close_rows",
    )(where, state_grad, *rows)


def front_on_cube(ranks, batches, where, turned, tile, rows_in, grad_rows, gain, gate_bias, state_in, w_gate, w_cand, w_out):
    half = w_gate.shape[0] // 2
    depth = w_gate.shape[0]
    halves = lambda w: (w[:half], w[half:])
    straight = turned == 0
    send = lambda value, offset: hop(value, offset, ranks)
    core = lambda value: hop(value, 1, ranks)
    over = lambda value: swap_batch(value, 1, batches)
    f_a = jnp.where(straight, w_gate[:half], w_cand[:half])
    f_a, where, w_gate, w_cand, own_t = after((f_a, where, w_gate, w_cand, w_out))
    own_f = [f_a, jnp.where(straight, w_gate[half:], w_cand[half:])]
    stack = lambda *parts: jnp.concatenate(parts, axis=0)
    cut = lambda held, *starts: [(held, start * half, half) for start in starts]
    f2a, f4a = send(own_f[0], 2), send(own_f[0], 4)
    f1 = [core(v) for v in own_f]
    both = jnp.stack([gate_bias, state_in[0]])
    both = jnp.concatenate([both, core(both)], axis=1)
    both = jnp.concatenate([both, send(both, 2)], axis=1)
    normed, grads = norm_call(where, rows_in, grad_rows, gain, depth)
    own_s = jnp.where(straight, w_cand, w_gate)
    t_a, t_b = halves(own_t)
    f2a, f4a, f1a, f1b, both, normed, grads, f_b, own_s, own_t, t_a, t_b = after(
        (f2a, f4a, f1[0], f1[1], both, normed, grads, own_f[1], own_s, own_t, t_a, t_b)
    )
    f2b, f4b = send(f_b, 2), send(f_b, 4)
    t2a, t4a = send(t_a, 2), send(t_a, 4)
    sa = over(stack(f2a, f4a))
    f2b, f4b, f3a, f5a = after((f2b, f4b, f2a, f4a))
    f3a, f5a = core(f3a), core(f5a)
    f2b, f4b, f_b2, sa, t2a, t4a, f3a, f5a, t_b, f2a = after(
        (f2b, f4b, stack(f2b, f4b), sa, t2a, t4a, f3a, f5a, t_b, f2a)
    )
    f6a, f6b = send(f2a, 4), send(f4b, 2)
    t2b, t4b = send(t_b, 2), send(t_b, 4)
    sb = over(f_b2)
    f6a, f6b, f3b, f5b, t3a, t5a = after((f6a, f6b, f2b, f4b, t2a, t4a))
    f3b, f5b, t3a, t5a = core(f3b), core(f5b), core(t3a), core(t5a)
    both, f6a, f6b, sb, t2b, t4b, f3b, f5b, t3a, t5a, sa, t2a = after(
        (both, f6a, f6b, sb, t2b, t4b, f3b, f5b, t3a, t5a, sa, t2a)
    )
    t6a, t6b = send(t2a, 4), send(t4b, 2)
    s6a = over(f6a)
    f7, cs = core(stack(f6a, f6b)), core(stack(sa, sb, own_s))
    first = Shards([own_f, [f1a, f1b], [f2a, f2b], [f3a, f3b], [f4a, f4b], [f5a, f5b], [f6a, f6b], [f7]])
    pairs = lambda one, two, row: cut(one, row) + cut(two, row)
    most = [[own_s], cut(cs, 4, 5), pairs(sa, sb, 0), cut(cs, 0, 2), pairs(sa, sb, 1), cut(cs, 1, 3)]
    first_pre = project_call(normed, first, tile, BF16)
    partial = project_call(normed, Shards(most), tile, F32)
    t6a, t6b, s6a, sb_out, first_pre, partial, own_t, both = after(
        (t6a, t6b, s6a, sb, first_pre, partial, own_t, both)
    )
    quarter = half // 2
    s6b = [send(sb_out[half : half + quarter], 2), send(sb_out[quarter:half], 4)]
    s7a = core(s6a)
    c4 = core(stack(t6a, t6b, t2b, t4b, own_t))
    third = Shards(
        [[own_t], cut(c4, 4, 5), [t2a, t2b], [t3a, (c4, 2 * half, half)], [t4a, t4b], [t5a, (c4, 3 * half, half)]]
        + [[t6a, t6b], cut(c4, 0, 1)]
    )
    both = jnp.concatenate([both, send(both, 4)], axis=1)
    back = back_call(where, grads, third)
    s6b_low, s6b_high, s7a, back, both = after((*s6b, s7a, back, both))
    last = [[s6a, s6b_low, s6b_high], [s7a, core(stack(s6b_low, s6b_high))]]
    second = Shards(most + last)
    second_pre, parts, whole, both = totals_call(
        where, normed, partial, Shards(last), len(most) * depth, first_pre, back, both, depth, tile
    )
    return where, first, second, third, first_pre, second_pre, back, both, parts, whole


def front(where, tile, rows_in, grad_rows, gain, gate_bias, state_in, w_gate, w_cand, w_out):
    first, second, third = (
        Shards([[lax.all_gather(w, "seq", tiled=True)]]) for w in (w_gate, w_cand, w_out)
    )
    both = lax.all_gather(jnp.stack([gate_bias, state_in[0]]), "seq", axis=1, tiled=True)
    normed, grads = norm_call(where, rows_in, grad_rows, gain, first.depth)
    first_pre = project_call(normed, first, tile, BF16)
    back = back_call(where, grads, third)
    second_pre, parts, whole, both = totals_call(
        where, normed, None, second, 0, first_pre, back, both, first.depth, tile
    )
    return where, first, second, third, first_pre, second_pre, back, both, parts, whole


def on_device(ranks, batches, inputs, output_grad, norm_gain, gate_bias, state_in, w_gate, w_cand, w_out):
    rows_in, grad_rows = inputs[0], output_grad[0]
    gain = norm_gain[None, :]
    hidden = w_gate.shape[1]
    tile = min(512, hidden)
    me = lax.axis_index("seq")
    given = (rows_in, grad_rows, gain, gate_bias, state_in, w_gate, w_cand, w_out)
    cube = ranks == 8 and batches in (2, 4, 8)
    if cube:
        turned = lax.axis_index("batch") % 2
        where = jnp.stack([me, turned, me]).astype(jnp.int32)
        found = front_on_cube(ranks, batches, where, turned, tile, *given)
    else:
        nought = jnp.zeros_like(me)
        where = jnp.stack([nought, nought, me]).astype(jnp.int32)
        found = front(where, tile, *given)
    where, first, second, third, first_pre, second_pre, back, both, parts, whole = found
    if cube:
        chip = jnp.stack([whole, hop(whole, 1, ranks)])
        wholes = [chip] + [hop(chip, offset, ranks) for offset in (2, 4, 6)]
    else:
        wholes = [lax.all_gather(whole, "seq")]
    state_rows, one, other, bias_part, state_grad = scan_call(
        where, first_pre, second_pre, back, both, parts, wholes, ranks, tile
    )
    width = hidden // ranks
    if cube:
        pair = bias_part + hop(bias_part, 1, ranks)
        layer_out = layer_call(where, state_rows, rows_in, third, tile)
        plane = [hop(pair, offset, ranks) for offset in (2, 4, 6)]
        layer_out, pair, *plane = after((layer_out, pair) + tuple(plane))
        plane = pair + plane[0] + plane[1] + plane[2]
        far = [swap_batch(plane, offset, batches) for offset in range(1, batches)]
        one, other, plane = after((one, other, plane), layer_out)
        input_grad = input_grad_call(where, one, other, first, second, rows_in, grad_rows, gain)
        state_out, bias_grad = close_call(where, state_grad, [plane] + far, width)
        bias_grad = bias_grad[0]
    else:
        over_seq = lax.psum_scatter(bias_part[0], "seq", scatter_dimension=0, tiled=True)
        bias_grad = lax.psum(over_seq, "batch")
        layer_out = layer_call(where, state_rows, rows_in, third, tile)
        input_grad = input_grad_call(where, one, other, first, second, rows_in, grad_rows, gain)
        state_out = lax.dynamic_slice_in_dim(state_grad, me * width, width, 1)
    return (layer_out[None], input_grad[None], state_out, bias_grad)


def solution(mesh):
    body = functools.partial(on_device, mesh.shape["seq"], mesh.shape["batch"])
    rows = P("batch", "seq", None)
    return jax.shard_map(
        body,
        mesh=mesh,
        in_specs=(rows, rows, P(), P("seq"), P("batch", "seq"), P("seq", None), P("seq", None), P("seq", None)),
        out_specs=(rows, rows, P("batch", "seq"), P("seq")),
        check_vma=False,
    )
```

```python
import functools

import jax
import jax.numpy as jnp
from jax import lax
from jax.experimental import pallas as pl
from jax.experimental.pallas import tpu as pltpu
from jax.sharding import PartitionSpec as P

EPSILON = 1e-06
SEGMENTS = 8
LARGE = 1e37
F32 = jnp.float32
BF16 = jnp.bfloat16


def params(mebibytes):
    return pltpu.CompilerParams(vmem_limit_bytes=mebibytes * 1024 * 1024)


def cost(flops, moved):
    return pl.CostEstimate(flops=int(flops), bytes_accessed=int(moved), transcendentals=0)


def hop(value, offset, count):
    return lax.ppermute(value, "seq", [(i, i ^ offset) for i in range(count)])


def swap_batch(value, offset, count):
    return lax.ppermute(value, "batch", [(i, i ^ offset) for i in range(count)])


def after(values, *earlier):
    return lax.optimization_barrier(tuple(values) + tuple(earlier))[: len(values)]


def place(rows):
    steps = rows // SEGMENTS
    out = lax.broadcasted_iota(jnp.int32, (rows, rows), 0)
    inn = lax.broadcasted_iota(jnp.int32, (rows, rows), 1)
    source = lax.rem(out, SEGMENTS) * steps + lax.div(out, SEGMENTS)
    return (source == inn).astype(F32).astype(BF16)


def place_back(rows):
    steps = rows // SEGMENTS
    out = lax.broadcasted_iota(jnp.int32, (rows, rows), 0)
    inn = lax.broadcasted_iota(jnp.int32, (rows, rows), 1)
    source = lax.rem(out, steps) * SEGMENTS + lax.div(out, steps)
    return (source == inn).astype(F32).astype(BF16)


def dot(a, b):
    return lax.dot_general(a, b, (((1,), (0,)), ((), ())), preferred_element_type=F32)


def tiles(count, tile, body):
    @pl.loop(0, count // tile)
    def _(index):
        body(pl.ds(pl.multiple_of(index * tile, tile), tile))


class Shards:
    def __init__(self, groups):
        self.pieces, self.groups = [], []
        for group in groups:
            made = []
            for piece in group:
                array, start, rows = piece if isinstance(piece, tuple) else (piece, 0, piece.shape[0])
                known = [index for index, other in enumerate(self.pieces) if other is array]
                if not known:
                    known = [len(self.pieces)]
                    self.pieces.append(array)
                made.append((known[0], start, rows))
            self.groups.append(made)
        self.depth = sum(rows for _, _, rows in self.groups[0])
        self.width = self.pieces[0].shape[1]

    def operands(self):
        return [pltpu.with_memory_space_constraint(piece, pltpu.VMEM) for piece in self.pieces]

    def block(self, refs, index, part, size):
        found, begin = [], 0
        for which, start, rows in self.groups[index]:
            low, high = max(part, begin), min(part + size, begin + rows)
            if low < high:
                found.append(refs[which][start + low - begin : start + high - begin, :])
            begin += rows
        return found[0] if len(found) == 1 else jnp.concatenate(found, axis=0)

    def product(self, x_ref, skip, refs, span):
        total = None
        joint = max(1, min(len(self.groups), 4))
        for index in range(0, len(self.groups), joint):
            groups = self.groups[index : index + joint]
            found = [refs[which][start : start + rows, span] for group in groups for which, start, rows in group]
            block = found[0] if len(found) == 1 else jnp.concatenate(found, axis=0)
            start = skip + index * self.depth
            term = dot(x_ref[:, start : start + len(groups) * self.depth], block)
            total = term if total is None else total + term
        return total


def near(value):
    return pltpu.with_memory_space_constraint(value, pltpu.VMEM)


VMEM_SPEC = pl.BlockSpec(memory_space=pltpu.VMEM)
SMEM_SPEC = pl.BlockSpec(memory_space=pltpu.SMEM)


def norm_call(where, x, g, gain, depth):
    rows, width = x.shape

    def kernel(where_ref, x_ref, g_ref, gain_ref, normed_ref, grads_ref, hold):
        def rows_body(span):
            x = x_ref[span, :].astype(F32)
            scale = lax.rsqrt(jnp.mean(x * x, axis=-1, keepdims=True) + EPSILON)
            hold[span, :] = (x * scale * gain_ref[...]).astype(BF16)

        tiles(rows, min(32, rows), rows_body)
        order = place(rows)
        for index in range(width // depth):
            source = pl.ds(pl.multiple_of((where_ref[0] ^ index) * depth, depth), depth)
            normed_ref[:, index * depth : (index + 1) * depth] = dot(order, hold[:, source]).astype(BF16)

        def grads_body(span):
            grads_ref[span, :] = dot(order, g_ref[:, span]).T.astype(BF16)

        tiles(width, min(512, width), grads_body)

    return pl.pallas_call(
        kernel,
        out_shape=[jax.ShapeDtypeStruct((rows, width), BF16), jax.ShapeDtypeStruct((width, rows), BF16)],
        in_specs=[SMEM_SPEC] + [VMEM_SPEC] * 3,
        out_specs=[VMEM_SPEC] * 2,
        scratch_shapes=[pltpu.VMEM(x.shape, BF16)],
        compiler_params=params(14),
        cost_estimate=cost(4 * rows * x.size, 8 * x.size),
        name="norm_rows",
    )(where, near(x), near(g), near(gain))


def project_call(x, shards, tile, dtype, skip=0):
    rows, width = x.shape[0], shards.width
    count, depth = len(shards.groups), shards.depth

    def kernel(x_ref, *refs):
        refs, out_ref = refs[:-1], refs[-1]

        def body(span):
            out_ref[:, span] = shards.product(x_ref, skip, refs, span).astype(dtype)

        tiles(width, tile, body)

    return pl.pallas_call(
        kernel,
        out_shape=jax.ShapeDtypeStruct((rows, width), dtype),
        in_specs=[VMEM_SPEC] + [VMEM_SPEC] * len(shards.pieces),
        out_specs=VMEM_SPEC,
        compiler_params=params(14),
        cost_estimate=cost(2 * rows * count * depth * width, 2 * count * depth * width),
        name="project",
    )(near(x), *shards.operands())


def back_call(where, grads, shards):
    width, rows = grads.shape
    count, depth = len(shards.groups), shards.depth

    def kernel(where_ref, g_ref, *refs):
        refs, out_ref = refs[:-1], refs[-1]
        size = min(depth, 256)
        for index in range(count):
            for part in range(0, depth, size):
                target = pl.multiple_of((where_ref[0] ^ index) * depth + part, size)
                term = dot(shards.block(refs, index, part, size), g_ref[...])
                out_ref[:, pl.ds(target, size)] = term.T.astype(BF16)

    return pl.pallas_call(
        kernel,
        out_shape=jax.ShapeDtypeStruct((rows, count * depth), BF16),
        in_specs=[SMEM_SPEC, VMEM_SPEC] + [VMEM_SPEC] * len(shards.pieces),
        out_specs=VMEM_SPEC,
        compiler_params=params(14),
        cost_estimate=cost(2 * rows * count * depth * width, 2 * count * depth * width),
        name="back_rows",
    )(where, near(grads), *shards.operands())


def gates(x):
    under = 1.0 + jnp.minimum(jnp.exp(-x), LARGE)
    rough = pl.reciprocal(under, approx=True)
    update = rough * (2.0 - under * rough)
    return update, 1.0 - update


def slab_pair(ref, pair, span):
    return split(ref[pair * 2 * SEGMENTS : (pair + 1) * 2 * SEGMENTS, span])


def split(both):
    both = both.astype(F32)
    return both[:SEGMENTS], both[SEGMENTS:]


def chosen_pair(where_ref, first_ref, second_ref, pair, span):
    here = slice(pair * 2 * SEGMENTS, (pair + 1) * 2 * SEGMENTS)
    gate, cand = choose(where_ref, first_ref[here, span], second_ref[here, span])
    return split(gate), split(cand)


def choose(where_ref, one, other):
    straight = where_ref[1] == 0
    return jnp.where(straight, one, other), jnp.where(straight, other, one)


def totals_call(where, x, partial, shards, skip, first_pre, back, both, block, tile):
    rows, width = first_pre.shape
    pairs = rows // (2 * SEGMENTS)
    count, depth = len(shards.groups), shards.depth
    extra = [] if partial is None else [partial]

    def kernel(where_ref, x_ref, first_ref, back_ref, both_ref, *refs):
        partial_refs, refs = refs[: len(extra)], refs[len(extra) :]
        refs, (second_ref, parts_ref, whole_ref, rows_ref) = refs[:-4], refs[-4:]
        for index in range(width // block):
            target = pl.multiple_of((where_ref[0] ^ index) * block, block)
            rows_ref[:, pl.ds(target, block)] = both_ref[:, index * block : (index + 1) * block]

        def body(span):
            total = shards.product(x_ref, skip, refs, span)
            for ref in partial_refs:
                total = total + ref[:, span]
            second_ref[:, span] = total.astype(BF16)
            bias = rows_ref[0:1, span]
            keep = jnp.ones((SEGMENTS, tile), F32)
            state = leaving = slope_run = slopes = updates = crossed = jnp.zeros((SEGMENTS, tile), F32)
            for pair in range(pairs):
                slabs = chosen_pair(where_ref, first_ref, second_ref, pair, span)
                for gate, cand, g in zip(*slabs, slab_pair(back_ref, pair, span)):
                    update, retain = gates(gate + bias)
                    slope = (cand - state) * update * retain
                    keep = keep * retain
                    state = retain * state + update * cand
                    kept_grad = keep * g
                    leaving = leaving + kept_grad
                    slope_run = retain * slope_run + slope
                    slopes = slopes + g * slope_run
                    updates = updates + update
                    crossed = crossed + kept_grad * updates
            parts_ref[0, :, span], parts_ref[1, :, span], parts_ref[2, :, span] = keep, state, leaving
            both_sides = keep * updates
            row = lambda value, s: value[s : s + 1]
            zero, one = row(keep, 0) * 0.0, row(keep, 0) * 0.0 + 1.0
            start, start_slope = [zero], [one]
            for s in range(SEGMENTS):
                start.append(row(keep, s) * start[-1] + row(state, s))
                start_slope.append(row(keep, s) * start_slope[-1])
            tail, tail_slope = [zero], [one]
            for s in range(SEGMENTS - 1, -1, -1):
                tail.append(row(keep, s) * tail[-1] + row(leaving, s))
                tail_slope.append(row(keep, s) * tail_slope[-1])
            whole = [start_slope[-1], start[-1], tail[-1]]
            start, start_slope = jnp.concatenate(start[:-1], axis=0), jnp.concatenate(start_slope[:-1], axis=0)
            tail = jnp.concatenate(tail[-2::-1], axis=0)
            tail_slope = jnp.concatenate(tail_slope[-2::-1], axis=0)
            by_tail = slope_run - both_sides * start
            by_start = crossed + both_sides * tail
            sums = [
                slopes + slope_run * tail - by_start * start,
                by_tail * tail_slope,
                by_start * start_slope,
                both_sides * tail_slope * start_slope,
            ]
            whole += [jnp.sum(value, axis=0, keepdims=True) for value in sums] + [zero]
            whole_ref[:, span] = jnp.concatenate(whole, axis=0)

        tiles(width, tile, body)

    return pl.pallas_call(
        kernel,
        out_shape=[
            jax.ShapeDtypeStruct((rows, width), BF16),
            jax.ShapeDtypeStruct((3, SEGMENTS, width), F32),
            jax.ShapeDtypeStruct((8, width), F32),
            jax.ShapeDtypeStruct((2, width), F32),
        ],
        in_specs=[SMEM_SPEC] + [VMEM_SPEC] * (4 + len(extra)) + [VMEM_SPEC] * len(shards.pieces),
        out_specs=[VMEM_SPEC] * 4,
        compiler_params=params(14),
        cost_estimate=cost(2 * rows * count * depth * width, 2 * count * depth * width),
        name="project_totals",
    )(where, *map(near, (x, first_pre, back, both, *extra)), *shards.operands())


def scan_call(where, first_pre, second_pre, back, both, parts, wholes, offsets, ranks, tile):
    rows, width = first_pre.shape
    pairs = rows // (2 * SEGMENTS)

    def kernel(where_ref, first_ref, second_ref, back_ref, both_ref, parts_ref, *refs):
        whole_refs, refs = refs[: len(wholes)], refs[len(wholes) :]
        (state_ref, one_ref, other_ref, bias_grad_ref, state_grad_ref) = refs[:5]
        hold, kept, updates, slopes, one_hold, other_hold, state_hold = refs[5:]
        me = where_ref[2]
        order, order_back = place_back(rows), place(rows)

        def body(span):
            for ref, members in zip(whole_refs, offsets):
                for member, offset in enumerate(members):
                    hold[where_ref[0] ^ offset] = ref[member, :, span]
            blocks = [hold[rank] for rank in range(ranks)]
            held = both_ref[1:2, span]
            entering, held_by = held, []
            for rank in range(ranks):
                block = blocks[rank]
                entering = jnp.where(rank == me, held, entering)
                held_by.append(held)
                held = block[0:1] * held + block[1:2]
            arriving = state_grad = bias_sum = held * 0.0
            for rank in range(ranks - 1, -1, -1):
                block, held = blocks[rank], held_by[rank]
                arriving = jnp.where(rank == me, state_grad, arriving)
                by_tail = block[4:5] - block[6:7] * held
                bias_sum = bias_sum + block[3:4] - block[5:6] * held + by_tail * state_grad
                state_grad = block[0:1] * state_grad + block[2:3]
            state_grad_ref[:, span] = state_grad
            bias_grad_ref[:, span] = bias_sum
            keep, ends, leaves = parts_ref[0, :, span], parts_ref[1, :, span], parts_ref[2, :, span]
            starts = [entering]
            for s in range(SEGMENTS - 1):
                starts.append(keep[s : s + 1] * starts[-1] + ends[s : s + 1])
            tails = [arriving]
            for s in range(SEGMENTS - 1, 0, -1):
                tails.append(keep[s : s + 1] * tails[-1] + leaves[s : s + 1])
            state = jnp.concatenate(starts, axis=0)
            leaving = jnp.concatenate(tails[::-1], axis=0)
            bias = both_ref[0:1, span]

            for pair in range(pairs):
                states, retains, ups, slope = [], [], [], []
                for gate, cand in zip(*chosen_pair(where_ref, first_ref, second_ref, pair, span)):
                    update, retain = gates(gate + bias)
                    retains.append(retain)
                    ups.append(update)
                    slope.append((cand - state) * update * retain)
                    state = retain * state + update * cand
                    states.append(state)
                here = slice(pair * 2 * SEGMENTS, (pair + 1) * 2 * SEGMENTS)
                state_hold[here, :] = jnp.concatenate(states, axis=0).astype(BF16)
                kept[here, :] = jnp.concatenate(retains, axis=0)
                updates[here, :] = jnp.concatenate(ups, axis=0)
                slopes[here, :] = jnp.concatenate(slope, axis=0)

            for pair in range(pairs - 1, -1, -1):
                here = slice(pair * 2 * SEGMENTS, (pair + 1) * 2 * SEGMENTS)
                grads = slab_pair(back_ref, pair, span)
                retain, update, slope = kept[here, :], updates[here, :], slopes[here, :]
                late = grads[1] + leaving
                early = grads[0] + retain[SEGMENTS:] * late
                leaving = retain[:SEGMENTS] * early
                carried = jnp.concatenate([early, late], axis=0)
                gate_grad = carried * slope
                cand_grad = carried * update
                one, other = choose(where_ref, gate_grad.astype(BF16), cand_grad.astype(BF16))
                one_hold[here, :] = one
                other_hold[here, :] = other
            state_ref[:, span] = dot(order, state_hold[...]).astype(BF16)
            one_ref[span, :] = dot(one_hold[...].T, order_back).astype(BF16)
            other_ref[span, :] = dot(other_hold[...].T, order_back).astype(BF16)

        tiles(width, tile, body)

    wide = jax.ShapeDtypeStruct((rows, width), BF16)
    tall = jax.ShapeDtypeStruct((width, rows), BF16)
    flat = jax.ShapeDtypeStruct((1, width), F32)
    return pl.pallas_call(
        kernel,
        out_shape=[wide, tall, tall, flat, flat],
        in_specs=[SMEM_SPEC] + [VMEM_SPEC] * (5 + len(wholes)),
        out_specs=[VMEM_SPEC] * 5,
        scratch_shapes=[pltpu.VMEM((ranks, SEGMENTS, tile), F32)]
        + [pltpu.VMEM((rows, tile), F32)] * 3
        + [pltpu.VMEM((rows, tile), BF16)] * 3,
        compiler_params=params(14),
        cost_estimate=cost(6 * rows * rows * width, 12 * rows * width),
        name="scan_rows",
    )(where, *map(near, (first_pre, second_pre, back, both, parts, *wholes)))


def layer_call(where, state_rows, residual, shards, tile):
    rows, width = residual.shape
    count, depth = len(shards.groups), shards.depth

    def kernel(where_ref, x_ref, residual_ref, *refs):
        refs, (out_ref, ordered) = refs[:-2], refs[-2:]
        for index in range(count):
            source = pl.ds(pl.multiple_of((where_ref[0] ^ index) * depth, depth), depth)
            ordered[:, index * depth : (index + 1) * depth] = x_ref[:, source]

        def body(span):
            total = shards.product(ordered, 0, refs, span)
            out_ref[:, span] = (residual_ref[:, span].astype(F32) + total).astype(BF16)

        tiles(width, tile, body)

    return pl.pallas_call(
        kernel,
        out_shape=jax.ShapeDtypeStruct((rows, width), BF16),
        in_specs=[SMEM_SPEC] + [VMEM_SPEC] * 2 + [VMEM_SPEC] * len(shards.pieces),
        out_specs=VMEM_SPEC,
        scratch_shapes=[pltpu.VMEM((rows, count * depth), BF16)],
        compiler_params=params(14),
        cost_estimate=cost(2 * rows * count * depth * width, 2 * count * depth * width),
        name="layer_rows",
    )(where, near(state_rows), near(residual), *shards.operands())


def input_grad_call(where, one, other, first, second, x, grads, gain):
    rows, width = x.shape
    hidden = one.shape[0]
    count, depth = len(first.groups), first.depth

    def kernel(where_ref, one_ref, other_ref, x_ref, grads_ref, gain_ref, *refs):
        first_refs = refs[: len(first.pieces)]
        second_refs = refs[len(first.pieces) : len(first.pieces) + len(second.pieces)]
        out_ref, total = refs[-2:]
        size = min(depth, 256)
        for index in range(count):
            for part in range(0, depth, size):
                target = pl.multiple_of((where_ref[0] ^ index) * depth + part, size)
                term = dot(first.block(first_refs, index, part, size), one_ref[...])
                term = term + dot(second.block(second_refs, index, part, size), other_ref[...])
                total[:, pl.ds(target, size)] = term.T

        def body(span):
            x = x_ref[span, :].astype(F32)
            scale = lax.rsqrt(jnp.mean(x * x, axis=-1, keepdims=True) + EPSILON)
            unit = x * scale
            unit_grad = total[span, :] * gain_ref[...]
            along = jnp.mean(unit_grad * unit, axis=-1, keepdims=True)
            out = grads_ref[span, :].astype(F32) + scale * (unit_grad - unit * along)
            out_ref[span, :] = out.astype(BF16)

        tiles(rows, min(32, rows), body)

    return pl.pallas_call(
        kernel,
        out_shape=jax.ShapeDtypeStruct((rows, width), BF16),
        in_specs=[SMEM_SPEC] + [VMEM_SPEC] * 5 + [VMEM_SPEC] * (len(first.pieces) + len(second.pieces)),
        out_specs=VMEM_SPEC,
        scratch_shapes=[pltpu.VMEM((rows, width), F32)],
        compiler_params=params(14),
        cost_estimate=cost(4 * one.size * width, 4 * hidden * width),
        name="input_grad_rows",
    )(where, *map(near, (one, other, x, grads, gain)), *first.operands(), *second.operands())


def close_call(where, state_grad, rows, block):
    def kernel(where_ref, state_ref, *refs):
        refs, (state_out_ref, bias_out_ref) = refs[:-2], refs[-2:]
        here = pl.ds(pl.multiple_of(where_ref[2] * block, block), block)
        state_out_ref[...] = state_ref[:, here]
        bias_out_ref[...] = sum((ref[:, here] for ref in refs[1:]), refs[0][:, here])

    return pl.pallas_call(
        kernel,
        out_shape=[jax.ShapeDtypeStruct((1, block), F32)] * 2,
        in_specs=[SMEM_SPEC] + [VMEM_SPEC] * (1 + len(rows)),
        out_specs=[VMEM_SPEC] * 2,
        compiler_params=params(2),
        cost_estimate=cost(1, 4 * state_grad.size),
        name="close_rows",
    )(where, state_grad, *rows)


def front_on_cube(ranks, batches, where, turned, tile, rows_in, grad_rows, gain, gate_bias, state_in, w_gate, w_cand, w_out):
    half = w_gate.shape[0] // 2
    depth = w_gate.shape[0]
    halves = lambda w: (w[:half], w[half:])
    straight = turned == 0
    send = lambda value, offset: hop(value, offset, ranks)
    core = lambda value: hop(value, 1, ranks)
    over = lambda value: swap_batch(value, 1, batches)
    f_a = jnp.where(straight, w_gate[:half], w_cand[:half])
    f_a, where, w_gate, w_cand, own_t = after((f_a, where, w_gate, w_cand, w_out))
    own_f = [f_a, jnp.where(straight, w_gate[half:], w_cand[half:])]
    stack = lambda *parts: jnp.concatenate(parts, axis=0)
    cut = lambda held, *starts: [(held, start * half, half) for start in starts]
    f2a, f4a = send(own_f[0], 2), send(own_f[0], 4)
    f1 = [core(v) for v in own_f]
    both = jnp.stack([gate_bias, state_in[0]])
    both = jnp.concatenate([both, core(both)], axis=1)
    both = jnp.concatenate([both, send(both, 2)], axis=1)
    normed, grads = norm_call(where, rows_in, grad_rows, gain, depth)
    own_s = jnp.where(straight, w_cand, w_gate)
    t_a, t_b = halves(own_t)
    f2a, f4a, f1a, f1b, both, normed, grads, f_b, own_s, own_t, t_a, t_b = after(
        (f2a, f4a, f1[0], f1[1], both, normed, grads, own_f[1], own_s, own_t, t_a, t_b)
    )
    f2b, f4b = send(f_b, 2), send(f_b, 4)
    t2a, t4a = send(t_a, 2), send(t_a, 4)
    sa = over(stack(f2a, f4a))
    f2b, f4b, f3a, f5a = after((f2b, f4b, f2a, f4a))
    f3a, f5a = core(f3a), core(f5a)
    f2b, f4b, f_b2, sa, t2a, t4a, f3a, f5a, t_b, f2a = after(
        (f2b, f4b, stack(f2b, f4b), sa, t2a, t4a, f3a, f5a, t_b, f2a)
    )
    f6a, f6b = send(f2a, 4), send(f4b, 2)
    t2b, t4b = send(t_b, 2), send(t_b, 4)
    sb = over(f_b2)
    f6a, f6b, f3b, f5b, t3a, t5a = after((f6a, f6b, f2b, f4b, t2a, t4a))
    f3b, f5b, t3a, t5a = core(f3b), core(f5b), core(t3a), core(t5a)
    both, f6a, f6b, sb, t2b, t4b, f3b, f5b, t3a, t5a, sa, t2a = after(
        (both, f6a, f6b, sb, t2b, t4b, f3b, f5b, t3a, t5a, sa, t2a)
    )
    t6a, t6b = send(t2a, 4), send(t4b, 2)
    s6a = over(f6a)
    f7, cs = core(stack(f6a, f6b)), core(stack(sa, sb, own_s))
    first = Shards([own_f, [f1a, f1b], [f2a, f2b], [f3a, f3b], [f4a, f4b], [f5a, f5b], [f6a, f6b], [f7]])
    pairs = lambda one, two, row: cut(one, row) + cut(two, row)
    most = [[own_s], cut(cs, 4, 5), pairs(sa, sb, 0), cut(cs, 0, 2), pairs(sa, sb, 1), cut(cs, 1, 3)]
    first_pre = project_call(normed, first, tile, BF16)
    partial = project_call(normed, Shards(most), tile, F32)
    t6a, t6b, s6a, sb_out, first_pre, partial, own_t, both = after(
        (t6a, t6b, s6a, sb, first_pre, partial, own_t, both)
    )
    quarter = half // 2
    s6b = [send(sb_out[half : half + quarter], 2), send(sb_out[quarter:half], 4)]
    s7a = core(s6a)
    c4 = core(stack(t6a, t6b, t2b, t4b, own_t))
    third = Shards(
        [[own_t], cut(c4, 4, 5), [t2a, t2b], [t3a, (c4, 2 * half, half)], [t4a, t4b], [t5a, (c4, 3 * half, half)]]
        + [[t6a, t6b], cut(c4, 0, 1)]
    )
    both = jnp.concatenate([both, send(both, 4)], axis=1)
    back = back_call(where, grads, third)
    s6b_low, s6b_high, s7a, back, both = after((*s6b, s7a, back, both))
    last = [[s6a, s6b_low, s6b_high], [s7a, core(stack(s6b_low, s6b_high))]]
    second = Shards(most + last)
    second_pre, parts, whole, both = totals_call(
        where, normed, partial, Shards(last), len(most) * depth, first_pre, back, both, depth, tile
    )
    return where, first, second, third, first_pre, second_pre, back, both, parts, whole


def front(where, tile, rows_in, grad_rows, gain, gate_bias, state_in, w_gate, w_cand, w_out):
    first, second, third = (
        Shards([[lax.all_gather(w, "seq", tiled=True)]]) for w in (w_gate, w_cand, w_out)
    )
    both = lax.all_gather(jnp.stack([gate_bias, state_in[0]]), "seq", axis=1, tiled=True)
    normed, grads = norm_call(where, rows_in, grad_rows, gain, first.depth)
    first_pre = project_call(normed, first, tile, BF16)
    back = back_call(where, grads, third)
    second_pre, parts, whole, both = totals_call(
        where, normed, None, second, 0, first_pre, back, both, first.depth, tile
    )
    return where, first, second, third, first_pre, second_pre, back, both, parts, whole


def on_device(ranks, batches, inputs, output_grad, norm_gain, gate_bias, state_in, w_gate, w_cand, w_out):
    rows_in, grad_rows = inputs[0], output_grad[0]
    gain = norm_gain[None, :]
    hidden = w_gate.shape[1]
    tile = min(512, hidden)
    me = lax.axis_index("seq")
    given = (rows_in, grad_rows, gain, gate_bias, state_in, w_gate, w_cand, w_out)
    cube = ranks == 8 and batches in (2, 4, 8)
    if cube:
        turned = lax.axis_index("batch") % 2
        where = jnp.stack([me, turned, me]).astype(jnp.int32)
        found = front_on_cube(ranks, batches, where, turned, tile, *given)
    else:
        nought = jnp.zeros_like(me)
        where = jnp.stack([nought, nought, me]).astype(jnp.int32)
        found = front(where, tile, *given)
    where, first, second, third, first_pre, second_pre, back, both, parts, whole = found
    if cube:
        found = jnp.stack([hop(whole, offset, ranks) for offset in (2, 4, 6)])
        wholes = [jnp.stack([whole, hop(whole, 1, ranks)]), found, hop(found, 1, ranks)]
        offsets = [(0, 1), (2, 4, 6), (3, 5, 7)]
    else:
        wholes, offsets = [lax.all_gather(whole, "seq")], [range(ranks)]
    state_rows, one, other, bias_part, state_grad = scan_call(
        where, first_pre, second_pre, back, both, parts, wholes, offsets, ranks, tile
    )
    width = hidden // ranks
    if cube:
        came = swap_batch(bias_part, 1, batches)
        layer_out = layer_call(where, state_rows, rows_in, third, tile)
        layer_out, bias_part, came, one, other = after((layer_out, bias_part, came, one, other))
        for offset in range(1, batches.bit_length() - 1):
            bias_part = bias_part + came
            came = swap_batch(bias_part, 1 << offset, batches)
        input_grad = input_grad_call(where, one, other, first, second, rows_in, grad_rows, gain)
        state_out, bias_grad = close_call(where, state_grad, [bias_part, came], width)
        bias_grad = bias_grad[0]
    else:
        own_block = lax.dynamic_slice_in_dim(bias_part[0], me * width, width, 0)
        bias_grad = lax.psum(own_block, "batch")
        layer_out = layer_call(where, state_rows, rows_in, third, tile)
        input_grad = input_grad_call(where, one, other, first, second, rows_in, grad_rows, gain)
        state_out = lax.dynamic_slice_in_dim(state_grad, me * width, width, 1)
    return (layer_out[None], input_grad[None], state_out, bias_grad)


def solution(mesh):
    body = functools.partial(on_device, mesh.shape["seq"], mesh.shape["batch"])
    rows = P("batch", "seq", None)
    return jax.shard_map(
        body,
        mesh=mesh,
        in_specs=(rows, rows, P(), P("seq"), P("batch", "seq"), P("seq", None), P("seq", None), P("seq", None)),
        out_specs=(rows, rows, P("batch", "seq"), P("seq")),
        check_vma=False,
    )
```

```python
import functools

import jax
import jax.numpy as jnp
from jax import lax
from jax.experimental import pallas as pl
from jax.experimental.pallas import tpu as pltpu
from jax.sharding import PartitionSpec as P

EPSILON = 1e-06
SEGMENTS = 8
LARGE = 1e37
F32 = jnp.float32
BF16 = jnp.bfloat16


def params(mebibytes):
    return pltpu.CompilerParams(vmem_limit_bytes=mebibytes * 1024 * 1024)


def cost(flops, moved):
    return pl.CostEstimate(flops=int(flops), bytes_accessed=int(moved), transcendentals=0)


def hop(value, offset, count):
    return lax.ppermute(value, "seq", [(i, i ^ offset) for i in range(count)])


def swap_batch(value, offset, count):
    return lax.ppermute(value, "batch", [(i, i ^ offset) for i in range(count)])


def after(values, *earlier):
    return lax.optimization_barrier(tuple(values) + tuple(earlier))[: len(values)]


def place(rows):
    steps = rows // SEGMENTS
    out = lax.broadcasted_iota(jnp.int32, (rows, rows), 0)
    inn = lax.broadcasted_iota(jnp.int32, (rows, rows), 1)
    source = lax.rem(out, SEGMENTS) * steps + lax.div(out, SEGMENTS)
    return (source == inn).astype(F32).astype(BF16)


def place_back(rows):
    steps = rows // SEGMENTS
    out = lax.broadcasted_iota(jnp.int32, (rows, rows), 0)
    inn = lax.broadcasted_iota(jnp.int32, (rows, rows), 1)
    source = lax.rem(out, steps) * SEGMENTS + lax.div(out, steps)
    return (source == inn).astype(F32).astype(BF16)


def dot(a, b):
    return lax.dot_general(a, b, (((1,), (0,)), ((), ())), preferred_element_type=F32)


def tiles(count, tile, body):
    @pl.loop(0, count // tile)
    def _(index):
        body(pl.ds(pl.multiple_of(index * tile, tile), tile))


class Shards:
    def __init__(self, groups):
        self.pieces, self.groups = [], []
        for group in groups:
            made = []
            for piece in group:
                array, start, rows = piece if isinstance(piece, tuple) else (piece, 0, piece.shape[0])
                known = [index for index, other in enumerate(self.pieces) if other is array]
                if not known:
                    known = [len(self.pieces)]
                    self.pieces.append(array)
                made.append((known[0], start, rows))
            self.groups.append(made)
        self.depth = sum(rows for _, _, rows in self.groups[0])
        self.width = self.pieces[0].shape[1]

    def operands(self):
        return [pltpu.with_memory_space_constraint(piece, pltpu.VMEM) for piece in self.pieces]

    def block(self, refs, index, part, size):
        found, begin = [], 0
        for which, start, rows in self.groups[index]:
            low, high = max(part, begin), min(part + size, begin + rows)
            if low < high:
                found.append(refs[which][start + low - begin : start + high - begin, :])
            begin += rows
        return found[0] if len(found) == 1 else jnp.concatenate(found, axis=0)

    def product(self, x_ref, skip, refs, span):
        total = None
        joint = max(1, min(len(self.groups), 4))
        for index in range(0, len(self.groups), joint):
            groups = self.groups[index : index + joint]
            found = [refs[which][start : start + rows, span] for group in groups for which, start, rows in group]
            block = found[0] if len(found) == 1 else jnp.concatenate(found, axis=0)
            start = skip + index * self.depth
            term = dot(x_ref[:, start : start + len(groups) * self.depth], block)
            total = term if total is None else total + term
        return total


def near(value):
    return pltpu.with_memory_space_constraint(value, pltpu.VMEM)


VMEM_SPEC = pl.BlockSpec(memory_space=pltpu.VMEM)
SMEM_SPEC = pl.BlockSpec(memory_space=pltpu.SMEM)


def norm_call(where, x, g, gain, depth):
    rows, width = x.shape

    def kernel(where_ref, x_ref, g_ref, gain_ref, normed_ref, grads_ref, hold):
        def rows_body(span):
            x = x_ref[span, :].astype(F32)
            scale = lax.rsqrt(jnp.mean(x * x, axis=-1, keepdims=True) + EPSILON)
            hold[span, :] = (x * scale * gain_ref[...]).astype(BF16)

        tiles(rows, min(32, rows), rows_body)
        order = place(rows)
        for index in range(width // depth):
            source = pl.ds(pl.multiple_of((where_ref[0] ^ index) * depth, depth), depth)
            normed_ref[:, index * depth : (index + 1) * depth] = dot(order, hold[:, source]).astype(BF16)

        def grads_body(span):
            grads_ref[span, :] = dot(order, g_ref[:, span]).T.astype(BF16)

        tiles(width, min(512, width), grads_body)

    return pl.pallas_call(
        kernel,
        out_shape=[jax.ShapeDtypeStruct((rows, width), BF16), jax.ShapeDtypeStruct((width, rows), BF16)],
        in_specs=[SMEM_SPEC] + [VMEM_SPEC] * 3,
        out_specs=[VMEM_SPEC] * 2,
        scratch_shapes=[pltpu.VMEM(x.shape, BF16)],
        compiler_params=params(14),
        cost_estimate=cost(4 * rows * x.size, 8 * x.size),
        name="norm_rows",
    )(where, near(x), near(g), near(gain))


def project_call(x, shards, tile, dtype, skip=0):
    rows, width = x.shape[0], shards.width
    count, depth = len(shards.groups), shards.depth

    def kernel(x_ref, *refs):
        refs, out_ref = refs[:-1], refs[-1]

        def body(span):
            out_ref[:, span] = shards.product(x_ref, skip, refs, span).astype(dtype)

        tiles(width, tile, body)

    return pl.pallas_call(
        kernel,
        out_shape=jax.ShapeDtypeStruct((rows, width), dtype),
        in_specs=[VMEM_SPEC] + [VMEM_SPEC] * len(shards.pieces),
        out_specs=VMEM_SPEC,
        compiler_params=params(14),
        cost_estimate=cost(2 * rows * count * depth * width, 2 * count * depth * width),
        name="project",
    )(near(x), *shards.operands())


def back_call(where, grads, shards):
    width, rows = grads.shape
    count, depth = len(shards.groups), shards.depth

    def kernel(where_ref, g_ref, *refs):
        refs, out_ref = refs[:-1], refs[-1]
        size = min(depth, 256)
        for index in range(count):
            for part in range(0, depth, size):
                target = pl.multiple_of((where_ref[0] ^ index) * depth + part, size)
                term = dot(shards.block(refs, index, part, size), g_ref[...])
                out_ref[:, pl.ds(target, size)] = term.T.astype(BF16)

    return pl.pallas_call(
        kernel,
        out_shape=jax.ShapeDtypeStruct((rows, count * depth), BF16),
        in_specs=[SMEM_SPEC, VMEM_SPEC] + [VMEM_SPEC] * len(shards.pieces),
        out_specs=VMEM_SPEC,
        compiler_params=params(14),
        cost_estimate=cost(2 * rows * count * depth * width, 2 * count * depth * width),
        name="back_rows",
    )(where, near(grads), *shards.operands())


def gates(x):
    under = 1.0 + jnp.minimum(jnp.exp(-x), LARGE)
    rough = pl.reciprocal(under, approx=True)
    update = rough * (2.0 - under * rough)
    return update, 1.0 - update


def slab_pair(ref, pair, span):
    return split(ref[pair * 2 * SEGMENTS : (pair + 1) * 2 * SEGMENTS, span])


def split(both):
    both = both.astype(F32)
    return both[:SEGMENTS], both[SEGMENTS:]


def chosen_pair(where_ref, first_ref, second_ref, pair, span):
    here = slice(pair * 2 * SEGMENTS, (pair + 1) * 2 * SEGMENTS)
    gate, cand = choose(where_ref, first_ref[here, span], second_ref[here, span])
    return split(gate), split(cand)


def choose(where_ref, one, other):
    straight = where_ref[1] == 0
    return jnp.where(straight, one, other), jnp.where(straight, other, one)


def totals_call(where, x, partial, shards, skip, first_pre, back, both, block, tile):
    rows, width = first_pre.shape
    pairs = rows // (2 * SEGMENTS)
    count, depth = len(shards.groups), shards.depth
    extra = [] if partial is None else [partial]

    def kernel(where_ref, x_ref, first_ref, back_ref, both_ref, *refs):
        partial_refs, refs = refs[: len(extra)], refs[len(extra) :]
        refs, (second_ref, parts_ref, whole_ref, rows_ref) = refs[:-4], refs[-4:]
        for index in range(width // block):
            target = pl.multiple_of((where_ref[0] ^ index) * block, block)
            rows_ref[:, pl.ds(target, block)] = both_ref[:, index * block : (index + 1) * block]

        def body(span):
            total = shards.product(x_ref, skip, refs, span)
            for ref in partial_refs:
                total = total + ref[:, span]
            second_ref[:, span] = total.astype(BF16)
            bias = rows_ref[0:1, span]
            keep = jnp.ones((SEGMENTS, tile), F32)
            state = leaving = slope_run = slopes = updates = crossed = jnp.zeros((SEGMENTS, tile), F32)
            for pair in range(pairs):
                slabs = chosen_pair(where_ref, first_ref, second_ref, pair, span)
                for gate, cand, g in zip(*slabs, slab_pair(back_ref, pair, span)):
                    update, retain = gates(gate + bias)
                    slope = (cand - state) * update * retain
                    keep = keep * retain
                    state = retain * state + update * cand
                    kept_grad = keep * g
                    leaving = leaving + kept_grad
                    slope_run = retain * slope_run + slope
                    slopes = slopes + g * slope_run
                    updates = updates + update
                    crossed = crossed + kept_grad * updates
            parts_ref[0, :, span], parts_ref[1, :, span], parts_ref[2, :, span] = keep, state, leaving
            both_sides = keep * updates
            row = lambda value, s: value[s : s + 1]
            zero, one = row(keep, 0) * 0.0, row(keep, 0) * 0.0 + 1.0
            start, start_slope = [zero], [one]
            for s in range(SEGMENTS):
                start.append(row(keep, s) * start[-1] + row(state, s))
                start_slope.append(row(keep, s) * start_slope[-1])
            tail, tail_slope = [zero], [one]
            for s in range(SEGMENTS - 1, -1, -1):
                tail.append(row(keep, s) * tail[-1] + row(leaving, s))
                tail_slope.append(row(keep, s) * tail_slope[-1])
            whole = [start_slope[-1], start[-1], tail[-1]]
            start, start_slope = jnp.concatenate(start[:-1], axis=0), jnp.concatenate(start_slope[:-1], axis=0)
            tail = jnp.concatenate(tail[-2::-1], axis=0)
            tail_slope = jnp.concatenate(tail_slope[-2::-1], axis=0)
            by_tail = slope_run - both_sides * start
            by_start = crossed + both_sides * tail
            sums = [
                slopes + slope_run * tail - by_start * start,
                by_tail * tail_slope,
                by_start * start_slope,
                both_sides * tail_slope * start_slope,
            ]
            whole += [jnp.sum(value, axis=0, keepdims=True) for value in sums] + [zero]
            whole_ref[:, span] = jnp.concatenate(whole, axis=0)

        tiles(width, tile, body)

    return pl.pallas_call(
        kernel,
        out_shape=[
            jax.ShapeDtypeStruct((rows, width), BF16),
            jax.ShapeDtypeStruct((3, SEGMENTS, width), F32),
            jax.ShapeDtypeStruct((8, width), F32),
            jax.ShapeDtypeStruct((2, width), F32),
        ],
        in_specs=[SMEM_SPEC] + [VMEM_SPEC] * (4 + len(extra)) + [VMEM_SPEC] * len(shards.pieces),
        out_specs=[VMEM_SPEC] * 4,
        compiler_params=params(14),
        cost_estimate=cost(2 * rows * count * depth * width, 2 * count * depth * width),
        name="project_totals",
    )(where, *map(near, (x, first_pre, back, both, *extra)), *shards.operands())


def scan_call(where, first_pre, second_pre, back, both, parts, wholes, offsets, ranks, shard, tile):
    rows, width = first_pre.shape
    pairs = rows // (2 * SEGMENTS)

    def kernel(where_ref, first_ref, second_ref, back_ref, both_ref, parts_ref, *refs):
        whole_refs, refs = refs[: len(wholes)], refs[len(wholes) :]
        (state_ref, one_ref, other_ref, bias_grad_ref, state_grad_ref) = refs[:5]
        hold, kept, updates, slopes, one_hold, other_hold, state_hold = refs[5:]
        me = where_ref[2]
        order, order_back = place_back(rows), place(rows)

        def body(span):
            for ref, members in zip(whole_refs, offsets):
                for member, offset in enumerate(members):
                    hold[where_ref[0] ^ offset] = ref[member, :, span]
            blocks = [hold[rank] for rank in range(ranks)]
            held = both_ref[1:2, span]
            entering, held_by = held, []
            for rank in range(ranks):
                block = blocks[rank]
                entering = jnp.where(rank == me, held, entering)
                held_by.append(held)
                held = block[0:1] * held + block[1:2]
            arriving = state_grad = bias_sum = held * 0.0
            for rank in range(ranks - 1, -1, -1):
                block, held = blocks[rank], held_by[rank]
                arriving = jnp.where(rank == me, state_grad, arriving)
                by_tail = block[4:5] - block[6:7] * held
                bias_sum = bias_sum + block[3:4] - block[5:6] * held + by_tail * state_grad
                state_grad = block[0:1] * state_grad + block[2:3]
            state_grad_ref[:, span] = state_grad
            bias_grad_ref[:, span] = bias_sum
            keep, ends, leaves = parts_ref[0, :, span], parts_ref[1, :, span], parts_ref[2, :, span]
            starts = [entering]
            for s in range(SEGMENTS - 1):
                starts.append(keep[s : s + 1] * starts[-1] + ends[s : s + 1])
            tails = [arriving]
            for s in range(SEGMENTS - 1, 0, -1):
                tails.append(keep[s : s + 1] * tails[-1] + leaves[s : s + 1])
            state = jnp.concatenate(starts, axis=0)
            leaving = jnp.concatenate(tails[::-1], axis=0)
            bias = both_ref[0:1, span]

            for pair in range(pairs):
                states, retains, ups, slope = [], [], [], []
                for gate, cand in zip(*chosen_pair(where_ref, first_ref, second_ref, pair, span)):
                    update, retain = gates(gate + bias)
                    retains.append(retain)
                    ups.append(update)
                    slope.append((cand - state) * update * retain)
                    state = retain * state + update * cand
                    states.append(state)
                here = slice(pair * 2 * SEGMENTS, (pair + 1) * 2 * SEGMENTS)
                state_hold[here, :] = jnp.concatenate(states, axis=0).astype(BF16)
                kept[here, :] = jnp.concatenate(retains, axis=0)
                updates[here, :] = jnp.concatenate(ups, axis=0)
                slopes[here, :] = jnp.concatenate(slope, axis=0)

            for pair in range(pairs - 1, -1, -1):
                here = slice(pair * 2 * SEGMENTS, (pair + 1) * 2 * SEGMENTS)
                grads = slab_pair(back_ref, pair, span)
                retain, update, slope = kept[here, :], updates[here, :], slopes[here, :]
                late = grads[1] + leaving
                early = grads[0] + retain[SEGMENTS:] * late
                leaving = retain[:SEGMENTS] * early
                carried = jnp.concatenate([early, late], axis=0)
                gate_grad = carried * slope
                cand_grad = carried * update
                one, other = choose(where_ref, gate_grad.astype(BF16), cand_grad.astype(BF16))
                one_hold[here, :] = one
                other_hold[here, :] = other
            found = dot(order, state_hold[...]).astype(BF16)
            size = min(shard, tile)
            for part in range(0, tile, size):
                target = span.start + part
                if shard <= tile:
                    target = (where_ref[0] ^ lax.div(target, shard)) * shard
                state_ref[:, pl.ds(pl.multiple_of(target, size), size)] = found[:, part : part + size]
            one_ref[span, :] = dot(one_hold[...].T, order_back).astype(BF16)
            other_ref[span, :] = dot(other_hold[...].T, order_back).astype(BF16)

        tiles(width, tile, body)

    wide = jax.ShapeDtypeStruct((rows, width), BF16)
    tall = jax.ShapeDtypeStruct((width, rows), BF16)
    flat = jax.ShapeDtypeStruct((1, width), F32)
    return pl.pallas_call(
        kernel,
        out_shape=[wide, tall, tall, flat, flat],
        in_specs=[SMEM_SPEC] + [VMEM_SPEC] * (5 + len(wholes)),
        out_specs=[VMEM_SPEC] * 5,
        scratch_shapes=[pltpu.VMEM((ranks, SEGMENTS, tile), F32)]
        + [pltpu.VMEM((rows, tile), F32)] * 3
        + [pltpu.VMEM((rows, tile), BF16)] * 3,
        compiler_params=params(14),
        cost_estimate=cost(6 * rows * rows * width, 12 * rows * width),
        name="scan_rows",
    )(where, *map(near, (first_pre, second_pre, back, both, parts, *wholes)))


def layer_call(where, state_rows, residual, shards, tile):
    rows, width = residual.shape
    count, depth = len(shards.groups), shards.depth

    def kernel(where_ref, x_ref, residual_ref, *refs):
        refs, out_ref = refs[:-1], refs[-1]
        def body(span):
            total = shards.product(x_ref, 0, refs, span)
            out_ref[:, span] = (residual_ref[:, span].astype(F32) + total).astype(BF16)

        tiles(width, tile, body)

    return pl.pallas_call(
        kernel,
        out_shape=jax.ShapeDtypeStruct((rows, width), BF16),
        in_specs=[SMEM_SPEC] + [VMEM_SPEC] * 2 + [VMEM_SPEC] * len(shards.pieces),
        out_specs=VMEM_SPEC,
        compiler_params=params(14),
        cost_estimate=cost(2 * rows * count * depth * width, 2 * count * depth * width),
        name="layer_rows",
    )(where, near(state_rows), near(residual), *shards.operands())


def input_grad_call(where, one, other, first, second, x, grads, gain):
    rows, width = x.shape
    hidden = one.shape[0]
    count, depth = len(first.groups), first.depth

    def kernel(where_ref, one_ref, other_ref, x_ref, grads_ref, gain_ref, *refs):
        first_refs = refs[: len(first.pieces)]
        second_refs = refs[len(first.pieces) : len(first.pieces) + len(second.pieces)]
        out_ref, total = refs[-2:]
        size = min(depth, 256)
        for index in range(count):
            for part in range(0, depth, size):
                target = pl.multiple_of((where_ref[0] ^ index) * depth + part, size)
                term = dot(first.block(first_refs, index, part, size), one_ref[...])
                term = term + dot(second.block(second_refs, index, part, size), other_ref[...])
                total[:, pl.ds(target, size)] = term.T

        def body(span):
            x = x_ref[span, :].astype(F32)
            scale = lax.rsqrt(jnp.mean(x * x, axis=-1, keepdims=True) + EPSILON)
            unit = x * scale
            unit_grad = total[span, :] * gain_ref[...]
            along = jnp.mean(unit_grad * unit, axis=-1, keepdims=True)
            out = grads_ref[span, :].astype(F32) + scale * (unit_grad - unit * along)
            out_ref[span, :] = out.astype(BF16)

        tiles(rows, min(32, rows), body)

    return pl.pallas_call(
        kernel,
        out_shape=jax.ShapeDtypeStruct((rows, width), BF16),
        in_specs=[SMEM_SPEC] + [VMEM_SPEC] * 5 + [VMEM_SPEC] * (len(first.pieces) + len(second.pieces)),
        out_specs=VMEM_SPEC,
        scratch_shapes=[pltpu.VMEM((rows, width), F32)],
        compiler_params=params(14),
        cost_estimate=cost(4 * one.size * width, 4 * hidden * width),
        name="input_grad_rows",
    )(where, *map(near, (one, other, x, grads, gain)), *first.operands(), *second.operands())


def close_call(where, state_grad, rows, block):
    def kernel(where_ref, state_ref, *refs):
        refs, (state_out_ref, bias_out_ref) = refs[:-2], refs[-2:]
        here = pl.ds(pl.multiple_of(where_ref[2] * block, block), block)
        state_out_ref[...] = state_ref[:, here]
        bias_out_ref[...] = sum((ref[:, here] for ref in refs[1:]), refs[0][:, here])

    return pl.pallas_call(
        kernel,
        out_shape=[jax.ShapeDtypeStruct((1, block), F32)] * 2,
        in_specs=[SMEM_SPEC] + [VMEM_SPEC] * (1 + len(rows)),
        out_specs=[VMEM_SPEC] * 2,
        compiler_params=params(2),
        cost_estimate=cost(1, 4 * state_grad.size),
        name="close_rows",
    )(where, state_grad, *rows)


def front_on_cube(ranks, batches, where, turned, tile, rows_in, grad_rows, gain, gate_bias, state_in, w_gate, w_cand, w_out):
    half = w_gate.shape[0] // 2
    depth = w_gate.shape[0]
    halves = lambda w: (w[:half], w[half:])
    straight = turned == 0
    send = lambda value, offset: hop(value, offset, ranks)
    core = lambda value: hop(value, 1, ranks)
    over = lambda value: swap_batch(value, 1, batches)
    f_a = jnp.where(straight, w_gate[:half], w_cand[:half])
    f_a, where, w_gate, w_cand, own_t = after((f_a, where, w_gate, w_cand, w_out))
    own_f = [f_a, jnp.where(straight, w_gate[half:], w_cand[half:])]
    stack = lambda *parts: jnp.concatenate(parts, axis=0)
    cut = lambda held, *starts: [(held, start * half, half) for start in starts]
    f2a, f4a = send(own_f[0], 2), send(own_f[0], 4)
    f1 = [core(v) for v in own_f]
    both = jnp.stack([gate_bias, state_in[0]])
    both = jnp.concatenate([both, core(both)], axis=1)
    both = jnp.concatenate([both, send(both, 2)], axis=1)
    normed, grads = norm_call(where, rows_in, grad_rows, gain, depth)
    own_s = jnp.where(straight, w_cand, w_gate)
    t_a, t_b = halves(own_t)
    f2a, f4a, f1a, f1b, both, normed, grads, f_b, own_s, own_t, t_a, t_b = after(
        (f2a, f4a, f1[0], f1[1], both, normed, grads, own_f[1], own_s, own_t, t_a, t_b)
    )
    f2b, f4b = send(f_b, 2), send(f_b, 4)
    t2a, t4a = send(t_a, 2), send(t_a, 4)
    sa = over(stack(f2a, f4a))
    f2b, f4b, f3a, f5a = after((f2b, f4b, f2a, f4a))
    f3a, f5a = core(f3a), core(f5a)
    f2b, f4b, f_b2, sa, t2a, t4a, f3a, f5a, t_b, f2a = after(
        (f2b, f4b, stack(f2b, f4b), sa, t2a, t4a, f3a, f5a, t_b, f2a)
    )
    f6a, f6b = send(f2a, 4), send(f4b, 2)
    t2b, t4b = send(t_b, 2), send(t_b, 4)
    sb = over(f_b2)
    f6a, f6b, f3b, f5b = after((f6a, f6b, f2b, f4b))
    f3b, f5b = core(f3b), core(f5b)
    both, f6a, f6b, sb, t2b, t4b, f3b, f5b, sa, t2a = after((both, f6a, f6b, sb, t2b, t4b, f3b, f5b, sa, t2a))
    t6a, t6b = send(t2a, 4), send(t4b, 2)
    s6a = over(f6a)
    f7, cs = core(stack(f6a, f6b)), core(stack(sa, sb, own_s))
    first = Shards([own_f, [f1a, f1b], [f2a, f2b], [f3a, f3b], [f4a, f4b], [f5a, f5b], [f6a, f6b], [f7]])
    pairs = lambda one, two, row: cut(one, row) + cut(two, row)
    most = [[own_s], cut(cs, 4, 5), pairs(sa, sb, 0), cut(cs, 0, 2), pairs(sa, sb, 1), cut(cs, 1, 3)]
    first_pre = project_call(normed, first, tile, BF16)
    partial = project_call(normed, Shards(most), tile, F32)
    both = jnp.concatenate([both, send(after((both,), partial)[0], 4)], axis=1)
    t6a, t6b, s6a, sb_out, first_pre, partial, own_t, both = after(
        (t6a, t6b, s6a, sb, first_pre, partial, own_t, both)
    )
    quarter = half // 2
    s6b = [send(sb_out[half : half + quarter], 2), send(sb_out[quarter:half], 4)]
    s7a = core(s6a)
    c4 = core(stack(t6a, t6b, t2b, t4b, own_t, t2a, t4a))
    third = Shards(
        [[own_t], cut(c4, 4, 5), [t2a, t2b], cut(c4, 6, 2), [t4a, t4b], cut(c4, 7, 3)]
        + [[t6a, t6b], cut(c4, 0, 1)]
    )
    back = back_call(where, grads, third)
    s6b_low, s6b_high, s7a, back, both = after((*s6b, s7a, back, both))
    last = [[s6a, s6b_low, s6b_high], [s7a, core(stack(s6b_low, s6b_high))]]
    second = Shards(most + last)
    second_pre, parts, whole, both = totals_call(
        where, normed, partial, Shards(last), len(most) * depth, first_pre, back, both, depth, tile
    )
    return where, first, second, third, first_pre, second_pre, back, both, parts, whole


def front(where, tile, rows_in, grad_rows, gain, gate_bias, state_in, w_gate, w_cand, w_out):
    first, second, third = (
        Shards([[lax.all_gather(w, "seq", tiled=True)]]) for w in (w_gate, w_cand, w_out)
    )
    both = lax.all_gather(jnp.stack([gate_bias, state_in[0]]), "seq", axis=1, tiled=True)
    normed, grads = norm_call(where, rows_in, grad_rows, gain, first.depth)
    first_pre = project_call(normed, first, tile, BF16)
    back = back_call(where, grads, third)
    second_pre, parts, whole, both = totals_call(
        where, normed, None, second, 0, first_pre, back, both, first.depth, tile
    )
    return where, first, second, third, first_pre, second_pre, back, both, parts, whole


def on_device(ranks, batches, inputs, output_grad, norm_gain, gate_bias, state_in, w_gate, w_cand, w_out):
    rows_in, grad_rows = inputs[0], output_grad[0]
    gain = norm_gain[None, :]
    hidden = w_gate.shape[1]
    tile = min(512, hidden)
    me = lax.axis_index("seq")
    given = (rows_in, grad_rows, gain, gate_bias, state_in, w_gate, w_cand, w_out)
    cube = ranks == 8 and batches in (2, 4, 8)
    if cube:
        turned = lax.axis_index("batch") % 2
        where = jnp.stack([me, turned, me]).astype(jnp.int32)
        found = front_on_cube(ranks, batches, where, turned, tile, *given)
    else:
        nought = jnp.zeros_like(me)
        where = jnp.stack([nought, nought, me]).astype(jnp.int32)
        found = front(where, tile, *given)
    where, first, second, third, first_pre, second_pre, back, both, parts, whole = found
    if cube:
        found = jnp.stack([hop(whole, offset, ranks) for offset in (2, 4, 6)])
        wholes = [jnp.stack([whole, hop(whole, 1, ranks)]), found, hop(found, 1, ranks)]
        offsets = [(0, 1), (2, 4, 6), (3, 5, 7)]
    else:
        wholes, offsets = [lax.all_gather(whole, "seq")], [range(ranks)]
    state_rows, one, other, bias_part, state_grad = scan_call(
        where, first_pre, second_pre, back, both, parts, wholes, offsets, ranks, third.depth, tile
    )
    width = hidden // ranks
    if cube:
        came = swap_batch(bias_part, 1, batches)
        layer_out = layer_call(where, state_rows, rows_in, third, tile)
        layer_out, bias_part, came, one, other = after((layer_out, bias_part, came, one, other))
        for offset in range(1, batches.bit_length() - 1):
            bias_part = bias_part + came
            came = swap_batch(bias_part, 1 << offset, batches)
        input_grad = input_grad_call(where, one, other, first, second, rows_in, grad_rows, gain)
        state_out, bias_grad = close_call(where, state_grad, [bias_part, came], width)
        bias_grad = bias_grad[0]
    else:
        own_block = lax.dynamic_slice_in_dim(bias_part[0], me * width, width, 0)
        bias_grad = lax.psum(own_block, "batch")
        layer_out = layer_call(where, state_rows, rows_in, third, tile)
        input_grad = input_grad_call(where, one, other, first, second, rows_in, grad_rows, gain)
        state_out = lax.dynamic_slice_in_dim(state_grad, me * width, width, 1)
    return (layer_out[None], input_grad[None], state_out, bias_grad)


def solution(mesh):
    body = functools.partial(on_device, mesh.shape["seq"], mesh.shape["batch"])
    rows = P("batch", "seq", None)
    return jax.shard_map(
        body,
        mesh=mesh,
        in_specs=(rows, rows, P(), P("seq"), P("batch", "seq"), P("seq", None), P("seq", None), P("seq", None)),
        out_specs=(rows, rows, P("batch", "seq"), P("seq")),
        check_vma=False,
    )
```

```python
import functools

import jax
import jax.numpy as jnp
from jax import lax
from jax.experimental import pallas as pl
from jax.experimental.pallas import tpu as pltpu
from jax.sharding import PartitionSpec as P

EPSILON = 1e-06
SEGMENTS = 8
LARGE = 1e37
F32 = jnp.float32
BF16 = jnp.bfloat16


def params(mebibytes):
    return pltpu.CompilerParams(vmem_limit_bytes=mebibytes * 1024 * 1024)


def cost(flops, moved):
    return pl.CostEstimate(flops=int(flops), bytes_accessed=int(moved), transcendentals=0)


def hop(value, offset, count):
    return lax.ppermute(value, "seq", [(i, i ^ offset) for i in range(count)])


def swap_batch(value, offset, count):
    return lax.ppermute(value, "batch", [(i, i ^ offset) for i in range(count)])


def after(values, *earlier):
    return lax.optimization_barrier(tuple(values) + tuple(earlier))[: len(values)]


def place(rows):
    steps = rows // SEGMENTS
    out = lax.broadcasted_iota(jnp.int32, (rows, rows), 0)
    inn = lax.broadcasted_iota(jnp.int32, (rows, rows), 1)
    source = lax.rem(out, SEGMENTS) * steps + lax.div(out, SEGMENTS)
    return (source == inn).astype(F32).astype(BF16)


def place_back(rows):
    steps = rows // SEGMENTS
    out = lax.broadcasted_iota(jnp.int32, (rows, rows), 0)
    inn = lax.broadcasted_iota(jnp.int32, (rows, rows), 1)
    source = lax.rem(out, steps) * SEGMENTS + lax.div(out, steps)
    return (source == inn).astype(F32).astype(BF16)


def dot(a, b):
    return lax.dot_general(a, b, (((1,), (0,)), ((), ())), preferred_element_type=F32)


def tiles(count, tile, body):
    @pl.loop(0, count // tile)
    def _(index):
        body(pl.ds(pl.multiple_of(index * tile, tile), tile))


def unrolled(count, tile, body):
    for index in range(count // tile):
        body(pl.ds(index * tile, tile))


class Shards:
    def __init__(self, groups):
        self.pieces, self.groups = [], []
        for group in groups:
            made = []
            for piece in group:
                array, start, rows = piece if isinstance(piece, tuple) else (piece, 0, piece.shape[0])
                known = [index for index, other in enumerate(self.pieces) if other is array]
                if not known:
                    known = [len(self.pieces)]
                    self.pieces.append(array)
                made.append((known[0], start, rows))
            self.groups.append(made)
        self.depth = sum(rows for _, _, rows in self.groups[0])
        self.width = self.pieces[0].shape[1]

    def operands(self):
        return [pltpu.with_memory_space_constraint(piece, pltpu.VMEM) for piece in self.pieces]

    def block(self, refs, index, part, size):
        found, begin = [], 0
        for which, start, rows in self.groups[index]:
            low, high = max(part, begin), min(part + size, begin + rows)
            if low < high:
                found.append(refs[which][start + low - begin : start + high - begin, :])
            begin += rows
        return found[0] if len(found) == 1 else jnp.concatenate(found, axis=0)

    def product(self, x_ref, skip, refs, span):
        total = None
        joint = max(1, min(len(self.groups), 4))
        for index in range(0, len(self.groups), joint):
            groups = self.groups[index : index + joint]
            found = [refs[which][start : start + rows, span] for group in groups for which, start, rows in group]
            block = found[0] if len(found) == 1 else jnp.concatenate(found, axis=0)
            start = skip + index * self.depth
            term = dot(x_ref[:, start : start + len(groups) * self.depth], block)
            total = term if total is None else total + term
        return total


def near(value):
    return pltpu.with_memory_space_constraint(value, pltpu.VMEM)


VMEM_SPEC = pl.BlockSpec(memory_space=pltpu.VMEM)
SMEM_SPEC = pl.BlockSpec(memory_space=pltpu.SMEM)


def norm_call(where, x, g, gain, depth):
    rows, width = x.shape

    def kernel(where_ref, x_ref, g_ref, gain_ref, normed_ref, grads_ref, scale_ref, hold):
        def rows_body(span):
            x = x_ref[span, :].astype(F32)
            scale = lax.rsqrt(jnp.mean(x * x, axis=-1, keepdims=True) + EPSILON)
            scale_ref[span, :] = scale
            hold[span, :] = (x * scale * gain_ref[...]).astype(BF16)

        tiles(rows, min(32, rows), rows_body)
        order = place(rows)
        for index in range(width // depth):
            source = pl.ds(pl.multiple_of((where_ref[0] ^ index) * depth, depth), depth)
            normed_ref[:, index * depth : (index + 1) * depth] = dot(order, hold[:, source]).astype(BF16)

        def grads_body(span):
            grads_ref[span, :] = dot(order, g_ref[:, span]).T.astype(BF16)

        tiles(width, min(512, width), grads_body)

    return pl.pallas_call(
        kernel,
        out_shape=[
            jax.ShapeDtypeStruct((rows, width), BF16),
            jax.ShapeDtypeStruct((width, rows), BF16),
            jax.ShapeDtypeStruct((rows, 1), F32),
        ],
        in_specs=[SMEM_SPEC] + [VMEM_SPEC] * 3,
        out_specs=[VMEM_SPEC] * 3,
        scratch_shapes=[pltpu.VMEM(x.shape, BF16)],
        compiler_params=params(14),
        cost_estimate=cost(4 * rows * x.size, 8 * x.size),
        name="norm_rows",
    )(where, near(x), near(g), near(gain))


def project_call(x, shards, tile, dtype, skip=0):
    rows, width = x.shape[0], shards.width
    count, depth = len(shards.groups), shards.depth

    def kernel(x_ref, *refs):
        refs, out_ref = refs[:-1], refs[-1]

        def body(span):
            out_ref[:, span] = shards.product(x_ref, skip, refs, span).astype(dtype)

        tiles(width, tile, body)

    return pl.pallas_call(
        kernel,
        out_shape=jax.ShapeDtypeStruct((rows, width), dtype),
        in_specs=[VMEM_SPEC] + [VMEM_SPEC] * len(shards.pieces),
        out_specs=VMEM_SPEC,
        compiler_params=params(14),
        cost_estimate=cost(2 * rows * count * depth * width, 2 * count * depth * width),
        name="project",
    )(near(x), *shards.operands())


def back_call(where, grads, shards):
    width, rows = grads.shape
    count, depth = len(shards.groups), shards.depth

    def kernel(where_ref, g_ref, *refs):
        refs, out_ref = refs[:-1], refs[-1]
        size = min(depth, 256)
        for index in range(count):
            for part in range(0, depth, size):
                target = pl.multiple_of((where_ref[0] ^ index) * depth + part, size)
                term = dot(shards.block(refs, index, part, size), g_ref[...])
                out_ref[:, pl.ds(target, size)] = term.T.astype(BF16)

    return pl.pallas_call(
        kernel,
        out_shape=jax.ShapeDtypeStruct((rows, count * depth), BF16),
        in_specs=[SMEM_SPEC, VMEM_SPEC] + [VMEM_SPEC] * len(shards.pieces),
        out_specs=VMEM_SPEC,
        compiler_params=params(14),
        cost_estimate=cost(2 * rows * count * depth * width, 2 * count * depth * width),
        name="back_rows",
    )(where, near(grads), *shards.operands())


def gates(x):
    under = 1.0 + jnp.minimum(jnp.exp(-x), LARGE)
    rough = pl.reciprocal(under, approx=True)
    update = rough * (2.0 - under * rough)
    return update, 1.0 - update


def slab_pair(ref, pair, span):
    return split(ref[pair * 2 * SEGMENTS : (pair + 1) * 2 * SEGMENTS, span])


def split(both):
    both = both.astype(F32)
    return both[:SEGMENTS], both[SEGMENTS:]


def chosen_pair(where_ref, first_ref, second_ref, pair, span):
    here = slice(pair * 2 * SEGMENTS, (pair + 1) * 2 * SEGMENTS)
    gate, cand = choose(where_ref, first_ref[here, span], second_ref[here, span])
    return split(gate), split(cand)


def choose(where_ref, one, other):
    straight = where_ref[1] == 0
    return jnp.where(straight, one, other), jnp.where(straight, other, one)


def totals_call(where, x, partial, shards, skip, first_pre, back, both, block, tile):
    rows, width = first_pre.shape
    pairs = rows // (2 * SEGMENTS)
    count, depth = len(shards.groups), shards.depth
    extra = [] if partial is None else [partial]

    def kernel(where_ref, x_ref, first_ref, back_ref, both_ref, *refs):
        partial_refs, refs = refs[: len(extra)], refs[len(extra) :]
        refs, (second_ref, parts_ref, whole_ref, rows_ref) = refs[:-4], refs[-4:]
        for index in range(width // block):
            target = pl.multiple_of((where_ref[0] ^ index) * block, block)
            rows_ref[:, pl.ds(target, block)] = both_ref[:, index * block : (index + 1) * block]

        def body(span):
            total = shards.product(x_ref, skip, refs, span)
            for ref in partial_refs:
                total = total + ref[:, span]
            second_ref[:, span] = total.astype(BF16)
            bias = rows_ref[0:1, span]
            keep = jnp.ones((SEGMENTS, tile), F32)
            state = leaving = slope_run = slopes = updates = crossed = jnp.zeros((SEGMENTS, tile), F32)
            for pair in range(pairs):
                slabs = chosen_pair(where_ref, first_ref, second_ref, pair, span)
                for gate, cand, g in zip(*slabs, slab_pair(back_ref, pair, span)):
                    update, retain = gates(gate + bias)
                    slope = (cand - state) * update * retain
                    keep = keep * retain
                    state = retain * state + update * cand
                    kept_grad = keep * g
                    leaving = leaving + kept_grad
                    slope_run = retain * slope_run + slope
                    slopes = slopes + g * slope_run
                    updates = updates + update
                    crossed = crossed + kept_grad * updates
            parts_ref[0, :, span], parts_ref[1, :, span], parts_ref[2, :, span] = keep, state, leaving
            both_sides = keep * updates
            row = lambda value, s: value[s : s + 1]
            zero, one = row(keep, 0) * 0.0, row(keep, 0) * 0.0 + 1.0
            start, start_slope = [zero], [one]
            for s in range(SEGMENTS):
                start.append(row(keep, s) * start[-1] + row(state, s))
                start_slope.append(row(keep, s) * start_slope[-1])
            tail, tail_slope = [zero], [one]
            for s in range(SEGMENTS - 1, -1, -1):
                tail.append(row(keep, s) * tail[-1] + row(leaving, s))
                tail_slope.append(row(keep, s) * tail_slope[-1])
            whole = [start_slope[-1], start[-1], tail[-1]]
            start, start_slope = jnp.concatenate(start[:-1], axis=0), jnp.concatenate(start_slope[:-1], axis=0)
            tail = jnp.concatenate(tail[-2::-1], axis=0)
            tail_slope = jnp.concatenate(tail_slope[-2::-1], axis=0)
            by_tail = slope_run - both_sides * start
            by_start = crossed + both_sides * tail
            sums = [
                slopes + slope_run * tail - by_start * start,
                by_tail * tail_slope,
                by_start * start_slope,
                both_sides * tail_slope * start_slope,
            ]
            whole += [jnp.sum(value, axis=0, keepdims=True) for value in sums] + [zero]
            whole_ref[:, span] = jnp.concatenate(whole, axis=0)

        unrolled(width, tile, body)

    return pl.pallas_call(
        kernel,
        out_shape=[
            jax.ShapeDtypeStruct((rows, width), BF16),
            jax.ShapeDtypeStruct((3, SEGMENTS, width), F32),
            jax.ShapeDtypeStruct((8, width), F32),
            jax.ShapeDtypeStruct((2, width), F32),
        ],
        in_specs=[SMEM_SPEC] + [VMEM_SPEC] * (4 + len(extra)) + [VMEM_SPEC] * len(shards.pieces),
        out_specs=[VMEM_SPEC] * 4,
        compiler_params=params(14),
        cost_estimate=cost(2 * rows * count * depth * width, 2 * count * depth * width),
        name="project_totals",
    )(where, *map(near, (x, first_pre, back, both, *extra)), *shards.operands())


def scan_call(where, first_pre, second_pre, back, both, parts, wholes, offsets, ranks, shard, tile):
    rows, width = first_pre.shape
    pairs = rows // (2 * SEGMENTS)

    def kernel(where_ref, first_ref, second_ref, back_ref, both_ref, parts_ref, *refs):
        whole_refs, refs = refs[: len(wholes)], refs[len(wholes) :]
        (state_ref, one_ref, other_ref, bias_grad_ref, state_grad_ref) = refs[:5]
        hold, kept, updates, slopes, one_hold, other_hold, state_hold = refs[5:]
        me = where_ref[2]
        order, order_back = place_back(rows), place(rows)

        def body(span):
            for ref, members in zip(whole_refs, offsets):
                for member, offset in enumerate(members):
                    hold[where_ref[0] ^ offset] = ref[member, :, span]
            blocks = [hold[rank] for rank in range(ranks)]
            held = both_ref[1:2, span]
            entering, held_by = held, []
            for rank in range(ranks):
                block = blocks[rank]
                entering = jnp.where(rank == me, held, entering)
                held_by.append(held)
                held = block[0:1] * held + block[1:2]
            arriving = state_grad = bias_sum = held * 0.0
            for rank in range(ranks - 1, -1, -1):
                block, held = blocks[rank], held_by[rank]
                arriving = jnp.where(rank == me, state_grad, arriving)
                by_tail = block[4:5] - block[6:7] * held
                bias_sum = bias_sum + block[3:4] - block[5:6] * held + by_tail * state_grad
                state_grad = block[0:1] * state_grad + block[2:3]
            state_grad_ref[:, span] = state_grad
            bias_grad_ref[:, span] = bias_sum
            keep, ends, leaves = parts_ref[0, :, span], parts_ref[1, :, span], parts_ref[2, :, span]
            starts = [entering]
            for s in range(SEGMENTS - 1):
                starts.append(keep[s : s + 1] * starts[-1] + ends[s : s + 1])
            tails = [arriving]
            for s in range(SEGMENTS - 1, 0, -1):
                tails.append(keep[s : s + 1] * tails[-1] + leaves[s : s + 1])
            state = jnp.concatenate(starts, axis=0)
            leaving = jnp.concatenate(tails[::-1], axis=0)
            bias = both_ref[0:1, span]

            for pair in range(pairs):
                states, retains, ups, slope = [], [], [], []
                for gate, cand in zip(*chosen_pair(where_ref, first_ref, second_ref, pair, span)):
                    update, retain = gates(gate + bias)
                    retains.append(retain)
                    ups.append(update)
                    slope.append((cand - state) * update * retain)
                    state = retain * state + update * cand
                    states.append(state)
                here = slice(pair * 2 * SEGMENTS, (pair + 1) * 2 * SEGMENTS)
                state_hold[here, :] = jnp.concatenate(states, axis=0).astype(BF16)
                kept[here, :] = jnp.concatenate(retains, axis=0)
                updates[here, :] = jnp.concatenate(ups, axis=0)
                slopes[here, :] = jnp.concatenate(slope, axis=0)

            for pair in range(pairs - 1, -1, -1):
                here = slice(pair * 2 * SEGMENTS, (pair + 1) * 2 * SEGMENTS)
                grads = slab_pair(back_ref, pair, span)
                retain, update, slope = kept[here, :], updates[here, :], slopes[here, :]
                late = grads[1] + leaving
                early = grads[0] + retain[SEGMENTS:] * late
                leaving = retain[:SEGMENTS] * early
                carried = jnp.concatenate([early, late], axis=0)
                gate_grad = carried * slope
                cand_grad = carried * update
                one, other = choose(where_ref, gate_grad.astype(BF16), cand_grad.astype(BF16))
                one_hold[here, :] = one
                other_hold[here, :] = other
            found = dot(order, state_hold[...]).astype(BF16)
            size = min(shard, tile)
            for part in range(0, tile, size):
                target = span.start + part
                if shard <= tile:
                    target = (where_ref[0] ^ lax.div(target, shard)) * shard
                state_ref[:, pl.ds(pl.multiple_of(target, size), size)] = found[:, part : part + size]
            one_ref[span, :] = dot(one_hold[...].T, order_back).astype(BF16)
            other_ref[span, :] = dot(other_hold[...].T, order_back).astype(BF16)

        unrolled(width, tile, body)

    wide = jax.ShapeDtypeStruct((rows, width), BF16)
    tall = jax.ShapeDtypeStruct((width, rows), BF16)
    flat = jax.ShapeDtypeStruct((1, width), F32)
    return pl.pallas_call(
        kernel,
        out_shape=[wide, tall, tall, flat, flat],
        in_specs=[SMEM_SPEC] + [VMEM_SPEC] * (5 + len(wholes)),
        out_specs=[VMEM_SPEC] * 5,
        scratch_shapes=[pltpu.VMEM((ranks, SEGMENTS, tile), F32)]
        + [pltpu.VMEM((rows, tile), F32)] * 3
        + [pltpu.VMEM((rows, tile), BF16)] * 3,
        compiler_params=params(14),
        cost_estimate=cost(6 * rows * rows * width, 12 * rows * width),
        name="scan_rows",
    )(where, *map(near, (first_pre, second_pre, back, both, parts, *wholes)))


def layer_call(where, state_rows, residual, shards, tile):
    rows, width = residual.shape
    count, depth = len(shards.groups), shards.depth

    def kernel(where_ref, x_ref, residual_ref, *refs):
        refs, out_ref = refs[:-1], refs[-1]
        def body(span):
            total = shards.product(x_ref, 0, refs, span)
            out_ref[:, span] = (residual_ref[:, span].astype(F32) + total).astype(BF16)

        unrolled(width, tile, body)

    return pl.pallas_call(
        kernel,
        out_shape=jax.ShapeDtypeStruct((rows, width), BF16),
        in_specs=[SMEM_SPEC] + [VMEM_SPEC] * 2 + [VMEM_SPEC] * len(shards.pieces),
        out_specs=VMEM_SPEC,
        compiler_params=params(14),
        cost_estimate=cost(2 * rows * count * depth * width, 2 * count * depth * width),
        name="layer_rows",
    )(where, near(state_rows), near(residual), *shards.operands())


def input_grad_call(where, one, other, first, second, x, scale, grads, gain):
    rows, width = x.shape
    hidden = one.shape[0]
    count, depth = len(first.groups), first.depth

    def kernel(where_ref, one_ref, other_ref, x_ref, scale_ref, grads_ref, gain_ref, *refs):
        first_refs = refs[: len(first.pieces)]
        second_refs = refs[len(first.pieces) : len(first.pieces) + len(second.pieces)]
        out_ref, total = refs[-2:]
        size = min(depth, 256)
        for index in range(count):
            for part in range(0, depth, size):
                target = pl.multiple_of((where_ref[0] ^ index) * depth + part, size)
                term = dot(first.block(first_refs, index, part, size), one_ref[...])
                term = term + dot(second.block(second_refs, index, part, size), other_ref[...])
                total[:, pl.ds(target, size)] = term.T

        def body(span):
            x = x_ref[span, :].astype(F32)
            scale = scale_ref[span, :]
            unit = x * scale
            unit_grad = total[span, :] * gain_ref[...]
            along = jnp.mean(unit_grad * unit, axis=-1, keepdims=True)
            out = grads_ref[span, :].astype(F32) + scale * (unit_grad - unit * along)
            out_ref[span, :] = out.astype(BF16)

        unrolled(rows, min(32, rows), body)

    return pl.pallas_call(
        kernel,
        out_shape=jax.ShapeDtypeStruct((rows, width), BF16),
        in_specs=[SMEM_SPEC] + [VMEM_SPEC] * 6 + [VMEM_SPEC] * (len(first.pieces) + len(second.pieces)),
        out_specs=VMEM_SPEC,
        scratch_shapes=[pltpu.VMEM((rows, width), F32)],
        compiler_params=params(14),
        cost_estimate=cost(4 * one.size * width, 4 * hidden * width),
        name="input_grad_rows",
    )(where, *map(near, (one, other, x, scale, grads, gain)), *first.operands(), *second.operands())


def close_call(where, state_grad, rows, block):
    def kernel(where_ref, state_ref, *refs):
        refs, (state_out_ref, bias_out_ref) = refs[:-2], refs[-2:]
        here = pl.ds(pl.multiple_of(where_ref[2] * block, block), block)
        state_out_ref[...] = state_ref[:, here]
        bias_out_ref[...] = sum((ref[:, here] for ref in refs[1:]), refs[0][:, here])

    return pl.pallas_call(
        kernel,
        out_shape=[jax.ShapeDtypeStruct((1, block), F32)] * 2,
        in_specs=[SMEM_SPEC] + [VMEM_SPEC] * (1 + len(rows)),
        out_specs=[VMEM_SPEC] * 2,
        compiler_params=params(2),
        cost_estimate=cost(1, 4 * state_grad.size),
        name="close_rows",
    )(where, state_grad, *rows)


def front_on_cube(ranks, batches, where, turned, tile, rows_in, grad_rows, gain, gate_bias, state_in, w_gate, w_cand, w_out):
    half = w_gate.shape[0] // 2
    depth = w_gate.shape[0]
    halves = lambda w: (w[:half], w[half:])
    straight = turned == 0
    send = lambda value, offset: hop(value, offset, ranks)
    core = lambda value: hop(value, 1, ranks)
    over = lambda value: swap_batch(value, 1, batches)
    f_a = jnp.where(straight, w_gate[:half], w_cand[:half])
    f_a, where, w_gate, w_cand, own_t = after((f_a, where, w_gate, w_cand, w_out))
    own_f = [f_a, jnp.where(straight, w_gate[half:], w_cand[half:])]
    stack = lambda *parts: jnp.concatenate(parts, axis=0)
    cut = lambda held, *starts: [(held, start * half, half) for start in starts]
    f2a, f4a = send(own_f[0], 2), send(own_f[0], 4)
    f1 = [core(v) for v in own_f]
    both = jnp.stack([gate_bias, state_in[0]])
    both = jnp.concatenate([both, core(both)], axis=1)
    both = jnp.concatenate([both, send(both, 2)], axis=1)
    normed, grads, scale = norm_call(where, rows_in, grad_rows, gain, depth)
    own_s = jnp.where(straight, w_cand, w_gate)
    t_a, t_b = halves(own_t)
    f2a, f4a, f1a, f1b, both, normed, grads, f_b, own_s, own_t, t_a, t_b = after(
        (f2a, f4a, f1[0], f1[1], both, normed, grads, own_f[1], own_s, own_t, t_a, t_b)
    )
    f2b, f4b = send(f_b, 2), send(f_b, 4)
    t2a, t4a = send(t_a, 2), send(t_a, 4)
    sa = over(stack(f2a, f4a))
    f2b, f4b, f3a, f5a = after((f2b, f4b, f2a, f4a))
    f3a, f5a = core(f3a), core(f5a)
    f2b, f4b, f_b2, sa, t2a, t4a, f3a, f5a, t_b, f2a = after(
        (f2b, f4b, stack(f2b, f4b), sa, t2a, t4a, f3a, f5a, t_b, f2a)
    )
    f6a, f6b = send(f2a, 4), send(f4b, 2)
    t2b, t4b = send(t_b, 2), send(t_b, 4)
    sb = over(f_b2)
    f6a, f6b, f3b, f5b = after((f6a, f6b, f2b, f4b))
    f3b, f5b = core(f3b), core(f5b)
    both, f6a, f6b, sb, t2b, t4b, f3b, f5b, sa, t2a = after((both, f6a, f6b, sb, t2b, t4b, f3b, f5b, sa, t2a))
    t6a, t6b = send(t2a, 4), send(t4b, 2)
    s6a = over(f6a)
    f7, cs = core(stack(f6a, f6b)), core(stack(sa, sb, own_s))
    first = Shards([own_f, [f1a, f1b], [f2a, f2b], [f3a, f3b], [f4a, f4b], [f5a, f5b], [f6a, f6b], [f7]])
    pairs = lambda one, two, row: cut(one, row) + cut(two, row)
    most = [[own_s], cut(cs, 4, 5), pairs(sa, sb, 0), cut(cs, 0, 2), pairs(sa, sb, 1), cut(cs, 1, 3)]
    first_pre = project_call(normed, first, tile, BF16)
    partial = project_call(normed, Shards(most), tile, F32)
    both = jnp.concatenate([both, send(after((both,), partial)[0], 4)], axis=1)
    t6a, t6b, s6a, sb_out, first_pre, partial, own_t, both = after(
        (t6a, t6b, s6a, sb, first_pre, partial, own_t, both)
    )
    quarter = half // 2
    s6b = [send(sb_out[half : half + quarter], 2), send(sb_out[quarter:half], 4)]
    s7a = core(s6a)
    c4 = core(stack(t6a, t6b, t2b, t4b, own_t, t2a, t4a))
    third = Shards(
        [[own_t], cut(c4, 4, 5), [t2a, t2b], cut(c4, 6, 2), [t4a, t4b], cut(c4, 7, 3)]
        + [[t6a, t6b], cut(c4, 0, 1)]
    )
    back = back_call(where, grads, third)
    s6b_low, s6b_high, s7a, back, both = after((*s6b, s7a, back, both))
    last = [[s6a, s6b_low, s6b_high], [s7a, core(stack(s6b_low, s6b_high))]]
    second = Shards(most + last)
    second_pre, parts, whole, both = totals_call(
        where, normed, partial, Shards(last), len(most) * depth, first_pre, back, both, depth, tile
    )
    return where, scale, first, second, third, first_pre, second_pre, back, both, parts, whole


def front(where, tile, rows_in, grad_rows, gain, gate_bias, state_in, w_gate, w_cand, w_out):
    first, second, third = (
        Shards([[lax.all_gather(w, "seq", tiled=True)]]) for w in (w_gate, w_cand, w_out)
    )
    both = lax.all_gather(jnp.stack([gate_bias, state_in[0]]), "seq", axis=1, tiled=True)
    normed, grads, scale = norm_call(where, rows_in, grad_rows, gain, first.depth)
    first_pre = project_call(normed, first, tile, BF16)
    back = back_call(where, grads, third)
    second_pre, parts, whole, both = totals_call(
        where, normed, None, second, 0, first_pre, back, both, first.depth, tile
    )
    return where, scale, first, second, third, first_pre, second_pre, back, both, parts, whole


def on_device(ranks, batches, inputs, output_grad, norm_gain, gate_bias, state_in, w_gate, w_cand, w_out):
    rows_in, grad_rows = inputs[0], output_grad[0]
    gain = norm_gain[None, :]
    hidden = w_gate.shape[1]
    tile = min(512, hidden)
    me = lax.axis_index("seq")
    given = (rows_in, grad_rows, gain, gate_bias, state_in, w_gate, w_cand, w_out)
    cube = ranks == 8 and batches in (2, 4, 8)
    if cube:
        turned = lax.axis_index("batch") % 2
        where = jnp.stack([me, turned, me]).astype(jnp.int32)
        found = front_on_cube(ranks, batches, where, turned, tile, *given)
    else:
        nought = jnp.zeros_like(me)
        where = jnp.stack([nought, nought, me]).astype(jnp.int32)
        found = front(where, tile, *given)
    where, scale, first, second, third, first_pre, second_pre, back, both, parts, whole = found
    if cube:
        found = jnp.stack([hop(whole, offset, ranks) for offset in (2, 4, 6)])
        wholes = [jnp.stack([whole, hop(whole, 1, ranks)]), found, hop(found, 1, ranks)]
        offsets = [(0, 1), (2, 4, 6), (3, 5, 7)]
    else:
        wholes, offsets = [lax.all_gather(whole, "seq")], [range(ranks)]
    state_rows, one, other, bias_part, state_grad = scan_call(
        where, first_pre, second_pre, back, both, parts, wholes, offsets, ranks, third.depth, tile
    )
    width = hidden // ranks
    if cube:
        came = swap_batch(bias_part, 1, batches)
        layer_out = layer_call(where, state_rows, rows_in, third, tile)
        layer_out, bias_part, came, one, other = after((layer_out, bias_part, came, one, other))
        for offset in range(1, batches.bit_length() - 1):
            bias_part = bias_part + came
            came = swap_batch(bias_part, 1 << offset, batches)
        input_grad = input_grad_call(where, one, other, first, second, rows_in, scale, grad_rows, gain)
        state_out, bias_grad = close_call(where, state_grad, [bias_part, came], width)
        bias_grad = bias_grad[0]
    else:
        own_block = lax.dynamic_slice_in_dim(bias_part[0], me * width, width, 0)
        bias_grad = lax.psum(own_block, "batch")
        layer_out = layer_call(where, state_rows, rows_in, third, tile)
        input_grad = input_grad_call(where, one, other, first, second, rows_in, scale, grad_rows, gain)
        state_out = lax.dynamic_slice_in_dim(state_grad, me * width, width, 1)
    return (layer_out[None], input_grad[None], state_out, bias_grad)


def solution(mesh):
    body = functools.partial(on_device, mesh.shape["seq"], mesh.shape["batch"])
    rows = P("batch", "seq", None)
    return jax.shard_map(
        body,
        mesh=mesh,
        in_specs=(rows, rows, P(), P("seq"), P("batch", "seq"), P("seq", None), P("seq", None), P("seq", None)),
        out_specs=(rows, rows, P("batch", "seq"), P("seq")),
        check_vma=False,
    )
```

```python
import functools

import jax
import jax.numpy as jnp
from jax import lax
from jax.experimental import pallas as pl
from jax.experimental.pallas import tpu as pltpu
from jax.sharding import PartitionSpec as P

EPSILON = 1e-06
SEGMENTS = 8
LARGE = 1e37
F32 = jnp.float32
BF16 = jnp.bfloat16


def params(mebibytes):
    return pltpu.CompilerParams(vmem_limit_bytes=mebibytes * 1024 * 1024)


def cost(flops, moved):
    return pl.CostEstimate(flops=int(flops), bytes_accessed=int(moved), transcendentals=0)


def hop(value, offset, count):
    return lax.ppermute(value, "seq", [(i, i ^ offset) for i in range(count)])


def swap_batch(value, offset, count):
    return lax.ppermute(value, "batch", [(i, i ^ offset) for i in range(count)])


def after(values, *earlier):
    return lax.optimization_barrier(tuple(values) + tuple(earlier))[: len(values)]


def place(rows):
    steps = rows // SEGMENTS
    out = lax.broadcasted_iota(jnp.int32, (rows, rows), 0)
    inn = lax.broadcasted_iota(jnp.int32, (rows, rows), 1)
    source = lax.rem(out, SEGMENTS) * steps + lax.div(out, SEGMENTS)
    return (source == inn).astype(F32).astype(BF16)


def place_back(rows):
    steps = rows // SEGMENTS
    out = lax.broadcasted_iota(jnp.int32, (rows, rows), 0)
    inn = lax.broadcasted_iota(jnp.int32, (rows, rows), 1)
    source = lax.rem(out, steps) * SEGMENTS + lax.div(out, steps)
    return (source == inn).astype(F32).astype(BF16)


def dot(a, b):
    return lax.dot_general(a, b, (((1,), (0,)), ((), ())), preferred_element_type=F32)


def tiles(count, tile, body):
    @pl.loop(0, count // tile)
    def _(index):
        body(pl.ds(pl.multiple_of(index * tile, tile), tile))


def unrolled(count, tile, body):
    for index in range(count // tile):
        body(pl.ds(index * tile, tile))


class Shards:
    def __init__(self, groups):
        self.pieces, self.groups = [], []
        for group in groups:
            made = []
            for piece in group:
                array, start, rows = piece if isinstance(piece, tuple) else (piece, 0, piece.shape[0])
                known = [index for index, other in enumerate(self.pieces) if other is array]
                if not known:
                    known = [len(self.pieces)]
                    self.pieces.append(array)
                made.append((known[0], start, rows))
            self.groups.append(made)
        self.depth = sum(rows for _, _, rows in self.groups[0])
        self.width = self.pieces[0].shape[1]

    def operands(self):
        return [pltpu.with_memory_space_constraint(piece, pltpu.VMEM) for piece in self.pieces]

    def block(self, refs, index, part, size):
        found, begin = [], 0
        for which, start, rows in self.groups[index]:
            low, high = max(part, begin), min(part + size, begin + rows)
            if low < high:
                found.append(refs[which][start + low - begin : start + high - begin, :])
            begin += rows
        return found[0] if len(found) == 1 else jnp.concatenate(found, axis=0)

    def product(self, x_ref, skip, refs, span):
        total = None
        joint = max(1, min(len(self.groups), 4))
        for index in range(0, len(self.groups), joint):
            groups = self.groups[index : index + joint]
            found = [refs[which][start : start + rows, span] for group in groups for which, start, rows in group]
            block = found[0] if len(found) == 1 else jnp.concatenate(found, axis=0)
            start = skip + index * self.depth
            term = dot(x_ref[:, start : start + len(groups) * self.depth], block)
            total = term if total is None else total + term
        return total


def near(value):
    return pltpu.with_memory_space_constraint(value, pltpu.VMEM)


VMEM_SPEC = pl.BlockSpec(memory_space=pltpu.VMEM)
SMEM_SPEC = pl.BlockSpec(memory_space=pltpu.SMEM)


def norm_call(where, x, g, gain, depth):
    rows, width = x.shape

    def kernel(where_ref, x_ref, g_ref, gain_ref, normed_ref, grads_ref, scale_ref, hold):
        def rows_body(span):
            x = x_ref[span, :].astype(F32)
            scale = lax.rsqrt(jnp.mean(x * x, axis=-1, keepdims=True) + EPSILON)
            scale_ref[span, :] = scale
            hold[span, :] = (x * scale * gain_ref[...]).astype(BF16)

        tiles(rows, min(32, rows), rows_body)
        order = place(rows)
        for index in range(width // depth):
            source = pl.ds(pl.multiple_of((where_ref[0] ^ index) * depth, depth), depth)
            normed_ref[:, index * depth : (index + 1) * depth] = dot(order, hold[:, source]).astype(BF16)

        def grads_body(span):
            grads_ref[span, :] = dot(order, g_ref[:, span]).T.astype(BF16)

        tiles(width, min(512, width), grads_body)

    return pl.pallas_call(
        kernel,
        out_shape=[
            jax.ShapeDtypeStruct((rows, width), BF16),
            jax.ShapeDtypeStruct((width, rows), BF16),
            jax.ShapeDtypeStruct((rows, 1), F32),
        ],
        in_specs=[SMEM_SPEC] + [VMEM_SPEC] * 3,
        out_specs=[VMEM_SPEC] * 3,
        scratch_shapes=[pltpu.VMEM(x.shape, BF16)],
        compiler_params=params(14),
        cost_estimate=cost(4 * rows * x.size, 8 * x.size),
        name="norm_rows",
    )(where, near(x), near(g), near(gain))


def project_call(x, shards, tile, dtype, skip=0):
    rows, width = x.shape[0], shards.width
    count, depth = len(shards.groups), shards.depth

    def kernel(x_ref, *refs):
        refs, out_ref = refs[:-1], refs[-1]

        def body(span):
            out_ref[:, span] = shards.product(x_ref, skip, refs, span).astype(dtype)

        tiles(width, tile, body)

    return pl.pallas_call(
        kernel,
        out_shape=jax.ShapeDtypeStruct((rows, width), dtype),
        in_specs=[VMEM_SPEC] + [VMEM_SPEC] * len(shards.pieces),
        out_specs=VMEM_SPEC,
        compiler_params=params(14),
        cost_estimate=cost(2 * rows * count * depth * width, 2 * count * depth * width),
        name="project",
    )(near(x), *shards.operands())


def back_call(where, grads, shards):
    width, rows = grads.shape
    count, depth = len(shards.groups), shards.depth

    def kernel(where_ref, g_ref, *refs):
        refs, out_ref = refs[:-1], refs[-1]
        size = min(depth, 256)
        for index in range(count):
            for part in range(0, depth, size):
                target = pl.multiple_of((where_ref[0] ^ index) * depth + part, size)
                term = dot(shards.block(refs, index, part, size), g_ref[...])
                out_ref[:, pl.ds(target, size)] = term.T.astype(BF16)

    return pl.pallas_call(
        kernel,
        out_shape=jax.ShapeDtypeStruct((rows, count * depth), BF16),
        in_specs=[SMEM_SPEC, VMEM_SPEC] + [VMEM_SPEC] * len(shards.pieces),
        out_specs=VMEM_SPEC,
        compiler_params=params(14),
        cost_estimate=cost(2 * rows * count * depth * width, 2 * count * depth * width),
        name="back_rows",
    )(where, near(grads), *shards.operands())


def gates(x):
    under = 1.0 + jnp.minimum(jnp.exp(-x), LARGE)
    rough = pl.reciprocal(under, approx=True)
    update = rough * (2.0 - under * rough)
    return update, 1.0 - update


def slab_pair(ref, pair, span):
    return split(ref[pair * 2 * SEGMENTS : (pair + 1) * 2 * SEGMENTS, span])


def split(both):
    both = both.astype(F32)
    return both[:SEGMENTS], both[SEGMENTS:]


def chosen_pair(where_ref, first_ref, second_ref, pair, span):
    here = slice(pair * 2 * SEGMENTS, (pair + 1) * 2 * SEGMENTS)
    gate, cand = choose(where_ref, first_ref[here, span], second_ref[here, span])
    return split(gate), split(cand)


def choose(where_ref, one, other):
    straight = where_ref[1] == 0
    return jnp.where(straight, one, other), jnp.where(straight, other, one)


def totals_call(where, x, partial, shards, skip, first_pre, back, both, block, tile):
    rows, width = first_pre.shape
    pairs = rows // (2 * SEGMENTS)
    count, depth = len(shards.groups), shards.depth
    extra = [] if partial is None else [partial]

    def kernel(where_ref, x_ref, first_ref, back_ref, both_ref, *refs):
        partial_refs, refs = refs[: len(extra)], refs[len(extra) :]
        refs, (second_ref, parts_ref, whole_ref, rows_ref) = refs[:-4], refs[-4:]
        for index in range(width // block):
            target = pl.multiple_of((where_ref[0] ^ index) * block, block)
            rows_ref[:, pl.ds(target, block)] = both_ref[:, index * block : (index + 1) * block]

        def body(span):
            total = shards.product(x_ref, skip, refs, span)
            for ref in partial_refs:
                total = total + ref[:, span]
            second_ref[:, span] = total.astype(BF16)
            bias = rows_ref[0:1, span]
            keep = jnp.ones((SEGMENTS, tile), F32)
            state = leaving = slope_run = slopes = updates = crossed = jnp.zeros((SEGMENTS, tile), F32)
            for pair in range(pairs):
                slabs = chosen_pair(where_ref, first_ref, second_ref, pair, span)
                for gate, cand, g in zip(*slabs, slab_pair(back_ref, pair, span)):
                    update, retain = gates(gate + bias)
                    slope = (cand - state) * update * retain
                    keep = keep * retain
                    state = retain * state + update * cand
                    kept_grad = keep * g
                    leaving = leaving + kept_grad
                    slope_run = retain * slope_run + slope
                    slopes = slopes + g * slope_run
                    updates = updates + update
                    crossed = crossed + kept_grad * updates
            parts_ref[0, :, span], parts_ref[1, :, span], parts_ref[2, :, span] = keep, state, leaving
            both_sides = keep * updates
            row = lambda value, s: value[s : s + 1]
            zero, one = row(keep, 0) * 0.0, row(keep, 0) * 0.0 + 1.0
            start, start_slope = [zero], [one]
            for s in range(SEGMENTS):
                start.append(row(keep, s) * start[-1] + row(state, s))
                start_slope.append(row(keep, s) * start_slope[-1])
            tail, tail_slope = [zero], [one]
            for s in range(SEGMENTS - 1, -1, -1):
                tail.append(row(keep, s) * tail[-1] + row(leaving, s))
                tail_slope.append(row(keep, s) * tail_slope[-1])
            whole = [start_slope[-1], start[-1], tail[-1]]
            start, start_slope = jnp.concatenate(start[:-1], axis=0), jnp.concatenate(start_slope[:-1], axis=0)
            tail = jnp.concatenate(tail[-2::-1], axis=0)
            tail_slope = jnp.concatenate(tail_slope[-2::-1], axis=0)
            by_tail = slope_run - both_sides * start
            by_start = crossed + both_sides * tail
            sums = [
                slopes + slope_run * tail - by_start * start,
                by_tail * tail_slope,
                by_start * start_slope,
                both_sides * tail_slope * start_slope,
            ]
            whole += [jnp.sum(value, axis=0, keepdims=True) for value in sums] + [zero]
            whole_ref[:, span] = jnp.concatenate(whole, axis=0)

        unrolled(width, tile, body)

    return pl.pallas_call(
        kernel,
        out_shape=[
            jax.ShapeDtypeStruct((rows, width), BF16),
            jax.ShapeDtypeStruct((3, SEGMENTS, width), F32),
            jax.ShapeDtypeStruct((8, width), F32),
            jax.ShapeDtypeStruct((2, width), F32),
        ],
        in_specs=[SMEM_SPEC] + [VMEM_SPEC] * (4 + len(extra)) + [VMEM_SPEC] * len(shards.pieces),
        out_specs=[VMEM_SPEC] * 4,
        compiler_params=params(14),
        cost_estimate=cost(2 * rows * count * depth * width, 2 * count * depth * width),
        name="project_totals",
    )(where, *map(near, (x, first_pre, back, both, *extra)), *shards.operands())


def scan_call(where, first_pre, second_pre, back, both, parts, wholes, offsets, ranks, shard, tile):
    rows, width = first_pre.shape
    pairs = rows // (2 * SEGMENTS)

    def kernel(where_ref, first_ref, second_ref, back_ref, both_ref, parts_ref, *refs):
        whole_refs, refs = refs[: len(wholes)], refs[len(wholes) :]
        (state_ref, one_ref, other_ref, bias_grad_ref, state_grad_ref) = refs[:5]
        hold, kept, updates, slopes, one_hold, other_hold, state_hold = refs[5:]
        me = where_ref[2]
        order, order_back = place_back(rows), place(rows)

        def body(span):
            for ref, members in zip(whole_refs, offsets):
                for member, offset in enumerate(members):
                    hold[where_ref[0] ^ offset] = ref[member, :, span]
            blocks = [hold[rank] for rank in range(ranks)]
            held = both_ref[1:2, span]
            entering, held_by = held, []
            for rank in range(ranks):
                block = blocks[rank]
                entering = jnp.where(rank == me, held, entering)
                held_by.append(held)
                held = block[0:1] * held + block[1:2]
            arriving = state_grad = bias_sum = held * 0.0
            for rank in range(ranks - 1, -1, -1):
                block, held = blocks[rank], held_by[rank]
                arriving = jnp.where(rank == me, state_grad, arriving)
                by_tail = block[4:5] - block[6:7] * held
                bias_sum = bias_sum + block[3:4] - block[5:6] * held + by_tail * state_grad
                state_grad = block[0:1] * state_grad + block[2:3]
            state_grad_ref[:, span] = state_grad
            bias_grad_ref[:, span] = bias_sum
            keep, ends, leaves = parts_ref[0, :, span], parts_ref[1, :, span], parts_ref[2, :, span]
            starts = [entering]
            for s in range(SEGMENTS - 1):
                starts.append(keep[s : s + 1] * starts[-1] + ends[s : s + 1])
            tails = [arriving]
            for s in range(SEGMENTS - 1, 0, -1):
                tails.append(keep[s : s + 1] * tails[-1] + leaves[s : s + 1])
            state = jnp.concatenate(starts, axis=0)
            leaving = jnp.concatenate(tails[::-1], axis=0)
            bias = both_ref[0:1, span]

            for pair in range(pairs):
                states, retains, ups, slope = [], [], [], []
                for gate, cand in zip(*chosen_pair(where_ref, first_ref, second_ref, pair, span)):
                    update, retain = gates(gate + bias)
                    retains.append(retain)
                    ups.append(update)
                    slope.append((cand - state) * update * retain)
                    state = retain * state + update * cand
                    states.append(state)
                here = slice(pair * 2 * SEGMENTS, (pair + 1) * 2 * SEGMENTS)
                state_hold[here, :] = jnp.concatenate(states, axis=0).astype(BF16)
                kept[here, :] = jnp.concatenate(retains, axis=0)
                updates[here, :] = jnp.concatenate(ups, axis=0)
                slopes[here, :] = jnp.concatenate(slope, axis=0)

            for pair in range(pairs - 1, -1, -1):
                here = slice(pair * 2 * SEGMENTS, (pair + 1) * 2 * SEGMENTS)
                grads = slab_pair(back_ref, pair, span)
                retain, update, slope = kept[here, :], updates[here, :], slopes[here, :]
                late = grads[1] + leaving
                early = grads[0] + retain[SEGMENTS:] * late
                leaving = retain[:SEGMENTS] * early
                carried = jnp.concatenate([early, late], axis=0)
                gate_grad = carried * slope
                cand_grad = carried * update
                one, other = choose(where_ref, gate_grad.astype(BF16), cand_grad.astype(BF16))
                one_hold[here, :] = one
                other_hold[here, :] = other
            found = dot(order, state_hold[...]).astype(BF16)
            size = min(shard, tile)
            for part in range(0, tile, size):
                target = span.start + part
                if shard <= tile:
                    target = (where_ref[0] ^ lax.div(target, shard)) * shard
                state_ref[:, pl.ds(pl.multiple_of(target, size), size)] = found[:, part : part + size]
            one_ref[span, :] = dot(one_hold[...].T, order_back).astype(BF16)
            other_ref[span, :] = dot(other_hold[...].T, order_back).astype(BF16)

        unrolled(width, tile, body)

    wide = jax.ShapeDtypeStruct((rows, width), BF16)
    tall = jax.ShapeDtypeStruct((width, rows), BF16)
    flat = jax.ShapeDtypeStruct((1, width), F32)
    return pl.pallas_call(
        kernel,
        out_shape=[wide, tall, tall, flat, flat],
        in_specs=[SMEM_SPEC] + [VMEM_SPEC] * (5 + len(wholes)),
        out_specs=[VMEM_SPEC] * 5,
        scratch_shapes=[pltpu.VMEM((ranks, SEGMENTS, tile), F32)]
        + [pltpu.VMEM((rows, tile), F32)] * 3
        + [pltpu.VMEM((rows, tile), BF16)] * 3,
        compiler_params=params(14),
        cost_estimate=cost(6 * rows * rows * width, 12 * rows * width),
        name="scan_rows",
    )(where, *map(near, (first_pre, second_pre, back, both, parts, *wholes)))


def layer_call(where, state_rows, residual, shards, tile):
    rows, width = residual.shape
    count, depth = len(shards.groups), shards.depth

    def kernel(where_ref, x_ref, residual_ref, *refs):
        refs, out_ref = refs[:-1], refs[-1]
        def body(span):
            total = shards.product(x_ref, 0, refs, span)
            out_ref[:, span] = (residual_ref[:, span].astype(F32) + total).astype(BF16)

        unrolled(width, tile, body)

    return pl.pallas_call(
        kernel,
        out_shape=jax.ShapeDtypeStruct((rows, width), BF16),
        in_specs=[SMEM_SPEC] + [VMEM_SPEC] * 2 + [VMEM_SPEC] * len(shards.pieces),
        out_specs=VMEM_SPEC,
        compiler_params=params(14),
        cost_estimate=cost(2 * rows * count * depth * width, 2 * count * depth * width),
        name="layer_rows",
    )(where, near(state_rows), near(residual), *shards.operands())


def input_grad_call(where, one, other, first, second, x, scale, grads, gain):
    rows, width = x.shape
    hidden = one.shape[0]
    count, depth = len(first.groups), first.depth

    def kernel(where_ref, one_ref, other_ref, x_ref, scale_ref, grads_ref, gain_ref, *refs):
        first_refs = refs[: len(first.pieces)]
        second_refs = refs[len(first.pieces) : len(first.pieces) + len(second.pieces)]
        out_ref, total = refs[-2:]
        size = min(depth, 256)
        for index in range(count):
            for part in range(0, depth, size):
                target = pl.multiple_of((where_ref[0] ^ index) * depth + part, size)
                term = dot(first.block(first_refs, index, part, size), one_ref[...])
                term = term + dot(second.block(second_refs, index, part, size), other_ref[...])
                total[:, pl.ds(target, size)] = term.T

        def body(span):
            x = x_ref[span, :].astype(F32)
            scale = scale_ref[span, :]
            unit = x * scale
            unit_grad = total[span, :] * gain_ref[...]
            along = jnp.mean(unit_grad * unit, axis=-1, keepdims=True)
            out = grads_ref[span, :].astype(F32) + scale * (unit_grad - unit * along)
            out_ref[span, :] = out.astype(BF16)

        unrolled(rows, min(32, rows), body)

    return pl.pallas_call(
        kernel,
        out_shape=jax.ShapeDtypeStruct((rows, width), BF16),
        in_specs=[SMEM_SPEC] + [VMEM_SPEC] * 6 + [VMEM_SPEC] * (len(first.pieces) + len(second.pieces)),
        out_specs=VMEM_SPEC,
        scratch_shapes=[pltpu.VMEM((rows, width), F32)],
        compiler_params=params(14),
        cost_estimate=cost(4 * one.size * width, 4 * hidden * width),
        name="input_grad_rows",
    )(where, *map(near, (one, other, x, scale, grads, gain)), *first.operands(), *second.operands())


def close_call(where, state_grad, rows, block):
    def kernel(where_ref, state_ref, *refs):
        refs, (state_out_ref, bias_out_ref) = refs[:-2], refs[-2:]
        here = pl.ds(pl.multiple_of(where_ref[2] * block, block), block)
        state_out_ref[...] = state_ref[:, here]
        bias_out_ref[...] = sum((ref[:, here] for ref in refs[1:]), refs[0][:, here])

    return pl.pallas_call(
        kernel,
        out_shape=[jax.ShapeDtypeStruct((1, block), F32)] * 2,
        in_specs=[SMEM_SPEC] + [VMEM_SPEC] * (1 + len(rows)),
        out_specs=[VMEM_SPEC] * 2,
        compiler_params=params(2),
        cost_estimate=cost(1, 4 * state_grad.size),
        name="close_rows",
    )(where, state_grad, *rows)


def front_on_cube(ranks, batches, where, turned, tile, rows_in, grad_rows, gain, gate_bias, state_in, w_gate, w_cand, w_out):
    half = w_gate.shape[0] // 2
    depth = w_gate.shape[0]
    halves = lambda w: (w[:half], w[half:])
    straight = turned == 0
    send = lambda value, offset: hop(value, offset, ranks)
    core = lambda value: hop(value, 1, ranks)
    over = lambda value: swap_batch(value, 1, batches)
    f_a = jnp.where(straight, w_gate[:half], w_cand[:half])
    f_a, where, w_gate, w_cand, own_t = after((f_a, where, w_gate, w_cand, w_out))
    own_f = [f_a, jnp.where(straight, w_gate[half:], w_cand[half:])]
    stack = lambda *parts: jnp.concatenate(parts, axis=0)
    cut = lambda held, *starts: [(held, start * half, half) for start in starts]
    f2a, f4a = send(own_f[0], 2), send(own_f[0], 4)
    f1 = [core(v) for v in own_f]
    both = jnp.stack([gate_bias, state_in[0]])
    both = jnp.concatenate([both, core(both)], axis=1)
    both = jnp.concatenate([both, send(both, 2)], axis=1)
    normed, grads, scale = norm_call(where, rows_in, grad_rows, gain, depth)
    own_s = jnp.where(straight, w_cand, w_gate)
    t_a, t_b = halves(own_t)
    f2a, f4a, f1a, f1b, both, normed, grads, f_b, own_s, own_t, t_a, t_b = after(
        (f2a, f4a, f1[0], f1[1], both, normed, grads, own_f[1], own_s, own_t, t_a, t_b)
    )
    f2b, f4b = send(f_b, 2), send(f_b, 4)
    t2a, t4a = send(t_a, 2), send(t_a, 4)
    sa = over(stack(f2a, f4a))
    f2b, f4b, f3a, f5a = after((f2b, f4b, f2a, f4a))
    f3a, f5a = core(f3a), core(f5a)
    f2b, f4b, f_b2, sa, t2a, t4a, f3a, f5a, t_b, f2a = after(
        (f2b, f4b, stack(f2b, f4b), sa, t2a, t4a, f3a, f5a, t_b, f2a)
    )
    f6a, f6b = send(f2a, 4), send(f4b, 2)
    t2b, t4b = send(t_b, 2), send(t_b, 4)
    sb = over(f_b2)
    f6a, f6b, f3b, f5b = after((f6a, f6b, f2b, f4b))
    f3b, f5b = core(f3b), core(f5b)
    both, f6a, f6b, sb, t2b, t4b, f3b, f5b, sa, t2a = after((both, f6a, f6b, sb, t2b, t4b, f3b, f5b, sa, t2a))
    t6a, t6b = send(t2a, 4), send(t4b, 2)
    s6a = over(f6a)
    f7, cs = core(stack(f6a, f6b)), core(stack(sa, sb, own_s, own_t))
    first = Shards([own_f, [f1a, f1b], [f2a, f2b], [f3a, f3b], [f4a, f4b], [f5a, f5b], [f6a, f6b], [f7]])
    pairs = lambda one, two, row: cut(one, row) + cut(two, row)
    most = [[own_s], cut(cs, 4, 5), pairs(sa, sb, 0), cut(cs, 0, 2), pairs(sa, sb, 1), cut(cs, 1, 3)]
    first_pre = project_call(normed, first, tile, BF16)
    partial = project_call(normed, Shards(most), tile, F32)
    both = jnp.concatenate([both, send(after((both,), partial)[0], 4)], axis=1)
    t6a, t6b, s6a, sb_out, first_pre, partial, own_t, both = after(
        (t6a, t6b, s6a, sb, first_pre, partial, own_t, both)
    )
    quarter = half // 2
    s6b = [send(sb_out[half : half + quarter], 2), send(sb_out[quarter:half], 4)]
    s7a = core(s6a)
    c4 = core(stack(t6a, t6b, t2b, t4b, t2a, t4a))
    third = Shards(
        [[own_t], cut(cs, 6, 7), [t2a, t2b], cut(c4, 4, 2), [t4a, t4b], cut(c4, 5, 3)]
        + [[t6a, t6b], cut(c4, 0, 1)]
    )
    back = back_call(where, grads, third)
    s6b_low, s6b_high, s7a, back, both = after((*s6b, s7a, back, both))
    last = [[s6a, s6b_low, s6b_high], [s7a, core(stack(s6b_low, s6b_high))]]
    second = Shards(most + last)
    second_pre, parts, whole, both = totals_call(
        where, normed, partial, Shards(last), len(most) * depth, first_pre, back, both, depth, tile
    )
    return where, scale, first, second, third, first_pre, second_pre, back, both, parts, whole


def front(where, tile, rows_in, grad_rows, gain, gate_bias, state_in, w_gate, w_cand, w_out):
    first, second, third = (
        Shards([[lax.all_gather(w, "seq", tiled=True)]]) for w in (w_gate, w_cand, w_out)
    )
    both = lax.all_gather(jnp.stack([gate_bias, state_in[0]]), "seq", axis=1, tiled=True)
    normed, grads, scale = norm_call(where, rows_in, grad_rows, gain, first.depth)
    first_pre = project_call(normed, first, tile, BF16)
    back = back_call(where, grads, third)
    second_pre, parts, whole, both = totals_call(
        where, normed, None, second, 0, first_pre, back, both, first.depth, tile
    )
    return where, scale, first, second, third, first_pre, second_pre, back, both, parts, whole


def on_device(ranks, batches, inputs, output_grad, norm_gain, gate_bias, state_in, w_gate, w_cand, w_out):
    rows_in, grad_rows = inputs[0], output_grad[0]
    gain = norm_gain[None, :]
    hidden = w_gate.shape[1]
    tile = min(512, hidden)
    me = lax.axis_index("seq")
    given = (rows_in, grad_rows, gain, gate_bias, state_in, w_gate, w_cand, w_out)
    cube = ranks == 8 and batches in (2, 4, 8)
    if cube:
        turned = lax.axis_index("batch") % 2
        where = jnp.stack([me, turned, me]).astype(jnp.int32)
        found = front_on_cube(ranks, batches, where, turned, tile, *given)
    else:
        nought = jnp.zeros_like(me)
        where = jnp.stack([nought, nought, me]).astype(jnp.int32)
        found = front(where, tile, *given)
    where, scale, first, second, third, first_pre, second_pre, back, both, parts, whole = found
    if cube:
        found = jnp.stack([hop(whole, offset, ranks) for offset in (2, 4, 6)])
        wholes = [jnp.stack([whole, hop(whole, 1, ranks)]), found, hop(found, 1, ranks)]
        offsets = [(0, 1), (2, 4, 6), (3, 5, 7)]
    else:
        wholes, offsets = [lax.all_gather(whole, "seq")], [range(ranks)]
    state_rows, one, other, bias_part, state_grad = scan_call(
        where, first_pre, second_pre, back, both, parts, wholes, offsets, ranks, third.depth, tile
    )
    width = hidden // ranks
    if cube:
        came = swap_batch(bias_part, 1, batches)
        layer_out = layer_call(where, state_rows, rows_in, third, tile)
        layer_out, bias_part, came, one, other = after((layer_out, bias_part, came, one, other))
        for offset in range(1, batches.bit_length() - 1):
            bias_part = bias_part + came
            came = swap_batch(bias_part, 1 << offset, batches)
        input_grad = input_grad_call(where, one, other, first, second, rows_in, scale, grad_rows, gain)
        state_out, bias_grad = close_call(where, state_grad, [bias_part, came], width)
        bias_grad = bias_grad[0]
    else:
        own_block = lax.dynamic_slice_in_dim(bias_part[0], me * width, width, 0)
        bias_grad = lax.psum(own_block, "batch")
        layer_out = layer_call(where, state_rows, rows_in, third, tile)
        input_grad = input_grad_call(where, one, other, first, second, rows_in, scale, grad_rows, gain)
        state_out = lax.dynamic_slice_in_dim(state_grad, me * width, width, 1)
    return (layer_out[None], input_grad[None], state_out, bias_grad)


def solution(mesh):
    body = functools.partial(on_device, mesh.shape["seq"], mesh.shape["batch"])
    rows = P("batch", "seq", None)
    return jax.shard_map(
        body,
        mesh=mesh,
        in_specs=(rows, rows, P(), P("seq"), P("batch", "seq"), P("seq", None), P("seq", None), P("seq", None)),
        out_specs=(rows, rows, P("batch", "seq"), P("seq")),
        check_vma=False,
    )
```

```python
import functools

import jax
import jax.numpy as jnp
from jax import lax
from jax.experimental import pallas as pl
from jax.experimental.pallas import tpu as pltpu
from jax.sharding import PartitionSpec as P

EPSILON = 1e-06
SEGMENTS = 8
LARGE = 1e37
F32 = jnp.float32
BF16 = jnp.bfloat16


def params(mebibytes):
    return pltpu.CompilerParams(vmem_limit_bytes=mebibytes * 1024 * 1024)


def cost(flops, moved):
    return pl.CostEstimate(flops=int(flops), bytes_accessed=int(moved), transcendentals=0)


def hop(value, offset, count):
    return lax.ppermute(value, "seq", [(i, i ^ offset) for i in range(count)])


def swap_batch(value, offset, count):
    return lax.ppermute(value, "batch", [(i, i ^ offset) for i in range(count)])


def after(values, *earlier):
    return lax.optimization_barrier(tuple(values) + tuple(earlier))[: len(values)]


def place(rows):
    steps = rows // SEGMENTS
    out = lax.broadcasted_iota(jnp.int32, (rows, rows), 0)
    inn = lax.broadcasted_iota(jnp.int32, (rows, rows), 1)
    source = lax.rem(out, SEGMENTS) * steps + lax.div(out, SEGMENTS)
    return (source == inn).astype(F32).astype(BF16)


def place_back(rows):
    steps = rows // SEGMENTS
    out = lax.broadcasted_iota(jnp.int32, (rows, rows), 0)
    inn = lax.broadcasted_iota(jnp.int32, (rows, rows), 1)
    source = lax.rem(out, steps) * SEGMENTS + lax.div(out, steps)
    return (source == inn).astype(F32).astype(BF16)


def dot(a, b):
    return lax.dot_general(a, b, (((1,), (0,)), ((), ())), preferred_element_type=F32)


def tiles(count, tile, body):
    @pl.loop(0, count // tile)
    def _(index):
        body(pl.ds(pl.multiple_of(index * tile, tile), tile))


def unrolled(count, tile, body):
    for index in range(count // tile):
        body(pl.ds(index * tile, tile))


class Shards:
    def __init__(self, groups):
        self.pieces, self.groups = [], []
        for group in groups:
            made = []
            for piece in group:
                array, start, rows = piece if isinstance(piece, tuple) else (piece, 0, piece.shape[0])
                known = [index for index, other in enumerate(self.pieces) if other is array]
                if not known:
                    known = [len(self.pieces)]
                    self.pieces.append(array)
                made.append((known[0], start, rows))
            self.groups.append(made)
        self.depth = sum(rows for _, _, rows in self.groups[0])
        self.width = self.pieces[0].shape[1]

    def operands(self):
        return [pltpu.with_memory_space_constraint(piece, pltpu.VMEM) for piece in self.pieces]

    def block(self, refs, index, part, size):
        found, begin = [], 0
        for which, start, rows in self.groups[index]:
            low, high = max(part, begin), min(part + size, begin + rows)
            if low < high:
                found.append(refs[which][start + low - begin : start + high - begin, :])
            begin += rows
        return found[0] if len(found) == 1 else jnp.concatenate(found, axis=0)

    def product(self, x_ref, skip, refs, span):
        total = None
        joint = max(1, min(len(self.groups), 4))
        for index in range(0, len(self.groups), joint):
            groups = self.groups[index : index + joint]
            found = [refs[which][start : start + rows, span] for group in groups for which, start, rows in group]
            block = found[0] if len(found) == 1 else jnp.concatenate(found, axis=0)
            start = skip + index * self.depth
            term = dot(x_ref[:, start : start + len(groups) * self.depth], block)
            total = term if total is None else total + term
        return total


def near(value):
    return pltpu.with_memory_space_constraint(value, pltpu.VMEM)


VMEM_SPEC = pl.BlockSpec(memory_space=pltpu.VMEM)
SMEM_SPEC = pl.BlockSpec(memory_space=pltpu.SMEM)


def norm_call(where, x, g, gain, depth):
    rows, width = x.shape

    def kernel(where_ref, x_ref, g_ref, gain_ref, normed_ref, grads_ref, scale_ref, hold):
        def rows_body(span):
            x = x_ref[span, :].astype(F32)
            scale = lax.rsqrt(jnp.mean(x * x, axis=-1, keepdims=True) + EPSILON)
            scale_ref[span, :] = scale
            hold[span, :] = (x * scale * gain_ref[...]).astype(BF16)

        tiles(rows, min(32, rows), rows_body)
        order = place(rows)
        for index in range(width // depth):
            source = pl.ds(pl.multiple_of((where_ref[0] ^ index) * depth, depth), depth)
            normed_ref[:, index * depth : (index + 1) * depth] = dot(order, hold[:, source]).astype(BF16)

        def grads_body(span):
            grads_ref[span, :] = dot(order, g_ref[:, span]).T.astype(BF16)

        tiles(width, min(512, width), grads_body)

    return pl.pallas_call(
        kernel,
        out_shape=[
            jax.ShapeDtypeStruct((rows, width), BF16),
            jax.ShapeDtypeStruct((width, rows), BF16),
            jax.ShapeDtypeStruct((rows, 1), F32),
        ],
        in_specs=[SMEM_SPEC] + [VMEM_SPEC] * 3,
        out_specs=[VMEM_SPEC] * 3,
        scratch_shapes=[pltpu.VMEM(x.shape, BF16)],
        compiler_params=params(14),
        cost_estimate=cost(4 * rows * x.size, 8 * x.size),
        name="norm_rows",
    )(where, near(x), near(g), near(gain))


def project_call(x, shards, tile, dtype, skip=0):
    rows, width = x.shape[0], shards.width
    count, depth = len(shards.groups), shards.depth

    def kernel(x_ref, *refs):
        refs, out_ref = refs[:-1], refs[-1]

        def body(span):
            out_ref[:, span] = shards.product(x_ref, skip, refs, span).astype(dtype)

        tiles(width, tile, body)

    return pl.pallas_call(
        kernel,
        out_shape=jax.ShapeDtypeStruct((rows, width), dtype),
        in_specs=[VMEM_SPEC] + [VMEM_SPEC] * len(shards.pieces),
        out_specs=VMEM_SPEC,
        compiler_params=params(14),
        cost_estimate=cost(2 * rows * count * depth * width, 2 * count * depth * width),
        name="project",
    )(near(x), *shards.operands())


def back_call(where, grads, shards):
    width, rows = grads.shape
    count, depth = len(shards.groups), shards.depth

    def kernel(where_ref, g_ref, *refs):
        refs, out_ref = refs[:-1], refs[-1]
        size = min(depth, 256)
        for index in range(count):
            for part in range(0, depth, size):
                target = pl.multiple_of((where_ref[0] ^ index) * depth + part, size)
                term = dot(shards.block(refs, index, part, size), g_ref[...])
                out_ref[:, pl.ds(target, size)] = term.T.astype(BF16)

    return pl.pallas_call(
        kernel,
        out_shape=jax.ShapeDtypeStruct((rows, count * depth), BF16),
        in_specs=[SMEM_SPEC, VMEM_SPEC] + [VMEM_SPEC] * len(shards.pieces),
        out_specs=VMEM_SPEC,
        compiler_params=params(14),
        cost_estimate=cost(2 * rows * count * depth * width, 2 * count * depth * width),
        name="back_rows",
    )(where, near(grads), *shards.operands())


def gates(x):
    under = 1.0 + jnp.minimum(jnp.exp(-x), LARGE)
    rough = pl.reciprocal(under, approx=True)
    update = rough * (2.0 - under * rough)
    return update, 1.0 - update


def slab_pair(ref, pair, span):
    return split(ref[pair * 2 * SEGMENTS : (pair + 1) * 2 * SEGMENTS, span])


def split(both):
    both = both.astype(F32)
    return both[:SEGMENTS], both[SEGMENTS:]


def chosen_pair(where_ref, first_ref, second_ref, pair, span):
    here = slice(pair * 2 * SEGMENTS, (pair + 1) * 2 * SEGMENTS)
    gate, cand = choose(where_ref, first_ref[here, span], second_ref[here, span])
    return split(gate), split(cand)


def choose(where_ref, one, other):
    straight = where_ref[1] == 0
    return jnp.where(straight, one, other), jnp.where(straight, other, one)


def totals_call(where, x, partial, shards, skip, first_pre, back, both, block, tile):
    rows, width = first_pre.shape
    pairs = rows // (2 * SEGMENTS)
    count, depth = len(shards.groups), shards.depth
    extra = [] if partial is None else [partial]

    def kernel(where_ref, x_ref, first_ref, back_ref, both_ref, *refs):
        partial_refs, refs = refs[: len(extra)], refs[len(extra) :]
        refs, (second_ref, parts_ref, whole_ref, rows_ref) = refs[:-4], refs[-4:]
        for index in range(width // block):
            target = pl.multiple_of((where_ref[0] ^ index) * block, block)
            rows_ref[:, pl.ds(target, block)] = both_ref[:, index * block : (index + 1) * block]

        def body(span):
            total = shards.product(x_ref, skip, refs, span)
            for ref in partial_refs:
                total = total + ref[:, span]
            second_ref[:, span] = total.astype(BF16)
            bias = rows_ref[0:1, span]
            keep = jnp.ones((SEGMENTS, tile), F32)
            state = leaving = slope_run = slopes = updates = crossed = jnp.zeros((SEGMENTS, tile), F32)
            for pair in range(pairs):
                slabs = chosen_pair(where_ref, first_ref, second_ref, pair, span)
                for gate, cand, g in zip(*slabs, slab_pair(back_ref, pair, span)):
                    update, retain = gates(gate + bias)
                    slope = (cand - state) * update * retain
                    keep = keep * retain
                    state = retain * state + update * cand
                    kept_grad = keep * g
                    leaving = leaving + kept_grad
                    slope_run = retain * slope_run + slope
                    slopes = slopes + g * slope_run
                    updates = updates + update
                    crossed = crossed + kept_grad * updates
            parts_ref[0, :, span], parts_ref[1, :, span], parts_ref[2, :, span] = keep, state, leaving
            both_sides = keep * updates
            row = lambda value, s: value[s : s + 1]
            zero, one = row(keep, 0) * 0.0, row(keep, 0) * 0.0 + 1.0
            start, start_slope = [zero], [one]
            for s in range(SEGMENTS):
                start.append(row(keep, s) * start[-1] + row(state, s))
                start_slope.append(row(keep, s) * start_slope[-1])
            tail, tail_slope = [zero], [one]
            for s in range(SEGMENTS - 1, -1, -1):
                tail.append(row(keep, s) * tail[-1] + row(leaving, s))
                tail_slope.append(row(keep, s) * tail_slope[-1])
            whole = [start_slope[-1], start[-1], tail[-1]]
            start, start_slope = jnp.concatenate(start[:-1], axis=0), jnp.concatenate(start_slope[:-1], axis=0)
            tail = jnp.concatenate(tail[-2::-1], axis=0)
            tail_slope = jnp.concatenate(tail_slope[-2::-1], axis=0)
            by_tail = slope_run - both_sides * start
            by_start = crossed + both_sides * tail
            sums = [
                slopes + slope_run * tail - by_start * start,
                by_tail * tail_slope,
                by_start * start_slope,
                both_sides * tail_slope * start_slope,
            ]
            whole += [jnp.sum(value, axis=0, keepdims=True) for value in sums] + [zero]
            whole_ref[:, span] = jnp.concatenate(whole, axis=0)

        unrolled(width, tile, body)

    return pl.pallas_call(
        kernel,
        out_shape=[
            jax.ShapeDtypeStruct((rows, width), BF16),
            jax.ShapeDtypeStruct((3, SEGMENTS, width), F32),
            jax.ShapeDtypeStruct((8, width), F32),
            jax.ShapeDtypeStruct((2, width), F32),
        ],
        in_specs=[SMEM_SPEC] + [VMEM_SPEC] * (4 + len(extra)) + [VMEM_SPEC] * len(shards.pieces),
        out_specs=[VMEM_SPEC] * 4,
        compiler_params=params(14),
        cost_estimate=cost(2 * rows * count * depth * width, 2 * count * depth * width),
        name="project_totals",
    )(where, *map(near, (x, first_pre, back, both, *extra)), *shards.operands())


def scan_call(where, first_pre, second_pre, back, both, parts, wholes, offsets, ranks, shard, tile):
    rows, width = first_pre.shape
    pairs = rows // (2 * SEGMENTS)

    def kernel(where_ref, first_ref, second_ref, back_ref, both_ref, parts_ref, *refs):
        whole_refs, refs = refs[: len(wholes)], refs[len(wholes) :]
        (state_ref, one_ref, other_ref, bias_grad_ref, state_grad_ref) = refs[:5]
        hold, kept, updates, slopes, one_hold, other_hold, state_hold = refs[5:]
        me = where_ref[2]
        order, order_back = place_back(rows), place(rows)

        def body(span):
            for ref, members in zip(whole_refs, offsets):
                for member, offset in enumerate(members):
                    hold[where_ref[0] ^ offset] = ref[member, :, span]
            blocks = [hold[rank] for rank in range(ranks)]
            held = both_ref[1:2, span]
            entering, held_by = held, []
            for rank in range(ranks):
                block = blocks[rank]
                entering = jnp.where(rank == me, held, entering)
                held_by.append(held)
                held = block[0:1] * held + block[1:2]
            arriving = state_grad = bias_sum = held * 0.0
            for rank in range(ranks - 1, -1, -1):
                block, held = blocks[rank], held_by[rank]
                arriving = jnp.where(rank == me, state_grad, arriving)
                by_tail = block[4:5] - block[6:7] * held
                bias_sum = bias_sum + block[3:4] - block[5:6] * held + by_tail * state_grad
                state_grad = block[0:1] * state_grad + block[2:3]
            state_grad_ref[:, span] = state_grad
            bias_grad_ref[:, span] = bias_sum
            keep, ends, leaves = parts_ref[0, :, span], parts_ref[1, :, span], parts_ref[2, :, span]
            starts = [entering]
            for s in range(SEGMENTS - 1):
                starts.append(keep[s : s + 1] * starts[-1] + ends[s : s + 1])
            tails = [arriving]
            for s in range(SEGMENTS - 1, 0, -1):
                tails.append(keep[s : s + 1] * tails[-1] + leaves[s : s + 1])
            state = jnp.concatenate(starts, axis=0)
            leaving = jnp.concatenate(tails[::-1], axis=0)
            bias = both_ref[0:1, span]

            for pair in range(pairs):
                states, retains, ups, slope = [], [], [], []
                for gate, cand in zip(*chosen_pair(where_ref, first_ref, second_ref, pair, span)):
                    update, retain = gates(gate + bias)
                    retains.append(retain)
                    ups.append(update)
                    slope.append((cand - state) * update * retain)
                    state = retain * state + update * cand
                    states.append(state)
                here = slice(pair * 2 * SEGMENTS, (pair + 1) * 2 * SEGMENTS)
                state_hold[here, :] = jnp.concatenate(states, axis=0).astype(BF16)
                kept[here, :] = jnp.concatenate(retains, axis=0)
                updates[here, :] = jnp.concatenate(ups, axis=0)
                slopes[here, :] = jnp.concatenate(slope, axis=0)

            for pair in range(pairs - 1, -1, -1):
                here = slice(pair * 2 * SEGMENTS, (pair + 1) * 2 * SEGMENTS)
                grads = slab_pair(back_ref, pair, span)
                retain, update, slope = kept[here, :], updates[here, :], slopes[here, :]
                late = grads[1] + leaving
                early = grads[0] + retain[SEGMENTS:] * late
                leaving = retain[:SEGMENTS] * early
                carried = jnp.concatenate([early, late], axis=0)
                gate_grad = carried * slope
                cand_grad = carried * update
                one, other = choose(where_ref, gate_grad.astype(BF16), cand_grad.astype(BF16))
                one_hold[here, :] = one
                other_hold[here, :] = other
            found = dot(order, state_hold[...]).astype(BF16)
            size = min(shard, tile)
            for part in range(0, tile, size):
                target = span.start + part
                if shard <= tile:
                    target = (where_ref[0] ^ lax.div(target, shard)) * shard
                state_ref[:, pl.ds(pl.multiple_of(target, size), size)] = found[:, part : part + size]
            one_ref[span, :] = dot(one_hold[...].T, order_back).astype(BF16)
            other_ref[span, :] = dot(other_hold[...].T, order_back).astype(BF16)

        unrolled(width, tile, body)

    wide = jax.ShapeDtypeStruct((rows, width), BF16)
    tall = jax.ShapeDtypeStruct((width, rows), BF16)
    flat = jax.ShapeDtypeStruct((1, width), F32)
    return pl.pallas_call(
        kernel,
        out_shape=[wide, tall, tall, flat, flat],
        in_specs=[SMEM_SPEC] + [VMEM_SPEC] * (5 + len(wholes)),
        out_specs=[VMEM_SPEC] * 5,
        scratch_shapes=[pltpu.VMEM((ranks, SEGMENTS, tile), F32)]
        + [pltpu.VMEM((rows, tile), F32)] * 3
        + [pltpu.VMEM((rows, tile), BF16)] * 3,
        compiler_params=params(14),
        cost_estimate=cost(6 * rows * rows * width, 12 * rows * width),
        name="scan_rows",
    )(where, *map(near, (first_pre, second_pre, back, both, parts, *wholes)))


def layer_call(where, state_rows, residual, shards, tile):
    rows, width = residual.shape
    count, depth = len(shards.groups), shards.depth

    def kernel(where_ref, x_ref, residual_ref, *refs):
        refs, out_ref = refs[:-1], refs[-1]
        def body(span):
            total = shards.product(x_ref, 0, refs, span)
            out_ref[:, span] = (residual_ref[:, span].astype(F32) + total).astype(BF16)

        unrolled(width, tile, body)

    return pl.pallas_call(
        kernel,
        out_shape=jax.ShapeDtypeStruct((rows, width), BF16),
        in_specs=[SMEM_SPEC] + [VMEM_SPEC] * 2 + [VMEM_SPEC] * len(shards.pieces),
        out_specs=VMEM_SPEC,
        compiler_params=params(14),
        cost_estimate=cost(2 * rows * count * depth * width, 2 * count * depth * width),
        name="layer_rows",
    )(where, near(state_rows), near(residual), *shards.operands())


def input_grad_call(where, one, other, first, second, x, scale, grads, gain):
    rows, width = x.shape
    hidden = one.shape[0]
    count, depth = len(first.groups), first.depth

    def kernel(where_ref, one_ref, other_ref, x_ref, scale_ref, grads_ref, gain_ref, *refs):
        first_refs = refs[: len(first.pieces)]
        second_refs = refs[len(first.pieces) : len(first.pieces) + len(second.pieces)]
        out_ref, total = refs[-2:]
        size = min(depth, 256)
        for index in range(count):
            for part in range(0, depth, size):
                target = pl.multiple_of((where_ref[0] ^ index) * depth + part, size)
                term = dot(first.block(first_refs, index, part, size), one_ref[...])
                term = term + dot(second.block(second_refs, index, part, size), other_ref[...])
                total[:, pl.ds(target, size)] = term.T

        def body(span):
            x = x_ref[span, :].astype(F32)
            scale = scale_ref[span, :]
            unit = x * scale
            unit_grad = total[span, :] * gain_ref[...]
            along = jnp.mean(unit_grad * unit, axis=-1, keepdims=True)
            out = grads_ref[span, :].astype(F32) + scale * (unit_grad - unit * along)
            out_ref[span, :] = out.astype(BF16)

        unrolled(rows, min(32, rows), body)

    return pl.pallas_call(
        kernel,
        out_shape=jax.ShapeDtypeStruct((rows, width), BF16),
        in_specs=[SMEM_SPEC] + [VMEM_SPEC] * 6 + [VMEM_SPEC] * (len(first.pieces) + len(second.pieces)),
        out_specs=VMEM_SPEC,
        scratch_shapes=[pltpu.VMEM((rows, width), F32)],
        compiler_params=params(14),
        cost_estimate=cost(4 * one.size * width, 4 * hidden * width),
        name="input_grad_rows",
    )(where, *map(near, (one, other, x, scale, grads, gain)), *first.operands(), *second.operands())


def close_call(where, state_grad, rows, block):
    def kernel(where_ref, state_ref, *refs):
        refs, (state_out_ref, bias_out_ref) = refs[:-2], refs[-2:]
        here = pl.ds(pl.multiple_of(where_ref[2] * block, block), block)
        state_out_ref[...] = state_ref[:, here]
        bias_out_ref[...] = sum((ref[:, here] for ref in refs[1:]), refs[0][:, here])

    return pl.pallas_call(
        kernel,
        out_shape=[jax.ShapeDtypeStruct((1, block), F32)] * 2,
        in_specs=[SMEM_SPEC] + [VMEM_SPEC] * (1 + len(rows)),
        out_specs=[VMEM_SPEC] * 2,
        compiler_params=params(2),
        cost_estimate=cost(1, 4 * state_grad.size),
        name="close_rows",
    )(where, state_grad, *rows)


def front_on_cube(ranks, batches, where, turned, tile, rows_in, grad_rows, gain, gate_bias, state_in, w_gate, w_cand, w_out):
    half = w_gate.shape[0] // 2
    depth = w_gate.shape[0]
    halves = lambda w: (w[:half], w[half:])
    straight = turned == 0
    send = lambda value, offset: hop(value, offset, ranks)
    core = lambda value: hop(value, 1, ranks)
    over = lambda value: swap_batch(value, 1, batches)
    f_a = jnp.where(straight, w_gate[:half], w_cand[:half])
    f_a, where, w_gate, w_cand, own_t = after((f_a, where, w_gate, w_cand, w_out))
    own_f = [f_a, jnp.where(straight, w_gate[half:], w_cand[half:])]
    stack = lambda *parts: jnp.concatenate(parts, axis=0)
    cut = lambda held, *starts: [(held, start * half, half) for start in starts]
    f2a, f4a = send(own_f[0], 2), send(own_f[0], 4)
    f1 = [core(v) for v in own_f]
    both = jnp.stack([gate_bias, state_in[0]])
    both = jnp.concatenate([both, core(both)], axis=1)
    both = jnp.concatenate([both, send(both, 2)], axis=1)
    normed, grads, scale = norm_call(where, rows_in, grad_rows, gain, depth)
    own_s = jnp.where(straight, w_cand, w_gate)
    t_a, t_b = halves(own_t)
    f2a, f4a, f1a, f1b, both, normed, grads, f_b, own_s, own_t, t_a, t_b = after(
        (f2a, f4a, f1[0], f1[1], both, normed, grads, own_f[1], own_s, own_t, t_a, t_b)
    )
    f2b, f4b = send(f_b, 2), send(f_b, 4)
    t2a, t4a = send(t_a, 2), send(t_a, 4)
    sa = over(stack(f2a, f4a))
    f2b, f4b, f3a, f5a = after((f2b, f4b, f2a, f4a))
    f3a, f5a = core(f3a), core(f5a)
    f2b, f4b, f_b2, sa, t2a, t4a, f3a, f5a, t_b, f2a = after(
        (f2b, f4b, stack(f2b, f4b), sa, t2a, t4a, f3a, f5a, t_b, f2a)
    )
    f6a, f6b = send(f2a, 4), send(f4b, 2)
    t2b, t4b = send(t_b, 2), send(t_b, 4)
    sb = over(f_b2)
    f6a, f6b, f3b, f5b = after((f6a, f6b, f2b, f4b))
    f3b, f5b = core(f3b), core(f5b)
    both, f6a, f6b, sb, t2b, t4b, f3b, f5b, sa, t2a = after((both, f6a, f6b, sb, t2b, t4b, f3b, f5b, sa, t2a))
    t6a, t6b = send(t2a, 4), send(t4b, 2)
    s6a = over(f6a)
    f7, cs = core(stack(f6a, f6b)), core(stack(sa, sb, own_s, own_t))
    first = Shards([own_f, [f1a, f1b], [f2a, f2b], [f3a, f3b], [f4a, f4b], [f5a, f5b], [f6a, f6b], [f7]])
    pairs = lambda one, two, row: cut(one, row) + cut(two, row)
    most = [[own_s], cut(cs, 4, 5), pairs(sa, sb, 0), cut(cs, 0, 2), pairs(sa, sb, 1), cut(cs, 1, 3)]
    first_pre = project_call(normed, first, tile, BF16)
    partial = project_call(normed, Shards(most), tile, F32)
    both = jnp.concatenate([both, send(after((both,), partial)[0], 4)], axis=1)
    t6a, t6b, s6a, sb_out, f6b_out, first_pre, partial, own_t, both = after(
        (t6a, t6b, s6a, sb, f6b, first_pre, partial, own_t, both)
    )
    share = half * 3 // 8
    s6b = [send(sb_out[half : half + share], 2), send(sb_out[share : 2 * share], 4), over(f6b_out[2 * share :])]
    s7a = core(s6a)
    c4 = core(stack(t6a, t6b, t2b, t4b, t2a, t4a))
    third = Shards(
        [[own_t], cut(cs, 6, 7), [t2a, t2b], cut(c4, 4, 2), [t4a, t4b], cut(c4, 5, 3)]
        + [[t6a, t6b], cut(c4, 0, 1)]
    )
    back = back_call(where, grads, third)
    *s6b, s7a, back, both = after((*s6b, s7a, back, both))
    last = [[s6a, *s6b], [s7a, core(stack(*s6b))]]
    second = Shards(most + last)
    second_pre, parts, whole, both = totals_call(
        where, normed, partial, Shards(last), len(most) * depth, first_pre, back, both, depth, tile
    )
    return where, scale, first, second, third, first_pre, second_pre, back, both, parts, whole


def front(where, tile, rows_in, grad_rows, gain, gate_bias, state_in, w_gate, w_cand, w_out):
    first, second, third = (
        Shards([[lax.all_gather(w, "seq", tiled=True)]]) for w in (w_gate, w_cand, w_out)
    )
    both = lax.all_gather(jnp.stack([gate_bias, state_in[0]]), "seq", axis=1, tiled=True)
    normed, grads, scale = norm_call(where, rows_in, grad_rows, gain, first.depth)
    first_pre = project_call(normed, first, tile, BF16)
    back = back_call(where, grads, third)
    second_pre, parts, whole, both = totals_call(
        where, normed, None, second, 0, first_pre, back, both, first.depth, tile
    )
    return where, scale, first, second, third, first_pre, second_pre, back, both, parts, whole


def on_device(ranks, batches, inputs, output_grad, norm_gain, gate_bias, state_in, w_gate, w_cand, w_out):
    rows_in, grad_rows = inputs[0], output_grad[0]
    gain = norm_gain[None, :]
    hidden = w_gate.shape[1]
    tile = min(512, hidden)
    me = lax.axis_index("seq")
    given = (rows_in, grad_rows, gain, gate_bias, state_in, w_gate, w_cand, w_out)
    cube = ranks == 8 and batches in (2, 4, 8)
    if cube:
        turned = lax.axis_index("batch") % 2
        where = jnp.stack([me, turned, me]).astype(jnp.int32)
        found = front_on_cube(ranks, batches, where, turned, tile, *given)
    else:
        nought = jnp.zeros_like(me)
        where = jnp.stack([nought, nought, me]).astype(jnp.int32)
        found = front(where, tile, *given)
    where, scale, first, second, third, first_pre, second_pre, back, both, parts, whole = found
    if cube:
        found = jnp.stack([hop(whole, offset, ranks) for offset in (2, 4, 6)])
        wholes = [jnp.stack([whole, hop(whole, 1, ranks)]), found, hop(found, 1, ranks)]
        offsets = [(0, 1), (2, 4, 6), (3, 5, 7)]
    else:
        wholes, offsets = [lax.all_gather(whole, "seq")], [range(ranks)]
    state_rows, one, other, bias_part, state_grad = scan_call(
        where, first_pre, second_pre, back, both, parts, wholes, offsets, ranks, third.depth, tile
    )
    width = hidden // ranks
    if cube:
        came = swap_batch(bias_part, 1, batches)
        layer_out = layer_call(where, state_rows, rows_in, third, tile)
        layer_out, bias_part, came, one, other = after((layer_out, bias_part, came, one, other))
        for offset in range(1, batches.bit_length() - 1):
            bias_part = bias_part + came
            came = swap_batch(bias_part, 1 << offset, batches)
        input_grad = input_grad_call(where, one, other, first, second, rows_in, scale, grad_rows, gain)
        state_out, bias_grad = close_call(where, state_grad, [bias_part, came], width)
        bias_grad = bias_grad[0]
    else:
        own_block = lax.dynamic_slice_in_dim(bias_part[0], me * width, width, 0)
        bias_grad = lax.psum(own_block, "batch")
        layer_out = layer_call(where, state_rows, rows_in, third, tile)
        input_grad = input_grad_call(where, one, other, first, second, rows_in, scale, grad_rows, gain)
        state_out = lax.dynamic_slice_in_dim(state_grad, me * width, width, 1)
    return (layer_out[None], input_grad[None], state_out, bias_grad)


def solution(mesh):
    body = functools.partial(on_device, mesh.shape["seq"], mesh.shape["batch"])
    rows = P("batch", "seq", None)
    return jax.shard_map(
        body,
        mesh=mesh,
        in_specs=(rows, rows, P(), P("seq"), P("batch", "seq"), P("seq", None), P("seq", None), P("seq", None)),
        out_specs=(rows, rows, P("batch", "seq"), P("seq")),
        check_vma=False,
    )
```
